32 devices in a mesh: narrow: 2 (over y), wide: 16 (over z, x, core).
Axes of the slice: x: 2, y: 2, z: 4, core: 2. Of those that a mesh axis runs over, the one named last changes fastest.
Arguments:
- tokens: bfloat16 [65536, 384], P(('narrow', 'wide')), may hold values from -6 to 6
- cotangent: bfloat16 [65536, 384], P(('narrow', 'wide')), may hold values from -6 to 6
- valid: int32 [64, 1024], P(('narrow', 'wide')), may hold values from 0 to 1, as said below
- task_ids: int32 [64], P(('narrow', 'wide')), may hold values from 0 to 1
- top_counts: int32 [2], replicated, may hold values from 1 to 4
- expert_ids: int32 [65536, 4], P(('narrow', 'wide')), may hold values from 0 to 7, all different within a row
- attn_gain: bfloat16 [384], P('wide'), may hold values from 0.099609375 to 1.8984375
- attn_shift: bfloat16 [384], P('wide'), may hold values from -1.5 to 1.5
- proj_in: bfloat16 [384, 1152], P('wide'), may hold values from -0.3125 to 0.3125
- proj_out: bfloat16 [384, 384], P('wide'), may hold values from -4 to 4
- moe_gain: bfloat16 [384], P('wide'), may hold values from 0.099609375 to 1.8984375
- moe_shift: bfloat16 [384], P('wide'), may hold values from -1.5 to 1.5
- router: bfloat16 [2, 384, 8], P(None, 'wide'), may hold values from -0.15625 to 0.15625
- expert_in: bfloat16 [8, 384, 1536], P(None, 'wide'), may hold values from -0.3125 to 0.3125
- expert_out: bfloat16 [8, 1536, 384], P(None, 'wide'), may hold values from -1.25 to 1.25
Outputs:
- output: bfloat16 [65536, 384], P(('narrow', 'wide'))
- grad_tokens: bfloat16 [65536, 384], P(('narrow', 'wide'))
- grad_attn_gain: float32 [384], P('wide')
- grad_attn_shift: float32 [384], P('wide')
- grad_proj_in: float32 [384, 1152], P('wide')
- grad_proj_out: float32 [384, 384], P('wide')
- grad_moe_gain: float32 [384], P('wide')
- grad_moe_shift: float32 [384], P('wide')
- grad_router: float32 [2, 384, 8], P(None, 'wide')
- grad_expert_in: float32 [8, 384, 1536], P(None, 'wide')
- grad_expert_out: float32 [8, 1536, 384], P(None, 'wide')
The draws below stay inside these ranges and needn't reach their ends.
Inputs may be any that keep to these rules, and one draw needn't show every extreme that they name: `valid`: 1 marks a patch of the image's crop, a top-left rectangle of its square grid of 1024 patches; every image has at least one patch. `expert_ids`: each row names 4 different experts.
All inputs are finite; a program needn't handle non-finite values.
Results may differ from the reference program's by a relative error of at most 0.012.
Values may be sent and summed in bfloat16 or wider, within the bound.
A program may use at most 320 MiB of HBM per device.

```python
import math
import jax
import jax.numpy as jnp
from jax import lax

D = 384
HEADS = 6
HEAD_DIM = 64
FF = 1536
EXPERTS = 8
TOPMAX = 4
TASKS = 2
GRID = 1024
IMG_MB = 1
CAP = 256
TOKENS = 65536
IMAGES = 64


def draw_valid(key, part):
    key = jax.random.fold_in(key, 11)
    grid_side = math.isqrt(GRID)
    key_height, key_width = jax.random.split(key)
    height = jax.random.randint(key_height, (IMAGES, 1), grid_side // 2, grid_side + 1)
    width = jax.random.randint(key_width, (IMAGES, 1), grid_side // 2, grid_side + 1)
    patch_index = jnp.arange(GRID, dtype=jnp.int32)[None, :]
    patch_row = patch_index // grid_side
    patch_col = patch_index % grid_side
    return ((patch_row < height) & (patch_col < width)).astype(jnp.int32)


def draw_top_counts(key, part):
    key = jax.random.fold_in(key, 23)
    task_keys = jax.vmap(lambda index: jax.random.fold_in(key, index))(jnp.arange(TASKS, dtype=jnp.int32))
    counts = jax.vmap(lambda task_key: jax.random.randint(task_key, (), 1, TOPMAX + 1))(task_keys)
    return counts.astype(jnp.int32)


def with_ends(values, stream_key, low, top_value):
    shape = values.shape
    index_at = [jax.random.randint(jax.random.fold_in(stream_key, axis), (), 0, shape[axis]) for axis in range(len(shape))]
    values = values.at[tuple(index_at)].set(low)
    longest = shape.index(max(shape))
    index_at[longest] = (index_at[longest] + 1) % shape[longest]
    return values.at[tuple(index_at)].set(top_value)


def spiked(values, stream_key, source, target, shards_of, factor):
    def block_of(dim):
        return (jnp.arange(values.shape[dim]) // (values.shape[dim] // shards_of)).reshape((-1,) + (1,) * (values.ndim - 1 - dim))

    first = jax.random.permutation(stream_key, shards_of)[block_of(target)]
    other_side = (block_of(target) + shards_of // 2) % shards_of
    return jnp.where((block_of(source) == first) | (block_of(source) == other_side), factor * values, values)


def levels(own_key, dims, shards, smallest, largest):
    level, own = 1.0, jax.random.fold_in(own_key, 6)
    for dim, parts in shards:
        draws = jnp.exp(jax.random.uniform(jax.random.fold_in(own, dim), (parts,), jnp.float32, smallest / len(shards), largest / len(shards)))
        level = level * jnp.repeat(draws, dims[dim] // parts).reshape([-1 if axis == dim else 1 for axis in range(len(dims))])
    return level


def different_ones(own_key, rows, count, top, lift):
    sequence = jax.random.permutation(jax.random.fold_in(own_key, 1), count)
    favour = sequence
    for power in range(3):
        favour = favour * favour // count
    favour = favour * lift // count
    chance = jax.random.randint(jax.random.fold_in(own_key, 2), (rows, count), 0, 4096) + favour
    fixed_rows = jax.random.permutation(jax.random.fold_in(own_key, 3), rows)[jnp.arange(count) % rows]
    chance = jnp.where(jnp.arange(rows)[:, None] == fixed_rows[None, :], 1 << 14, chance)
    merit = chance * count + jnp.arange(count)
    return lax.top_k(merit.astype(jnp.int32), top)[1].astype(jnp.int32)


def noise(own_key, extent, scale, bound, cuts=(), kind=jnp.bfloat16):
    drawn = scale * jax.random.normal(own_key, extent, jnp.float32)
    if cuts:
        drawn = drawn * levels(own_key, extent, cuts, -0.22, 0.18)
    return jnp.clip(drawn, -bound, bound).astype(kind)


def bell_draw_with(stream_key, extent, scale, reach, cuts, heavy, held_as=jnp.bfloat16):
    values = scale * jax.random.normal(stream_key, extent, jnp.float32)
    if cuts:
        values = values * levels(stream_key, extent, cuts, -0.22, 0.18)
    return jnp.clip(spiked(values, jax.random.fold_in(stream_key, 3), *heavy), -reach, reach).astype(held_as)


def setup_inputs(seed: int = 0) -> dict:
    key_of = jax.random.split(jax.random.key(seed), 16)
    return {
        "tokens": bell_draw_with(key_of[0], (TOKENS, D), 1.0, 6.0, ((0, 32),), (0, 1, 32, 2.75)),
        "cotangent": bell_draw_with(key_of[1], (TOKENS, D), 1.0, 6.0, ((0, 32),), (0, 1, 32, 2.75)),
        "valid": draw_valid(jax.random.fold_in(key_of[15], 71), 0),
        "task_ids": with_ends(jax.random.randint(key_of[3], (IMAGES,), 0, TASKS), jax.random.fold_in(key_of[3], 1), 0, TASKS - 1).astype(jnp.int32),
        "top_counts": draw_top_counts(jax.random.fold_in(key_of[15], 71), 0),
        "expert_ids": different_ones(key_of[5], TOKENS, EXPERTS, TOPMAX, 4096),
        "attn_gain": jnp.clip(1.0 + 0.18 * jax.random.normal(key_of[6], (D,), jnp.float32), 0.099609375, 1.8984375).astype(jnp.bfloat16),
        "attn_shift": noise(key_of[7], (D,), 0.3, 1.5, ((0, 16),)),
        "proj_in": noise(key_of[8], (D, 3 * D), D ** -0.5, 0.3125, ((0, 16),)),
        "proj_out": noise(key_of[9], (D, D), 2 ** -0.5, 4.0, ((0, 16),)),
        "moe_gain": jnp.clip(1.0 + 0.18 * jax.random.normal(key_of[10], (D,), jnp.float32), 0.099609375, 1.8984375).astype(jnp.bfloat16),
        "moe_shift": noise(key_of[11], (D,), 0.3, 1.5, ((0, 16),)),
        "router": noise(key_of[12], (TASKS, D, EXPERTS), (4 * D) ** -0.5, 0.15625, ((1, 16),)),
        "expert_in": noise(key_of[13], (EXPERTS, D, FF), D ** -0.5, 0.3125, ((1, 16),)),
        "expert_out": noise(key_of[14], (EXPERTS, FF, D), (max(FF // 64, 1)) ** -0.5, 1.25, ((1, 16),)),
    }


@jax.custom_vjp
def low(v):
    return lax.optimization_barrier(v.astype(jnp.bfloat16)).astype(jnp.float32)

@jax.custom_vjp
def low_back(v):
    return v

def low_keep(v):
    return (low(v), None)

def low_pass(kept, grad):
    return (grad,)

def back_keep(v):
    return (v, None)

def back_low(kept, grad):
    return (low(grad),)
low.defvjp(low_keep, low_pass)
low_back.defvjp(back_keep, back_low)
NEGATIVE = -1e+30
EPSILON = 1e-06
HIGHEST = lax.Precision.HIGHEST

def layer_norm(values, gain, shift):
    center = values - lax.optimization_barrier(jnp.mean(values, axis=-1, keepdims=True))
    return center * lax.rsqrt(lax.optimization_barrier(jnp.mean(center * center, axis=-1, keepdims=True)) + EPSILON) * gain + shift

def softmax_rows(logits):
    raised = jnp.exp(logits - lax.optimization_barrier(jnp.max(logits, axis=-1, keepdims=True)))
    return raised / lax.optimization_barrier(jnp.sum(raised, axis=-1, keepdims=True))

def route(valid, task_ids, top_counts, expert_ids):
    row_count = expert_ids.shape[0]
    task_match = task_ids[:, None] == jnp.arange(TASKS, dtype=jnp.int32)[None, :]
    choose = lax.optimization_barrier(jnp.sum(jnp.where(task_match, top_counts[None, :], 0), axis=1, dtype=jnp.int32))
    per_row = jnp.repeat(choose, GRID)
    live_rows = valid.reshape(row_count) > 0
    choice_ranks = jnp.arange(TOPMAX, dtype=jnp.int32)
    used_mask = live_rows[:, None] & (choice_ranks[None, :] < per_row[:, None])
    expert_match = expert_ids[:, :, None] == jnp.arange(EXPERTS, dtype=jnp.int32)[None, None, :]
    onehot = (expert_match & used_mask[:, :, None]).astype(jnp.int32)
    ordered = jnp.transpose(onehot, (1, 0, 2)).reshape(TOPMAX * row_count, EXPERTS)
    before = jnp.cumsum(ordered, axis=0, dtype=jnp.int32) - ordered
    slot_index = lax.optimization_barrier(jnp.sum(before * ordered, axis=1, dtype=jnp.int32)).reshape(TOPMAX, row_count).T
    kept_mask = used_mask & (slot_index < CAP)
    position = jnp.where(kept_mask, expert_ids * CAP + slot_index, EXPERTS * CAP).astype(jnp.int32)
    entries = jnp.full((EXPERTS * CAP + 1,), row_count * TOPMAX, jnp.int32)
    entries = entries.at[position.reshape(-1)].set(jnp.arange(row_count * TOPMAX, dtype=jnp.int32))
    return (position, kept_mask.astype(jnp.float32), entries[:EXPERTS * CAP])

def attend_block(query_block, key_rows, value_rows, live_keys):
    score_scale = 1.0 / math.sqrt(HEAD_DIM)
    scores = low_back(jnp.einsum('qhd,khd->hqk', query_block, key_rows, precision=HIGHEST) * score_scale)
    scores = jnp.where(live_keys[None, None, :] > 0, scores, NEGATIVE)
    weights = softmax_rows(scores)
    return jnp.einsum('hqk,khd->qhd', low(weights), value_rows, precision=HIGHEST)

def attend_image(query, key_rows, value_rows, live_keys):
    block_span = min(512, GRID)
    blocks = query.reshape(GRID // block_span, block_span, HEADS, HEAD_DIM)
    block_step = jax.checkpoint(lambda query_block: attend_block(query_block, key_rows, value_rows, live_keys))
    return lax.map(block_step, blocks).reshape(GRID, HEADS, HEAD_DIM)

def group_forward(params, top_counts, pieces):
    attn_gain, attn_shift, proj_in, proj_out, moe_gain, moe_shift, router, expert_in, expert_out = params
    inputs, valid, task_ids, expert_ids = pieces
    row_count = inputs.shape[0]
    images = valid.shape[0]
    normed_a = low(layer_norm(inputs, attn_gain, attn_shift))
    mixed = low_back(low(jnp.dot(normed_a, proj_in, precision=HIGHEST)))
    head_parts = mixed.reshape(images, GRID, 3, HEADS, HEAD_DIM)
    attended = lax.map(lambda group: attend_image(group[0], group[1], group[2], group[3]), (head_parts[:, :, 0], head_parts[:, :, 1], head_parts[:, :, 2], valid))
    attended = low_back(low(attended.reshape(row_count, D)))
    branch = low_back(jnp.dot(attended, proj_out, precision=HIGHEST))
    resid = inputs + branch
    normed_b = low(layer_norm(resid, moe_gain, moe_shift))
    chosen = router[task_ids]
    logits = jnp.einsum('igd,ide->ige', normed_b.reshape(images, GRID, D), chosen, precision=HIGHEST)
    logits = low_back(logits.reshape(row_count, EXPERTS))
    router_probs = softmax_rows(logits)
    position, kept_mask, entries = route(valid, task_ids, top_counts, expert_ids)
    onehot = (expert_ids[:, :, None] == jnp.arange(EXPERTS, dtype=jnp.int32)[None, None, :]).astype(jnp.float32)
    gate_values = lax.optimization_barrier(jnp.sum(router_probs[:, None, :] * onehot, axis=-1)) * kept_mask
    padded = jnp.concatenate([normed_b, jnp.zeros((1, D), jnp.float32)], axis=0)
    dispatched = padded[entries // TOPMAX].reshape(EXPERTS, CAP, D)
    pre_gelu = low_back(jnp.einsum('ecd,edf->ecf', dispatched, expert_in, precision=HIGHEST))
    hidden = low(jax.nn.gelu(pre_gelu))
    result = low_back(low(jnp.einsum('ecf,efd->ecd', hidden, expert_out, precision=HIGHEST)))
    result_rows = jnp.concatenate([result.reshape(EXPERTS * CAP, D), jnp.zeros((1, D), jnp.float32)], axis=0)
    return resid + lax.optimization_barrier(jnp.sum(gate_values[:, :, None] * result_rows[position], axis=1))

def reference(tokens, cotangent, valid, task_ids, top_counts, expert_ids, attn_gain, attn_shift, proj_in, proj_out, moe_gain, moe_shift, router, expert_in, expert_out):
    group_rows = IMG_MB * GRID
    groups = TOKENS // group_rows
    params = (attn_gain.astype(jnp.float32), attn_shift.astype(jnp.float32), proj_in.astype(jnp.float32), proj_out.astype(jnp.float32), moe_gain.astype(jnp.float32), moe_shift.astype(jnp.float32), router.astype(jnp.float32), expert_in.astype(jnp.float32), expert_out.astype(jnp.float32))
    checked = jax.checkpoint(group_forward)

    def forward(inputs, weights):

        def scan_step(running, pieces):
            return (running, checked(weights, top_counts, pieces))
        _, produced = lax.scan(scan_step, jnp.zeros((), jnp.float32), (inputs.reshape(groups, group_rows, D), valid.reshape(groups, IMG_MB, GRID), task_ids.reshape(groups, IMG_MB), expert_ids.reshape(groups, group_rows, TOPMAX)))
        return produced.reshape(TOKENS, D)
    output, pullback = jax.vjp(forward, tokens.astype(jnp.float32), params)
    grad_inputs, grads = pullback(cotangent.astype(jnp.float32))
    return (output.astype(jnp.bfloat16), grad_inputs.astype(jnp.bfloat16), grads[0], grads[1], grads[2], grads[3], grads[4], grads[5], grads[6], grads[7], grads[8])
```

```python
import functools
import math

import jax
import jax.numpy as jnp
from jax import lax
from jax.experimental import pallas as pl
from jax.experimental.pallas import tpu as pltpu
from jax.sharding import PartitionSpec as P

D = 384
HEADS = 6
HEAD_DIM = 64
FF = 1536
EXPERTS = 8
TOPMAX = 4
TASKS = 2
GRID = 1024
CAP = 256
PAIRS = HEADS // 2
QB = 256
FC = 512
EPSILON = 1e-06
NEGATIVE = -1e30
SCALE = 1.0 / math.sqrt(HEAD_DIM)
MISC = 3 * D + D
DENSE = MISC + 128

F32 = jnp.float32
BF16 = jnp.bfloat16
VMEM_LIMIT = 60 * 1024 * 1024


def nn(a, b):
    return lax.dot_general(a, b, (((1,), (0,)), ((), ())), preferred_element_type=F32)


def nt(a, b):
    return lax.dot_general(a, b, (((1,), (1,)), ((), ())), preferred_element_type=F32)


def tn(a, b):
    return lax.dot_general(a, b, (((0,), (0,)), ((), ())), preferred_element_type=F32)


def lanes(shape):
    return lax.broadcasted_iota(jnp.int32, shape, 1)


def norm_rows(values):
    center = values - jnp.mean(values, axis=-1, keepdims=True)
    inverse = lax.rsqrt(jnp.mean(center * center, axis=-1, keepdims=True) + EPSILON)
    return center * inverse, inverse


def split3(value):
    high = value.astype(BF16).astype(F32)
    rest = value - high
    mid = rest.astype(BF16).astype(F32)
    return high, mid, rest - mid


def misc_rows(dense_ref):
    return dense_ref[:, MISC:].astype(F32).T


def router_of(dense_ref, task):
    block = dense_ref[:, MISC:].astype(F32)
    first = pltpu.roll(block, 128 - 4, 1)
    second = pltpu.roll(block, 128 - 12, 1)
    chosen = jnp.where(task == 0, first, second)
    return jnp.where(lanes(chosen.shape) < EXPERTS, chosen, 0.0).astype(BF16)


def column_of(row):
    return jnp.broadcast_to(row, (128, row.shape[1])).T


def forward_kernel(
    task_ref,
    count_ref,
    tokens_ref,
    valid_ref,
    ids_ref,
    dense_ref,
    mixed_ref,
    attended_ref,
    resid_ref,
    normed_ref,
    aux_ref,
    rows_ref,
    lse_ref,
    att_t,
):
    image = pl.program_id(0)
    task = task_ref[image]
    count = count_ref[task]
    misc = misc_rows(dense_ref)
    inputs = tokens_ref[...].astype(F32)
    unit_a, _ = norm_rows(inputs)
    normed_a = (unit_a * misc[0:1] + misc[1:2]).astype(BF16)
    mixed_ref[...] = nn(normed_a, dense_ref[:, : 3 * D]).astype(BF16)
    live_col = column_of(valid_ref[pl.ds(image, 1), :].astype(F32))
    lane = lanes((GRID, 128))
    key_ext = jnp.where((lane == 0) & (live_col < 0.5), NEGATIVE, 0.0).astype(BF16)
    query_ext = jnp.where(lanes((QB, 128)) == 0, 1.0, 0.0).astype(BF16)
    ones_rows = jnp.ones((16, GRID), BF16)

    def pair_step(pair, carry):
        at = pl.multiple_of(pair * 128, 128)
        keys = mixed_ref[:, pl.ds(D + at, 128)]
        values = mixed_ref[:, pl.ds(2 * D + at, 128)]
        key_full = jnp.concatenate([keys, key_ext], axis=1)
        value_t = jnp.concatenate([values.astype(F32).T.astype(BF16), ones_rows], axis=0)
        half = lanes((QB, 128)) // HEAD_DIM
        for block in range(GRID // QB):
            span = pl.ds(block * QB, QB)
            query = mixed_ref[span, pl.ds(at, 128)].astype(F32) * SCALE
            for part in range(2):
                own = jnp.where(half == part, query, 0.0).astype(BF16)
                scores = nt(key_full, jnp.concatenate([own, query_ext], axis=1))
                top = jnp.max(scores, axis=0, keepdims=True)
                raised = jnp.exp(scores - top).astype(BF16)
                produced = nn(value_t, raised)
                total = produced[128:129]
                mine = produced[part * HEAD_DIM : (part + 1) * HEAD_DIM] / total
                att_t[pl.ds(at + part * HEAD_DIM, HEAD_DIM), span] = mine
                lse_ref[0, pl.ds(pair * 2 + part, 1), span] = top + jnp.log(total)
        return carry

    lax.fori_loop(0, PAIRS, pair_step, 0)
    lse_ref[0, HEADS:, :] = jnp.zeros((8 - HEADS, GRID), F32)
    attended = att_t[...].T.astype(BF16)
    attended_ref[...] = attended
    resid = inputs + nn(attended, dense_ref[:, 3 * D : MISC])
    resid_ref[...] = resid
    unit_b, _ = norm_rows(resid)
    normed_b = (unit_b * misc[2:3] + misc[3:4]).astype(BF16)
    normed_ref[...] = normed_b
    logits = nn(normed_b, router_of(dense_ref, task))
    logits = jnp.where(lane < EXPERTS, logits, NEGATIVE)
    raised = jnp.exp(logits - jnp.max(logits, axis=-1, keepdims=True))
    probs = raised / jnp.sum(raised, axis=-1, keepdims=True)
    choice = lane // EXPERTS
    wanted = jnp.full((GRID, 128), -1, jnp.int32)
    for rank in range(TOPMAX):
        wanted = jnp.where(choice == rank, ids_ref[:, rank : rank + 1], wanted)
    used = (wanted == lane % EXPERTS) & (choice < count) & (live_col > 0.5)
    used = jnp.where(used, 1.0, 0.0)
    span = 256
    row_at = lax.broadcasted_iota(jnp.int32, (span, span), 0)
    earlier = jnp.where(row_at > lanes((span, span)), 1.0, 0.0).astype(BF16)
    running = jnp.zeros((1, 128), F32)
    pieces = []
    for block in range(GRID // span):
        part = used[block * span : (block + 1) * span]
        pieces.append(nn(earlier, part.astype(BF16)) + running)
        running = running + jnp.sum(part, axis=0, keepdims=True)
    before = jnp.concatenate(pieces, axis=0)
    totals = jnp.broadcast_to(running, (8, 128))
    lane8 = lanes((8, 128))
    base = jnp.zeros((8, 128), F32)
    for rank in range(1, TOPMAX):
        shift = rank * EXPERTS
        base = base + jnp.where(lane8 >= shift, pltpu.roll(totals, shift, 1), 0.0)
    slot = before + base[0:1]
    found = jnp.where((used > 0.5) & (slot < CAP), slot + 1.0, 0.0)
    folded = found
    for rank in range(1, TOPMAX):
        folded = folded + pltpu.roll(found, 128 - rank * EXPERTS, 1)
    slots = jnp.where(lane < EXPERTS, folded - 1.0, -1.0)
    gates = jnp.where(slots >= 0.0, probs, 0.0)
    aux = probs + jnp.where(
        (choice == 1), pltpu.roll(slots, EXPERTS, 1), 0.0
    ) + jnp.where(choice == 2, pltpu.roll(gates, 2 * EXPERTS, 1), 0.0)
    aux_ref[...] = aux
    rows_ref[0] = aux.T[0 : 4 * EXPERTS]


def forward_call(task_ids, top_counts, tokens, valid, expert_ids, dense):
    images = valid.shape[0]
    rows = images * GRID
    by_image = lambda width: pl.BlockSpec((GRID, width), lambda i, *_: (i, 0))
    whole = lambda shape: pl.BlockSpec(shape, lambda i, *_: (0,) * len(shape))
    lead = lambda shape: pl.BlockSpec((1,) + shape, lambda i, *_: (i, 0, 0))
    return pl.pallas_call(
        forward_kernel,
        grid_spec=pltpu.PrefetchScalarGridSpec(
            num_scalar_prefetch=2,
            grid=(images,),
            in_specs=[by_image(D), whole(valid.shape), by_image(TOPMAX), whole(dense.shape)],
            out_specs=[
                by_image(3 * D),
                by_image(D),
                by_image(D),
                by_image(D),
                by_image(128),
                lead((4 * EXPERTS, GRID)),
                lead((8, GRID)),
            ],
            scratch_shapes=[pltpu.VMEM((D, GRID), F32)],
        ),
        out_shape=[
            jax.ShapeDtypeStruct((rows, 3 * D), BF16),
            jax.ShapeDtypeStruct((rows, D), BF16),
            jax.ShapeDtypeStruct((rows, D), F32),
            jax.ShapeDtypeStruct((rows, D), BF16),
            jax.ShapeDtypeStruct((rows, 128), F32),
            jax.ShapeDtypeStruct((images, 4 * EXPERTS, GRID), F32),
            jax.ShapeDtypeStruct((images, 8, GRID), F32),
        ],
        compiler_params=pltpu.CompilerParams(vmem_limit_bytes=VMEM_LIMIT),
        name="attention_forward",
    )(task_ids, top_counts, tokens, valid, expert_ids, dense)


def expert_kernel(
    images,
    normed_ref,
    cot_ref,
    aux_ref,
    rows_ref,
    in_ref,
    out_ref,
    sums_ref,
    dprobs_ref,
    grad_in_ref,
    grad_out_ref,
    both,
    given,
    upstream,
    dres_s,
):
    expert = pl.program_id(0)

    @pl.when(expert == 0)
    def _():
        for image in range(images):
            span = pl.ds(image * GRID, GRID)
            both[span, :D] = normed_ref[span, :]
            both[span, D:] = cot_ref[span, :]

    slot_at = lax.broadcasted_iota(jnp.int32, (CAP, GRID), 0).astype(F32)
    for image in range(images):
        part = pl.ds(image * CAP, CAP)
        slot_row = rows_ref[image, pl.ds(EXPERTS + expert, 1), :]
        gate_row = rows_ref[image, pl.ds(2 * EXPERTS + expert, 1), :]
        match = slot_at == slot_row
        sent = nn(jnp.where(match, 1.0, 0.0).astype(BF16), both[pl.ds(image * GRID, GRID), :])
        gate = jnp.sum(jnp.where(match, gate_row, 0.0), axis=1, keepdims=True)
        given[part, :] = sent[:, :D].astype(BF16)
        upstream[part, :D] = sent[:, D:]
        upstream[part, D:] = jnp.broadcast_to(gate, (CAP, 128))
        dres_s[part, :] = (gate * sent[:, D:]).astype(BF16)
    slots = given[...]
    dres = dres_s[...]
    result = jnp.zeros((images * CAP, D), F32)
    back = jnp.zeros((images * CAP, D), F32)
    c1 = math.sqrt(2.0 / math.pi)
    c3 = c1 * 0.044715
    for chunk in range(FF // FC):
        span = pl.ds(chunk * FC, FC)
        w_in = in_ref[0, :, span]
        w_out = out_ref[0, span, :]
        pre = nn(slots, w_in)
        square = pre * pre
        curve = jnp.tanh(pre * (c1 + c3 * square))
        lifted = 0.5 * (1.0 + curve)
        hidden = (pre * lifted).astype(BF16)
        slope = lifted + (0.5 * pre) * (1.0 - curve * curve) * (c1 + (3.0 * c3) * square)
        result = result + nn(hidden, w_out)
        dpre = (nt(dres, w_out) * slope).astype(BF16)
        back = back + nt(dpre, w_in)
        grad_out_ref[0, span, :] = tn(hidden, dres).astype(grad_out_ref.dtype)
        grad_in_ref[0, :, span] = tn(slots, dpre).astype(grad_in_ref.dtype)
    result = result.astype(BF16).astype(F32)
    dgate = jnp.sum(result * upstream[:, :D], axis=1, keepdims=True)
    gated = result * upstream[:, D : D + 1]
    returned = jnp.concatenate([gated.astype(BF16), back.astype(BF16)], axis=1)
    for image in range(images):
        part = slice(image * CAP, (image + 1) * CAP)
        span = pl.ds(image * GRID, GRID)
        slot_row = rows_ref[image, pl.ds(EXPERTS + expert, 1), :]
        match = slot_at == slot_row
        dprobs_ref[image, pl.ds(expert, 1), :] = jnp.sum(
            jnp.where(match, dgate[part], 0.0), axis=0, keepdims=True
        )
        hit = jnp.where(match, 1.0, 0.0).astype(BF16)
        landed = tn(hit, returned[part])

        @pl.when(expert == 0)
        def _():
            sums_ref[span, :] = landed

        @pl.when(expert > 0)
        def _():
            sums_ref[span, :] = sums_ref[span, :] + landed


def expert_call(normed_b, cotangent, aux, rows, expert_in, expert_out):
    images = rows.shape[0]
    count = images * GRID
    whole = lambda shape: pl.BlockSpec(shape, lambda e: (0,) * len(shape))
    return pl.pallas_call(
        functools.partial(expert_kernel, images),
        grid=(EXPERTS,),
        in_specs=[
            whole((count, D)),
            whole((count, D)),
            whole((count, 128)),
            whole(rows.shape),
            pl.BlockSpec((1, D, FF), lambda e: (e, 0, 0)),
            pl.BlockSpec((1, FF, D), lambda e: (e, 0, 0)),
        ],
        out_specs=[
            whole((count, 2 * D)),
            whole((images, EXPERTS, GRID)),
            pl.BlockSpec((1, D, FF), lambda e: (e, 0, 0)),
            pl.BlockSpec((1, FF, D), lambda e: (e, 0, 0)),
        ],
        out_shape=[
            jax.ShapeDtypeStruct((count, 2 * D), F32),
            jax.ShapeDtypeStruct((images, EXPERTS, GRID), F32),
            jax.ShapeDtypeStruct((EXPERTS, D, FF), BF16),
            jax.ShapeDtypeStruct((EXPERTS, FF, D), BF16),
        ],
        scratch_shapes=[
            pltpu.VMEM((count, 2 * D), BF16),
            pltpu.VMEM((images * CAP, D), BF16),
            pltpu.VMEM((images * CAP, D + 128), F32),
            pltpu.VMEM((images * CAP, D), BF16),
        ],
        compiler_params=pltpu.CompilerParams(vmem_limit_bytes=VMEM_LIMIT),
        name="experts",
    )(normed_b, cotangent, aux, rows, expert_in, expert_out)


def norm_back(upstream, unit_rows, inverse, gain):
    scaled = upstream * gain
    centered = scaled - jnp.mean(scaled, axis=-1, keepdims=True)
    centered = centered - unit_rows * jnp.mean(scaled * unit_rows, axis=-1, keepdims=True)
    return inverse * centered


def backward_kernel(
    task_ref,
    tokens_ref,
    cot_ref,
    valid_ref,
    dense_ref,
    mixed_ref,
    attended_ref,
    resid_ref,
    normed_ref,
    aux_ref,
    lse_ref,
    sums_ref,
    dprobs_ref,
    output_ref,
    grad_tokens_ref,
    grad_dense_ref,
    grad_rows_ref,
    dmixed,
    dattended,
    acc_k,
    acc_v,
    dq_t,
):
    image = pl.program_id(0)
    task = task_ref[image]
    misc = misc_rows(dense_ref)
    lane = lanes((GRID, 128))
    upstream = cot_ref[...].astype(F32)
    resid = resid_ref[...]
    output_ref[...] = (resid + sums_ref[:, :D]).astype(BF16)
    unit_b, inverse_b = norm_rows(resid)
    probs = jnp.where(lane < EXPERTS, aux_ref[...], 0.0)
    dprobs = jnp.concatenate(
        [dprobs_ref[0], jnp.zeros((128 - EXPERTS, GRID), F32)], axis=0
    ).T
    dlogits = probs * (dprobs - jnp.sum(dprobs * probs, axis=-1, keepdims=True))
    dlogits = dlogits.astype(BF16)
    router = router_of(dense_ref, task)
    grad_router = tn(normed_ref[...], dlogits)
    dnormed_b = sums_ref[:, D:] + nt(dlogits, router)
    dresid = upstream + norm_back(dnormed_b, unit_b, inverse_b, misc[2:3])
    dbranch = dresid.astype(BF16)
    grad_proj_out = tn(attended_ref[...], dbranch)
    dattended[...] = nt(dbranch, dense_ref[:, 3 * D : MISC]).astype(BF16)
    live_col = column_of(valid_ref[pl.ds(image, 1), :].astype(F32))
    lse_col = jnp.concatenate([lse_ref[0], jnp.zeros((120, GRID), F32)], axis=0).T
    key_ext = jnp.where((lane == 0) & (live_col < 0.5), NEGATIVE, 0.0)
    key_ext = jnp.where((lane >= 1) & (lane <= 3), 1.0, key_ext).astype(BF16)
    value_ext = jnp.where(lane < 3, 1.0, 0.0).astype(BF16)
    small = lanes((QB, 128))
    half = small // HEAD_DIM

    def pair_step(pair, carry):
        at = pl.multiple_of(pair * 128, 128)
        keys = mixed_ref[:, pl.ds(D + at, 128)]
        values = mixed_ref[:, pl.ds(2 * D + at, 128)]
        key_full = jnp.concatenate([keys, key_ext], axis=1)
        value_full = jnp.concatenate([values, value_ext], axis=1)
        key_t = keys.astype(F32).T.astype(BF16)
        for block in range(GRID // QB):
            span = pl.ds(block * QB, QB)
            query = mixed_ref[span, pl.ds(at, 128)].astype(F32) * SCALE
            grad = dattended[span, pl.ds(at, 128)].astype(F32)
            seen = attended_ref[span, pl.ds(at, 128)].astype(F32) * grad
            for part in range(2):
                own = half == part
                inner = jnp.sum(jnp.where(own, seen, 0.0), axis=-1, keepdims=True)
                high, mid, low = split3(-inner)
                grad_ext = jnp.where(
                    small == 0, high, jnp.where(small == 1, mid, jnp.where(small == 2, low, 0.0))
                ).astype(BF16)
                head = pair * 2 + part
                shift = jnp.sum(
                    jnp.where(small == head, lse_col[block * QB : (block + 1) * QB], 0.0),
                    axis=-1,
                    keepdims=True,
                )
                high, mid, low = split3(-shift)
                query_ext = jnp.where(
                    small == 0,
                    1.0,
                    jnp.where(
                        small == 1, high, jnp.where(small == 2, mid, jnp.where(small == 3, low, 0.0))
                    ),
                ).astype(BF16)
                my_query = jnp.where(own, query, 0.0).astype(BF16)
                my_grad = jnp.where(own, grad, 0.0).astype(BF16)
                weights = jnp.exp(nt(key_full, jnp.concatenate([my_query, query_ext], axis=1)))
                drift = nt(value_full, jnp.concatenate([my_grad, grad_ext], axis=1))
                dscores = (weights * drift).astype(BF16)
                dkey = nn(dscores, my_query)
                dvalue = nn(weights.astype(BF16), my_grad)
                if block == 0 and part == 0:
                    acc_k[...] = dkey
                    acc_v[...] = dvalue
                else:
                    acc_k[...] += dkey
                    acc_v[...] += dvalue
                rows = slice(part * HEAD_DIM, (part + 1) * HEAD_DIM)
                dq_t[rows, span] = nn(key_t[rows], dscores)
        dmixed[:, pl.ds(at, 128)] = (dq_t[...].T * SCALE).astype(BF16)
        dmixed[:, pl.ds(D + at, 128)] = acc_k[...].astype(BF16)
        dmixed[:, pl.ds(2 * D + at, 128)] = acc_v[...].astype(BF16)
        return carry

    lax.fori_loop(0, PAIRS, pair_step, 0)
    unit_a, inverse_a = norm_rows(tokens_ref[...].astype(F32))
    normed_a = (unit_a * misc[0:1] + misc[1:2]).astype(BF16)
    grad_proj_in = tn(normed_a, dmixed[...])
    dnormed_a = nt(dmixed[...], dense_ref[:, : 3 * D])
    grad_tokens_ref[...] = (dresid + norm_back(dnormed_a, unit_a, inverse_a, misc[0:1])).astype(BF16)
    sums = [
        jnp.sum(dnormed_a * unit_a, axis=0, keepdims=True),
        jnp.sum(dnormed_a, axis=0, keepdims=True),
        jnp.sum(dnormed_b * unit_b, axis=0, keepdims=True),
        jnp.sum(dnormed_b, axis=0, keepdims=True),
        jnp.zeros((4, D), F32),
    ]
    sums = jnp.concatenate(sums, axis=0)
    placed = jnp.where(task == 0, pltpu.roll(grad_router, 4, 1), pltpu.roll(grad_router, 12, 1))

    @pl.when(image == 0)
    def _():
        grad_dense_ref[:, : 3 * D] = grad_proj_in
        grad_dense_ref[:, 3 * D : MISC] = grad_proj_out
        grad_dense_ref[:, MISC:] = placed
        grad_rows_ref[...] = sums

    @pl.when(image > 0)
    def _():
        grad_dense_ref[:, : 3 * D] += grad_proj_in
        grad_dense_ref[:, 3 * D : MISC] += grad_proj_out
        grad_dense_ref[:, MISC:] += placed
        grad_rows_ref[...] += sums

    @pl.when(image == pl.num_programs(0) - 1)
    def _():
        columns = jnp.concatenate([grad_rows_ref[...], jnp.zeros((120, D), F32)], axis=0).T
        keep = lanes((D, 128)) < 4
        grad_dense_ref[:, MISC:] = jnp.where(keep, columns, grad_dense_ref[:, MISC:])


def backward_call(
    task_ids, tokens, cotangent, valid, dense, mixed, attended, resid, normed_b, aux, lse, sums, dprobs
):
    images = valid.shape[0]
    rows = images * GRID
    by_image = lambda width: pl.BlockSpec((GRID, width), lambda i, *_: (i, 0))
    whole = lambda shape: pl.BlockSpec(shape, lambda i, *_: (0,) * len(shape))
    lead = lambda shape: pl.BlockSpec((1,) + shape, lambda i, *_: (i, 0, 0))
    return pl.pallas_call(
        backward_kernel,
        grid_spec=pltpu.PrefetchScalarGridSpec(
            num_scalar_prefetch=1,
            grid=(images,),
            in_specs=[
                by_image(D),
                by_image(D),
                whole(valid.shape),
                whole(dense.shape),
                by_image(3 * D),
                by_image(D),
                by_image(D),
                by_image(D),
                by_image(128),
                lead((8, GRID)),
                by_image(2 * D),
                lead((EXPERTS, GRID)),
            ],
            out_specs=[by_image(D), by_image(D), whole((D, DENSE)), whole((8, D))],
            scratch_shapes=[
                pltpu.VMEM((GRID, 3 * D), BF16),
                pltpu.VMEM((GRID, D), BF16),
                pltpu.VMEM((GRID, 128), F32),
                pltpu.VMEM((GRID, 128), F32),
                pltpu.VMEM((128, GRID), F32),
            ],
        ),
        out_shape=[
            jax.ShapeDtypeStruct((rows, D), BF16),
            jax.ShapeDtypeStruct((rows, D), BF16),
            jax.ShapeDtypeStruct((D, DENSE), F32),
            jax.ShapeDtypeStruct((8, D), F32),
        ],
        compiler_params=pltpu.CompilerParams(vmem_limit_bytes=VMEM_LIMIT),
        name="attention_backward",
    )(task_ids, tokens, cotangent, valid, dense, mixed, attended, resid, normed_b, aux, lse, sums, dprobs)


def body(
    tokens,
    cotangent,
    valid,
    task_ids,
    top_counts,
    expert_ids,
    attn_gain,
    attn_shift,
    proj_in,
    proj_out,
    moe_gain,
    moe_shift,
    router,
    expert_in,
    expert_out,
):
    own = attn_gain.shape[0]
    misc = jnp.concatenate(
        [
            jnp.stack([attn_gain, attn_shift, moe_gain, moe_shift], axis=1),
            router[0],
            router[1],
            jnp.zeros((own, 128 - 4 - TASKS * EXPERTS), BF16),
        ],
        axis=1,
    )
    packed = jnp.concatenate([proj_in, proj_out, misc], axis=1)
    dense = lax.all_gather(packed, "wide", axis=0, tiled=True)
    full_in = lax.all_gather(expert_in, "wide", axis=1, tiled=True)
    full_out = lax.all_gather(expert_out, "wide", axis=1, tiled=True)
    mixed, attended, resid, normed_b, aux, rows, lse = forward_call(
        task_ids, top_counts, tokens, valid, expert_ids, dense
    )
    sums, dprobs, grad_in, grad_out = expert_call(normed_b, cotangent, aux, rows, full_in, full_out)
    part_in = lax.psum_scatter(grad_in, "wide", scatter_dimension=1, tiled=True)
    part_out = lax.psum_scatter(grad_out, "wide", scatter_dimension=1, tiled=True)
    output, grad_tokens, grad_dense, _ = backward_call(
        task_ids, tokens, cotangent, valid, dense, mixed, attended, resid, normed_b, aux, lse, sums, dprobs
    )
    part_dense = lax.psum_scatter(grad_dense.astype(BF16), "wide", scatter_dimension=0, tiled=True)
    sum_in, sum_out, sum_dense = lax.psum((part_in, part_out, part_dense), "narrow")
    sum_in = sum_in.astype(F32)
    sum_out = sum_out.astype(F32)
    sum_dense = sum_dense.astype(F32)
    vectors = sum_dense[:, MISC : MISC + 4].T
    grad_router = jnp.stack(
        [sum_dense[:, MISC + 4 : MISC + 12], sum_dense[:, MISC + 12 : MISC + 20]], axis=0
    )
    return (
        output,
        grad_tokens,
        vectors[0],
        vectors[1],
        sum_dense[:, : 3 * D],
        sum_dense[:, 3 * D : MISC],
        vectors[2],
        vectors[3],
        grad_router,
        sum_in,
        sum_out,
    )


def solution(mesh):
    rows = P(("narrow", "wide"), None)
    middle = P(None, "wide", None)
    return jax.shard_map(
        body,
        mesh=mesh,
        in_specs=(
            rows,
            rows,
            rows,
            P(("narrow", "wide")),
            P(),
            rows,
            P("wide"),
            P("wide"),
            P("wide", None),
            P("wide", None),
            P("wide"),
            P("wide"),
            middle,
            middle,
            middle,
        ),
        out_specs=(
            rows,
            rows,
            P("wide"),
            P("wide"),
            P("wide", None),
            P("wide", None),
            P("wide"),
            P("wide"),
            middle,
            middle,
            middle,
        ),
        check_vma=False,
    )
```

```python
import functools
import math

import jax
import jax.numpy as jnp
from jax import lax
from jax.experimental import pallas as pl
from jax.experimental.pallas import tpu as pltpu
from jax.sharding import PartitionSpec as P

D = 384
HEADS = 6
HEAD_DIM = 64
FF = 1536
EXPERTS = 8
TOPMAX = 4
TASKS = 2
GRID = 1024
CAP = 256
PAIRS = HEADS // 2
QB = 256
FC = 512
EPSILON = 1e-06
NEGATIVE = -1e30
SCALE = 1.0 / math.sqrt(HEAD_DIM)
MISC = 3 * D + D
DENSE = MISC + 128

F32 = jnp.float32
BF16 = jnp.bfloat16
VMEM_LIMIT = 60 * 1024 * 1024


def nn(a, b):
    return lax.dot_general(a, b, (((1,), (0,)), ((), ())), preferred_element_type=F32)


def nt(a, b):
    return lax.dot_general(a, b, (((1,), (1,)), ((), ())), preferred_element_type=F32)


def tn(a, b):
    return lax.dot_general(a, b, (((0,), (0,)), ((), ())), preferred_element_type=F32)


def lanes(shape):
    return lax.broadcasted_iota(jnp.int32, shape, 1)


def norm_rows(values):
    center = values - jnp.mean(values, axis=-1, keepdims=True)
    inverse = lax.rsqrt(jnp.mean(center * center, axis=-1, keepdims=True) + EPSILON)
    return center * inverse, inverse


def split3(value):
    high = value.astype(BF16).astype(F32)
    rest = value - high
    mid = rest.astype(BF16).astype(F32)
    return high, mid, rest - mid


def misc_rows(dense_ref):
    return dense_ref[:, MISC:].astype(F32).T


def router_of(dense_ref, task):
    block = dense_ref[:, MISC:].astype(F32)
    first = pltpu.roll(block, 128 - 4, 1)
    second = pltpu.roll(block, 128 - 12, 1)
    chosen = jnp.where(task == 0, first, second)
    return jnp.where(lanes(chosen.shape) < EXPERTS, chosen, 0.0).astype(BF16)


def column_of(row):
    return jnp.broadcast_to(row, (128, row.shape[1])).T


MESH = pl.DeviceIdType.MESH


def hello(first, last, here, there, sems):
    def copy():
        core = lax.axis_index("wide") ^ 1
        return pltpu.make_async_remote_copy(
            src_ref=here, dst_ref=there, send_sem=sems.at[0], recv_sem=sems.at[1],
            device_id={"wide": core}, device_id_type=MESH)

    @pl.when(first)
    def _():
        barrier = pltpu.get_barrier_semaphore()
        pl.semaphore_signal(barrier, inc=1, device_id={"wide": lax.axis_index("wide") ^ 1}, device_id_type=MESH)
        pl.semaphore_wait(barrier, 1)
        here[...] = jnp.ones_like(here)
        copy().start()

    @pl.when(last)
    def _():
        copy().wait()


HELLO = [pltpu.VMEM((16, 128), jnp.bfloat16), pltpu.VMEM((16, 128), jnp.bfloat16), pltpu.SemaphoreType.DMA((2,))]


def forward_kernel(
    task_ref,
    count_ref,
    tokens_ref,
    valid_ref,
    ids_ref,
    dense_ref,
    mixed_ref,
    attended_ref,
    resid_ref,
    normed_ref,
    aux_ref,
    rows_ref,
    lse_ref,
    att_t,
    *more,
):
    hello(pl.program_id(0) == 0, pl.program_id(0) == pl.num_programs(0) - 1, *more)
    image = pl.program_id(0)
    task = task_ref[image]
    count = count_ref[task]
    misc = misc_rows(dense_ref)
    inputs = tokens_ref[...].astype(F32)
    unit_a, _ = norm_rows(inputs)
    normed_a = (unit_a * misc[0:1] + misc[1:2]).astype(BF16)
    mixed_ref[...] = nn(normed_a, dense_ref[:, : 3 * D]).astype(BF16)
    live_col = column_of(valid_ref[pl.ds(image, 1), :].astype(F32))
    lane = lanes((GRID, 128))
    key_ext = jnp.where((lane == 0) & (live_col < 0.5), NEGATIVE, 0.0).astype(BF16)
    query_ext = jnp.where(lanes((QB, 128)) == 0, 1.0, 0.0).astype(BF16)
    ones_rows = jnp.ones((16, GRID), BF16)

    def pair_step(pair, carry):
        at = pl.multiple_of(pair * 128, 128)
        keys = mixed_ref[:, pl.ds(D + at, 128)]
        values = mixed_ref[:, pl.ds(2 * D + at, 128)]
        key_full = jnp.concatenate([keys, key_ext], axis=1)
        value_t = jnp.concatenate([values.astype(F32).T.astype(BF16), ones_rows], axis=0)
        half = lanes((QB, 128)) // HEAD_DIM
        for block in range(GRID // QB):
            span = pl.ds(block * QB, QB)
            query = mixed_ref[span, pl.ds(at, 128)].astype(F32) * SCALE
            for part in range(2):
                own = jnp.where(half == part, query, 0.0).astype(BF16)
                scores = nt(key_full, jnp.concatenate([own, query_ext], axis=1))
                top = jnp.max(scores, axis=0, keepdims=True)
                raised = jnp.exp(scores - top).astype(BF16)
                produced = nn(value_t, raised)
                total = produced[128:129]
                mine = produced[part * HEAD_DIM : (part + 1) * HEAD_DIM] / total
                att_t[pl.ds(at + part * HEAD_DIM, HEAD_DIM), span] = mine
                lse_ref[0, pl.ds(pair * 2 + part, 1), span] = top + jnp.log(total)
        return carry

    lax.fori_loop(0, PAIRS, pair_step, 0)
    lse_ref[0, HEADS:, :] = jnp.zeros((8 - HEADS, GRID), F32)
    attended = att_t[...].T.astype(BF16)
    attended_ref[...] = attended
    resid = inputs + nn(attended, dense_ref[:, 3 * D : MISC])
    resid_ref[...] = resid
    unit_b, _ = norm_rows(resid)
    normed_b = (unit_b * misc[2:3] + misc[3:4]).astype(BF16)
    normed_ref[...] = normed_b
    logits = nn(normed_b, router_of(dense_ref, task))
    logits = jnp.where(lane < EXPERTS, logits, NEGATIVE)
    raised = jnp.exp(logits - jnp.max(logits, axis=-1, keepdims=True))
    probs = raised / jnp.sum(raised, axis=-1, keepdims=True)
    choice = lane // EXPERTS
    wanted = jnp.full((GRID, 128), -1, jnp.int32)
    for rank in range(TOPMAX):
        wanted = jnp.where(choice == rank, ids_ref[:, rank : rank + 1], wanted)
    used = (wanted == lane % EXPERTS) & (choice < count) & (live_col > 0.5)
    used = jnp.where(used, 1.0, 0.0)
    span = 256
    row_at = lax.broadcasted_iota(jnp.int32, (span, span), 0)
    earlier = jnp.where(row_at > lanes((span, span)), 1.0, 0.0).astype(BF16)
    running = jnp.zeros((1, 128), F32)
    pieces = []
    for block in range(GRID // span):
        part = used[block * span : (block + 1) * span]
        pieces.append(nn(earlier, part.astype(BF16)) + running)
        running = running + jnp.sum(part, axis=0, keepdims=True)
    before = jnp.concatenate(pieces, axis=0)
    totals = jnp.broadcast_to(running, (8, 128))
    lane8 = lanes((8, 128))
    base = jnp.zeros((8, 128), F32)
    for rank in range(1, TOPMAX):
        shift = rank * EXPERTS
        base = base + jnp.where(lane8 >= shift, pltpu.roll(totals, shift, 1), 0.0)
    slot = before + base[0:1]
    found = jnp.where((used > 0.5) & (slot < CAP), slot + 1.0, 0.0)
    folded = found
    for rank in range(1, TOPMAX):
        folded = folded + pltpu.roll(found, 128 - rank * EXPERTS, 1)
    slots = jnp.where(lane < EXPERTS, folded - 1.0, -1.0)
    gates = jnp.where(slots >= 0.0, probs, 0.0)
    aux = probs + jnp.where(
        (choice == 1), pltpu.roll(slots, EXPERTS, 1), 0.0
    ) + jnp.where(choice == 2, pltpu.roll(gates, 2 * EXPERTS, 1), 0.0)
    aux_ref[...] = aux
    rows_ref[0] = aux.T[0 : 4 * EXPERTS]


def forward_call(task_ids, top_counts, tokens, valid, expert_ids, dense):
    images = valid.shape[0]
    rows = images * GRID
    smem = pl.BlockSpec(memory_space=pltpu.SMEM)
    by_image = lambda width: pl.BlockSpec((GRID, width), lambda i, *_: (i, 0))
    whole = lambda shape: pl.BlockSpec(shape, lambda i, *_: (0,) * len(shape))
    lead = lambda shape: pl.BlockSpec((1,) + shape, lambda i, *_: (i, 0, 0))
    return pl.pallas_call(
        forward_kernel,
        grid_spec=pltpu.PrefetchScalarGridSpec(
            num_scalar_prefetch=0,
            grid=(images,),
            in_specs=[smem, smem, by_image(D), whole(valid.shape), by_image(TOPMAX), whole(dense.shape)],
            out_specs=[
                by_image(3 * D),
                by_image(D),
                by_image(D),
                by_image(D),
                by_image(128),
                lead((4 * EXPERTS, GRID)),
                lead((8, GRID)),
            ],
            scratch_shapes=[pltpu.VMEM((D, GRID), F32)] + HELLO,
        ),
        out_shape=[
            jax.ShapeDtypeStruct((rows, 3 * D), BF16),
            jax.ShapeDtypeStruct((rows, D), BF16),
            jax.ShapeDtypeStruct((rows, D), F32),
            jax.ShapeDtypeStruct((rows, D), BF16),
            jax.ShapeDtypeStruct((rows, 128), F32),
            jax.ShapeDtypeStruct((images, 4 * EXPERTS, GRID), F32),
            jax.ShapeDtypeStruct((images, 8, GRID), F32),
        ],
        compiler_params=pltpu.CompilerParams(vmem_limit_bytes=VMEM_LIMIT, collective_id=0, has_side_effects=True),
        name="attention_forward",
    )(task_ids, top_counts, tokens, valid, expert_ids, dense)


def expert_kernel(
    images,
    normed_ref,
    cot_ref,
    aux_ref,
    rows_ref,
    in_ref,
    out_ref,
    sums_ref,
    dprobs_ref,
    grad_in_ref,
    grad_out_ref,
    both,
    given,
    upstream,
    dres_s,
    *more,
):
    hello(pl.program_id(0) == 0, pl.program_id(0) == pl.num_programs(0) - 1, *more)
    expert = pl.program_id(0)

    @pl.when(expert == 0)
    def _():
        for image in range(images):
            span = pl.ds(image * GRID, GRID)
            both[span, :D] = normed_ref[span, :]
            both[span, D:] = cot_ref[span, :]

    slot_at = lax.broadcasted_iota(jnp.int32, (CAP, GRID), 0).astype(F32)
    for image in range(images):
        part = pl.ds(image * CAP, CAP)
        slot_row = rows_ref[image, pl.ds(EXPERTS + expert, 1), :]
        gate_row = rows_ref[image, pl.ds(2 * EXPERTS + expert, 1), :]
        match = slot_at == slot_row
        sent = nn(jnp.where(match, 1.0, 0.0).astype(BF16), both[pl.ds(image * GRID, GRID), :])
        gate = jnp.sum(jnp.where(match, gate_row, 0.0), axis=1, keepdims=True)
        given[part, :] = sent[:, :D].astype(BF16)
        upstream[part, :D] = sent[:, D:]
        upstream[part, D:] = jnp.broadcast_to(gate, (CAP, 128))
        dres_s[part, :] = (gate * sent[:, D:]).astype(BF16)
    slots = given[...]
    dres = dres_s[...]
    result = jnp.zeros((images * CAP, D), F32)
    back = jnp.zeros((images * CAP, D), F32)
    c1 = math.sqrt(2.0 / math.pi)
    c3 = c1 * 0.044715
    for chunk in range(FF // FC):
        span = pl.ds(chunk * FC, FC)
        w_in = in_ref[0, :, span]
        w_out = out_ref[0, span, :]
        pre = nn(slots, w_in)
        square = pre * pre
        curve = jnp.tanh(pre * (c1 + c3 * square))
        lifted = 0.5 * (1.0 + curve)
        hidden = (pre * lifted).astype(BF16)
        slope = lifted + (0.5 * pre) * (1.0 - curve * curve) * (c1 + (3.0 * c3) * square)
        result = result + nn(hidden, w_out)
        dpre = (nt(dres, w_out) * slope).astype(BF16)
        back = back + nt(dpre, w_in)
        grad_out_ref[0, span, :] = tn(hidden, dres).astype(grad_out_ref.dtype)
        grad_in_ref[0, :, span] = tn(slots, dpre).astype(grad_in_ref.dtype)
    result = result.astype(BF16).astype(F32)
    dgate = jnp.sum(result * upstream[:, :D], axis=1, keepdims=True)
    gated = result * upstream[:, D : D + 1]
    returned = jnp.concatenate([gated.astype(BF16), back.astype(BF16)], axis=1)
    for image in range(images):
        part = slice(image * CAP, (image + 1) * CAP)
        span = pl.ds(image * GRID, GRID)
        slot_row = rows_ref[image, pl.ds(EXPERTS + expert, 1), :]
        match = slot_at == slot_row
        dprobs_ref[image, pl.ds(expert, 1), :] = jnp.sum(
            jnp.where(match, dgate[part], 0.0), axis=0, keepdims=True
        )
        hit = jnp.where(match, 1.0, 0.0).astype(BF16)
        landed = tn(hit, returned[part])

        @pl.when(expert == 0)
        def _():
            sums_ref[span, :] = landed

        @pl.when(expert > 0)
        def _():
            sums_ref[span, :] = sums_ref[span, :] + landed


def expert_call(normed_b, cotangent, aux, rows, expert_in, expert_out):
    images = rows.shape[0]
    count = images * GRID
    whole = lambda shape: pl.BlockSpec(shape, lambda e: (0,) * len(shape))
    return pl.pallas_call(
        functools.partial(expert_kernel, images),
        grid=(EXPERTS,),
        in_specs=[
            whole((count, D)),
            whole((count, D)),
            whole((count, 128)),
            whole(rows.shape),
            pl.BlockSpec((1, D, FF), lambda e: (e, 0, 0)),
            pl.BlockSpec((1, FF, D), lambda e: (e, 0, 0)),
        ],
        out_specs=[
            whole((count, 2 * D)),
            whole((images, EXPERTS, GRID)),
            pl.BlockSpec((1, D, FF), lambda e: (e, 0, 0)),
            pl.BlockSpec((1, FF, D), lambda e: (e, 0, 0)),
        ],
        out_shape=[
            jax.ShapeDtypeStruct((count, 2 * D), F32),
            jax.ShapeDtypeStruct((images, EXPERTS, GRID), F32),
            jax.ShapeDtypeStruct((EXPERTS, D, FF), BF16),
            jax.ShapeDtypeStruct((EXPERTS, FF, D), BF16),
        ],
        scratch_shapes=[
            pltpu.VMEM((count, 2 * D), BF16),
            pltpu.VMEM((images * CAP, D), BF16),
            pltpu.VMEM((images * CAP, D + 128), F32),
            pltpu.VMEM((images * CAP, D), BF16),
        ] + HELLO,
        compiler_params=pltpu.CompilerParams(vmem_limit_bytes=VMEM_LIMIT, collective_id=1, has_side_effects=True),
        name="experts",
    )(normed_b, cotangent, aux, rows, expert_in, expert_out)


def norm_back(upstream, unit_rows, inverse, gain):
    scaled = upstream * gain
    centered = scaled - jnp.mean(scaled, axis=-1, keepdims=True)
    centered = centered - unit_rows * jnp.mean(scaled * unit_rows, axis=-1, keepdims=True)
    return inverse * centered


def backward_kernel(
    task_ref,
    tokens_ref,
    cot_ref,
    valid_ref,
    dense_ref,
    mixed_ref,
    attended_ref,
    resid_ref,
    normed_ref,
    aux_ref,
    lse_ref,
    sums_ref,
    dprobs_ref,
    output_ref,
    grad_tokens_ref,
    grad_dense_ref,
    grad_rows_ref,
    dmixed,
    dattended,
    acc_k,
    acc_v,
    dq_t,
    *more,
):
    hello(pl.program_id(0) == 0, pl.program_id(0) == pl.num_programs(0) - 1, *more)
    image = pl.program_id(0)
    task = task_ref[image]
    misc = misc_rows(dense_ref)
    lane = lanes((GRID, 128))
    upstream = cot_ref[...].astype(F32)
    resid = resid_ref[...]
    output_ref[...] = (resid + sums_ref[:, :D]).astype(BF16)
    unit_b, inverse_b = norm_rows(resid)
    probs = jnp.where(lane < EXPERTS, aux_ref[...], 0.0)
    dprobs = jnp.concatenate(
        [dprobs_ref[0], jnp.zeros((128 - EXPERTS, GRID), F32)], axis=0
    ).T
    dlogits = probs * (dprobs - jnp.sum(dprobs * probs, axis=-1, keepdims=True))
    dlogits = dlogits.astype(BF16)
    router = router_of(dense_ref, task)
    grad_router = tn(normed_ref[...], dlogits)
    dnormed_b = sums_ref[:, D:] + nt(dlogits, router)
    dresid = upstream + norm_back(dnormed_b, unit_b, inverse_b, misc[2:3])
    dbranch = dresid.astype(BF16)
    grad_proj_out = tn(attended_ref[...], dbranch)
    dattended[...] = nt(dbranch, dense_ref[:, 3 * D : MISC]).astype(BF16)
    live_col = column_of(valid_ref[pl.ds(image, 1), :].astype(F32))
    lse_col = jnp.concatenate([lse_ref[0], jnp.zeros((120, GRID), F32)], axis=0).T
    key_ext = jnp.where((lane == 0) & (live_col < 0.5), NEGATIVE, 0.0)
    key_ext = jnp.where((lane >= 1) & (lane <= 3), 1.0, key_ext).astype(BF16)
    value_ext = jnp.where(lane < 3, 1.0, 0.0).astype(BF16)
    small = lanes((QB, 128))
    half = small // HEAD_DIM

    def pair_step(pair, carry):
        at = pl.multiple_of(pair * 128, 128)
        keys = mixed_ref[:, pl.ds(D + at, 128)]
        values = mixed_ref[:, pl.ds(2 * D + at, 128)]
        key_full = jnp.concatenate([keys, key_ext], axis=1)
        value_full = jnp.concatenate([values, value_ext], axis=1)
        key_t = keys.astype(F32).T.astype(BF16)
        for block in range(GRID // QB):
            span = pl.ds(block * QB, QB)
            query = mixed_ref[span, pl.ds(at, 128)].astype(F32) * SCALE
            grad = dattended[span, pl.ds(at, 128)].astype(F32)
            seen = attended_ref[span, pl.ds(at, 128)].astype(F32) * grad
            for part in range(2):
                own = half == part
                inner = jnp.sum(jnp.where(own, seen, 0.0), axis=-1, keepdims=True)
                high, mid, low = split3(-inner)
                grad_ext = jnp.where(
                    small == 0, high, jnp.where(small == 1, mid, jnp.where(small == 2, low, 0.0))
                ).astype(BF16)
                head = pair * 2 + part
                shift = jnp.sum(
                    jnp.where(small == head, lse_col[block * QB : (block + 1) * QB], 0.0),
                    axis=-1,
                    keepdims=True,
                )
                high, mid, low = split3(-shift)
                query_ext = jnp.where(
                    small == 0,
                    1.0,
                    jnp.where(
                        small == 1, high, jnp.where(small == 2, mid, jnp.where(small == 3, low, 0.0))
                    ),
                ).astype(BF16)
                my_query = jnp.where(own, query, 0.0).astype(BF16)
                my_grad = jnp.where(own, grad, 0.0).astype(BF16)
                weights = jnp.exp(nt(key_full, jnp.concatenate([my_query, query_ext], axis=1)))
                drift = nt(value_full, jnp.concatenate([my_grad, grad_ext], axis=1))
                dscores = (weights * drift).astype(BF16)
                dkey = nn(dscores, my_query)
                dvalue = nn(weights.astype(BF16), my_grad)
                if block == 0 and part == 0:
                    acc_k[...] = dkey
                    acc_v[...] = dvalue
                else:
                    acc_k[...] += dkey
                    acc_v[...] += dvalue
                rows = slice(part * HEAD_DIM, (part + 1) * HEAD_DIM)
                dq_t[rows, span] = nn(key_t[rows], dscores)
        dmixed[:, pl.ds(at, 128)] = (dq_t[...].T * SCALE).astype(BF16)
        dmixed[:, pl.ds(D + at, 128)] = acc_k[...].astype(BF16)
        dmixed[:, pl.ds(2 * D + at, 128)] = acc_v[...].astype(BF16)
        return carry

    lax.fori_loop(0, PAIRS, pair_step, 0)
    unit_a, inverse_a = norm_rows(tokens_ref[...].astype(F32))
    normed_a = (unit_a * misc[0:1] + misc[1:2]).astype(BF16)
    grad_proj_in = tn(normed_a, dmixed[...])
    dnormed_a = nt(dmixed[...], dense_ref[:, : 3 * D])
    grad_tokens_ref[...] = (dresid + norm_back(dnormed_a, unit_a, inverse_a, misc[0:1])).astype(BF16)
    sums = [
        jnp.sum(dnormed_a * unit_a, axis=0, keepdims=True),
        jnp.sum(dnormed_a, axis=0, keepdims=True),
        jnp.sum(dnormed_b * unit_b, axis=0, keepdims=True),
        jnp.sum(dnormed_b, axis=0, keepdims=True),
        jnp.zeros((4, D), F32),
    ]
    sums = jnp.concatenate(sums, axis=0)
    placed = jnp.where(task == 0, pltpu.roll(grad_router, 4, 1), pltpu.roll(grad_router, 12, 1))

    @pl.when(image == 0)
    def _():
        grad_dense_ref[:, : 3 * D] = grad_proj_in
        grad_dense_ref[:, 3 * D : MISC] = grad_proj_out
        grad_dense_ref[:, MISC:] = placed
        grad_rows_ref[...] = sums

    @pl.when(image > 0)
    def _():
        grad_dense_ref[:, : 3 * D] += grad_proj_in
        grad_dense_ref[:, 3 * D : MISC] += grad_proj_out
        grad_dense_ref[:, MISC:] += placed
        grad_rows_ref[...] += sums

    @pl.when(image == pl.num_programs(0) - 1)
    def _():
        columns = jnp.concatenate([grad_rows_ref[...], jnp.zeros((120, D), F32)], axis=0).T
        keep = lanes((D, 128)) < 4
        grad_dense_ref[:, MISC:] = jnp.where(keep, columns, grad_dense_ref[:, MISC:])


def backward_call(
    task_ids, tokens, cotangent, valid, dense, mixed, attended, resid, normed_b, aux, lse, sums, dprobs
):
    images = valid.shape[0]
    rows = images * GRID
    smem = pl.BlockSpec(memory_space=pltpu.SMEM)
    by_image = lambda width: pl.BlockSpec((GRID, width), lambda i, *_: (i, 0))
    whole = lambda shape: pl.BlockSpec(shape, lambda i, *_: (0,) * len(shape))
    lead = lambda shape: pl.BlockSpec((1,) + shape, lambda i, *_: (i, 0, 0))
    return pl.pallas_call(
        backward_kernel,
        grid_spec=pltpu.PrefetchScalarGridSpec(
            num_scalar_prefetch=0,
            grid=(images,),
            in_specs=[
                smem,
                by_image(D),
                by_image(D),
                whole(valid.shape),
                whole(dense.shape),
                by_image(3 * D),
                by_image(D),
                by_image(D),
                by_image(D),
                by_image(128),
                lead((8, GRID)),
                by_image(2 * D),
                lead((EXPERTS, GRID)),
            ],
            out_specs=[by_image(D), by_image(D), whole((D, DENSE)), whole((8, D))],
            scratch_shapes=[
                pltpu.VMEM((GRID, 3 * D), BF16),
                pltpu.VMEM((GRID, D), BF16),
                pltpu.VMEM((GRID, 128), F32),
                pltpu.VMEM((GRID, 128), F32),
                pltpu.VMEM((128, GRID), F32),
            ] + HELLO,
        ),
        out_shape=[
            jax.ShapeDtypeStruct((rows, D), BF16),
            jax.ShapeDtypeStruct((rows, D), BF16),
            jax.ShapeDtypeStruct((D, DENSE), F32),
            jax.ShapeDtypeStruct((8, D), F32),
        ],
        compiler_params=pltpu.CompilerParams(vmem_limit_bytes=VMEM_LIMIT, collective_id=2, has_side_effects=True),
        name="attention_backward",
    )(task_ids, tokens, cotangent, valid, dense, mixed, attended, resid, normed_b, aux, lse, sums, dprobs)


def body(
    tokens,
    cotangent,
    valid,
    task_ids,
    top_counts,
    expert_ids,
    attn_gain,
    attn_shift,
    proj_in,
    proj_out,
    moe_gain,
    moe_shift,
    router,
    expert_in,
    expert_out,
):
    own = attn_gain.shape[0]
    misc = jnp.concatenate(
        [
            jnp.stack([attn_gain, attn_shift, moe_gain, moe_shift], axis=1),
            router[0],
            router[1],
            jnp.zeros((own, 128 - 4 - TASKS * EXPERTS), BF16),
        ],
        axis=1,
    )
    packed = jnp.concatenate([proj_in, proj_out, misc], axis=1)
    dense = lax.all_gather(packed, "wide", axis=0, tiled=True)
    full_in = lax.all_gather(expert_in, "wide", axis=1, tiled=True)
    full_out = lax.all_gather(expert_out, "wide", axis=1, tiled=True)
    mixed, attended, resid, normed_b, aux, rows, lse = forward_call(
        task_ids, top_counts, tokens, valid, expert_ids, dense
    )
    sums, dprobs, grad_in, grad_out = expert_call(normed_b, cotangent, aux, rows, full_in, full_out)
    part_in = lax.psum_scatter(grad_in, "wide", scatter_dimension=1, tiled=True)
    part_out = lax.psum_scatter(grad_out, "wide", scatter_dimension=1, tiled=True)
    output, grad_tokens, grad_dense, _ = backward_call(
        task_ids, tokens, cotangent, valid, dense, mixed, attended, resid, normed_b, aux, lse, sums, dprobs
    )
    part_dense = lax.psum_scatter(grad_dense.astype(BF16), "wide", scatter_dimension=0, tiled=True)
    sum_in, sum_out, sum_dense = lax.psum((part_in, part_out, part_dense), "narrow")
    sum_in = sum_in.astype(F32)
    sum_out = sum_out.astype(F32)
    sum_dense = sum_dense.astype(F32)
    vectors = sum_dense[:, MISC : MISC + 4].T
    grad_router = jnp.stack(
        [sum_dense[:, MISC + 4 : MISC + 12], sum_dense[:, MISC + 12 : MISC + 20]], axis=0
    )
    return (
        output,
        grad_tokens,
        vectors[0],
        vectors[1],
        sum_dense[:, : 3 * D],
        sum_dense[:, 3 * D : MISC],
        vectors[2],
        vectors[3],
        grad_router,
        sum_in,
        sum_out,
    )


def solution(mesh):
    rows = P(("narrow", "wide"), None)
    middle = P(None, "wide", None)
    return jax.shard_map(
        body,
        mesh=mesh,
        in_specs=(
            rows,
            rows,
            rows,
            P(("narrow", "wide")),
            P(),
            rows,
            P("wide"),
            P("wide"),
            P("wide", None),
            P("wide", None),
            P("wide"),
            P("wide"),
            middle,
            middle,
            middle,
        ),
        out_specs=(
            rows,
            rows,
            P("wide"),
            P("wide"),
            P("wide", None),
            P("wide", None),
            P("wide"),
            P("wide"),
            middle,
            middle,
            middle,
        ),
        check_vma=False,
    )
```

```python
import functools
import math

import jax
import jax.numpy as jnp
from jax import lax
from jax.experimental import pallas as pl
from jax.experimental.pallas import tpu as pltpu
from jax.sharding import PartitionSpec as P

D = 384
HEADS = 6
HEAD_DIM = 64
FF = 1536
EXPERTS = 8
TOPMAX = 4
TASKS = 2
GRID = 1024
CAP = 256
PAIRS = HEADS // 2
QB = 256
FC = 512
EPSILON = 1e-06
NEGATIVE = -1e30
SCALE = 1.0 / math.sqrt(HEAD_DIM)
MISC = 3 * D + D
DENSE = MISC + 128

F32 = jnp.float32
BF16 = jnp.bfloat16
VMEM_LIMIT = 60 * 1024 * 1024


def nn(a, b):
    return lax.dot_general(a, b, (((1,), (0,)), ((), ())), preferred_element_type=F32)


def nt(a, b):
    return lax.dot_general(a, b, (((1,), (1,)), ((), ())), preferred_element_type=F32)


def tn(a, b):
    return lax.dot_general(a, b, (((0,), (0,)), ((), ())), preferred_element_type=F32)


def lanes(shape):
    return lax.broadcasted_iota(jnp.int32, shape, 1)


def norm_rows(values):
    center = values - jnp.mean(values, axis=-1, keepdims=True)
    inverse = lax.rsqrt(jnp.mean(center * center, axis=-1, keepdims=True) + EPSILON)
    return center * inverse, inverse


def split3(value):
    high = value.astype(BF16).astype(F32)
    rest = value - high
    mid = rest.astype(BF16).astype(F32)
    return high, mid, rest - mid


def misc_rows(dense_ref):
    return dense_ref[:, MISC:].astype(F32).T


def router_of(dense_ref, task):
    block = dense_ref[:, MISC:].astype(F32)
    first = pltpu.roll(block, 128 - 4, 1)
    second = pltpu.roll(block, 128 - 12, 1)
    chosen = jnp.where(task == 0, first, second)
    return jnp.where(lanes(chosen.shape) < EXPERTS, chosen, 0.0).astype(BF16)


def column_of(row):
    return jnp.broadcast_to(row, (128, row.shape[1])).T


def forward_kernel(
    task_ref,
    count_ref,
    tokens_ref,
    valid_ref,
    ids_ref,
    dense_ref,
    mixed_ref,
    attended_ref,
    resid_ref,
    normed_ref,
    aux_ref,
    rows_ref,
    lse_ref,
    att_t,
):
    image = pl.program_id(0)
    task = task_ref[image]
    count = count_ref[task]
    misc = misc_rows(dense_ref)
    inputs = tokens_ref[...].astype(F32)
    unit_a, _ = norm_rows(inputs)
    normed_a = (unit_a * misc[0:1] + misc[1:2]).astype(BF16)
    mixed_ref[...] = nn(normed_a, dense_ref[:, : 3 * D]).astype(BF16)
    live_col = column_of(valid_ref[pl.ds(image, 1), :].astype(F32))
    lane = lanes((GRID, 128))
    key_ext = jnp.where((lane == 0) & (live_col < 0.5), NEGATIVE, 0.0).astype(BF16)
    query_ext = jnp.where(lanes((QB, 128)) == 0, 1.0, 0.0).astype(BF16)
    ones_rows = jnp.ones((16, GRID), BF16)

    def pair_step(pair, carry):
        at = pl.multiple_of(pair * 128, 128)
        keys = mixed_ref[:, pl.ds(D + at, 128)]
        values = mixed_ref[:, pl.ds(2 * D + at, 128)]
        key_full = jnp.concatenate([keys, key_ext], axis=1)
        value_t = jnp.concatenate([values.astype(F32).T.astype(BF16), ones_rows], axis=0)
        half = lanes((QB, 128)) // HEAD_DIM
        for block in range(GRID // QB):
            span = pl.ds(block * QB, QB)
            query = mixed_ref[span, pl.ds(at, 128)].astype(F32) * SCALE
            for part in range(2):
                own = jnp.where(half == part, query, 0.0).astype(BF16)
                scores = nt(key_full, jnp.concatenate([own, query_ext], axis=1))
                top = jnp.max(scores, axis=0, keepdims=True)
                raised = jnp.exp(scores - top).astype(BF16)
                produced = nn(value_t, raised)
                total = produced[128:129]
                mine = produced[part * HEAD_DIM : (part + 1) * HEAD_DIM] / total
                att_t[pl.ds(at + part * HEAD_DIM, HEAD_DIM), span] = mine
                lse_ref[0, pl.ds(pair * 2 + part, 1), span] = top + jnp.log(total)
        return carry

    lax.fori_loop(0, PAIRS, pair_step, 0)
    lse_ref[0, HEADS:, :] = jnp.zeros((8 - HEADS, GRID), F32)
    attended = att_t[...].T.astype(BF16)
    attended_ref[...] = attended
    resid = inputs + nn(attended, dense_ref[:, 3 * D : MISC])
    resid_ref[...] = resid
    unit_b, _ = norm_rows(resid)
    normed_b = (unit_b * misc[2:3] + misc[3:4]).astype(BF16)
    normed_ref[...] = normed_b
    logits = nn(normed_b, router_of(dense_ref, task))
    logits = jnp.where(lane < EXPERTS, logits, NEGATIVE)
    raised = jnp.exp(logits - jnp.max(logits, axis=-1, keepdims=True))
    probs = raised / jnp.sum(raised, axis=-1, keepdims=True)
    choice = lane // EXPERTS
    wanted = jnp.full((GRID, 128), -1, jnp.int32)
    for rank in range(TOPMAX):
        wanted = jnp.where(choice == rank, ids_ref[:, rank : rank + 1], wanted)
    used = (wanted == lane % EXPERTS) & (choice < count) & (live_col > 0.5)
    used = jnp.where(used, 1.0, 0.0)
    span = 256
    row_at = lax.broadcasted_iota(jnp.int32, (span, span), 0)
    earlier = jnp.where(row_at > lanes((span, span)), 1.0, 0.0).astype(BF16)
    running = jnp.zeros((1, 128), F32)
    pieces = []
    for block in range(GRID // span):
        part = used[block * span : (block + 1) * span]
        pieces.append(nn(earlier, part.astype(BF16)) + running)
        running = running + jnp.sum(part, axis=0, keepdims=True)
    before = jnp.concatenate(pieces, axis=0)
    totals = jnp.broadcast_to(running, (8, 128))
    lane8 = lanes((8, 128))
    base = jnp.zeros((8, 128), F32)
    for rank in range(1, TOPMAX):
        shift = rank * EXPERTS
        base = base + jnp.where(lane8 >= shift, pltpu.roll(totals, shift, 1), 0.0)
    slot = before + base[0:1]
    found = jnp.where((used > 0.5) & (slot < CAP), slot + 1.0, 0.0)
    folded = found
    for rank in range(1, TOPMAX):
        folded = folded + pltpu.roll(found, 128 - rank * EXPERTS, 1)
    slots = jnp.where(lane < EXPERTS, folded - 1.0, -1.0)
    gates = jnp.where(slots >= 0.0, probs, 0.0)
    aux = probs + jnp.where(
        (choice == 1), pltpu.roll(slots, EXPERTS, 1), 0.0
    ) + jnp.where(choice == 2, pltpu.roll(gates, 2 * EXPERTS, 1), 0.0)
    aux_ref[...] = aux
    rows_ref[0] = aux.T[0 : 4 * EXPERTS]


def forward_call(task_ids, top_counts, tokens, valid, expert_ids, dense):
    images = valid.shape[0]
    rows = images * GRID
    by_image = lambda width: pl.BlockSpec((GRID, width), lambda i, *_: (i, 0))
    whole = lambda shape: pl.BlockSpec(shape, lambda i, *_: (0,) * len(shape))
    lead = lambda shape: pl.BlockSpec((1,) + shape, lambda i, *_: (i, 0, 0))
    return pl.pallas_call(
        forward_kernel,
        grid_spec=pltpu.PrefetchScalarGridSpec(
            num_scalar_prefetch=2,
            grid=(images,),
            in_specs=[by_image(D), whole(valid.shape), by_image(TOPMAX), whole(dense.shape)],
            out_specs=[
                by_image(3 * D),
                by_image(D),
                by_image(D),
                by_image(D),
                by_image(128),
                lead((4 * EXPERTS, GRID)),
                lead((8, GRID)),
            ],
            scratch_shapes=[pltpu.VMEM((D, GRID), F32)],
        ),
        out_shape=[
            jax.ShapeDtypeStruct((rows, 3 * D), BF16),
            jax.ShapeDtypeStruct((rows, D), BF16),
            jax.ShapeDtypeStruct((rows, D), F32),
            jax.ShapeDtypeStruct((rows, D), BF16),
            jax.ShapeDtypeStruct((rows, 128), F32),
            jax.ShapeDtypeStruct((images, 4 * EXPERTS, GRID), F32),
            jax.ShapeDtypeStruct((images, 8, GRID), F32),
        ],
        compiler_params=pltpu.CompilerParams(vmem_limit_bytes=VMEM_LIMIT),
        name="attention_forward",
    )(task_ids, top_counts, tokens, valid, expert_ids, dense)


def expert_kernel(
    images,
    normed_ref,
    cot_ref,
    aux_ref,
    rows_ref,
    in_ref,
    out_ref,
    sums_ref,
    dprobs_ref,
    grad_in_ref,
    grad_out_ref,
    both,
    given,
    upstream,
    dres_s,
):
    expert = pl.program_id(0)

    @pl.when(expert == 0)
    def _():
        for image in range(images):
            span = pl.ds(image * GRID, GRID)
            both[span, :D] = normed_ref[span, :]
            both[span, D:] = cot_ref[span, :]

    slot_at = lax.broadcasted_iota(jnp.int32, (CAP, GRID), 0).astype(F32)
    for image in range(images):
        part = pl.ds(image * CAP, CAP)
        slot_row = rows_ref[image, pl.ds(EXPERTS + expert, 1), :]
        gate_row = rows_ref[image, pl.ds(2 * EXPERTS + expert, 1), :]
        match = slot_at == slot_row
        sent = nn(jnp.where(match, 1.0, 0.0).astype(BF16), both[pl.ds(image * GRID, GRID), :])
        gate = jnp.sum(jnp.where(match, gate_row, 0.0), axis=1, keepdims=True)
        given[part, :] = sent[:, :D].astype(BF16)
        upstream[part, :D] = sent[:, D:]
        upstream[part, D:] = jnp.broadcast_to(gate, (CAP, 128))
        dres_s[part, :] = (gate * sent[:, D:]).astype(BF16)
    slots = given[...]
    dres = dres_s[...]
    result = jnp.zeros((images * CAP, D), F32)
    back = jnp.zeros((images * CAP, D), F32)
    c1 = math.sqrt(2.0 / math.pi)
    c3 = c1 * 0.044715
    for chunk in range(FF // FC):
        span = pl.ds(chunk * FC, FC)
        w_in = in_ref[0, :, span]
        w_out = out_ref[0, span, :]
        pre = nn(slots, w_in)
        square = pre * pre
        curve = jnp.tanh(pre * (c1 + c3 * square))
        lifted = 0.5 * (1.0 + curve)
        hidden = (pre * lifted).astype(BF16)
        slope = lifted + (0.5 * pre) * (1.0 - curve * curve) * (c1 + (3.0 * c3) * square)
        result = result + nn(hidden, w_out)
        dpre = (nt(dres, w_out) * slope).astype(BF16)
        back = back + nt(dpre, w_in)
        grad_out_ref[0, span, :] = tn(hidden, dres).astype(grad_out_ref.dtype)
        grad_in_ref[0, :, span] = tn(slots, dpre).astype(grad_in_ref.dtype)
    result = result.astype(BF16).astype(F32)
    dgate = jnp.sum(result * upstream[:, :D], axis=1, keepdims=True)
    gated = result * upstream[:, D : D + 1]
    returned = jnp.concatenate([gated.astype(BF16), back.astype(BF16)], axis=1)
    for image in range(images):
        part = slice(image * CAP, (image + 1) * CAP)
        span = pl.ds(image * GRID, GRID)
        slot_row = rows_ref[image, pl.ds(EXPERTS + expert, 1), :]
        match = slot_at == slot_row
        dprobs_ref[image, pl.ds(expert, 1), :] = jnp.sum(
            jnp.where(match, dgate[part], 0.0), axis=0, keepdims=True
        )
        hit = jnp.where(match, 1.0, 0.0).astype(BF16)
        landed = tn(hit, returned[part])

        @pl.when(expert == 0)
        def _():
            sums_ref[span, :] = landed

        @pl.when(expert > 0)
        def _():
            sums_ref[span, :] = sums_ref[span, :] + landed


def expert_call(normed_b, cotangent, aux, rows, expert_in, expert_out):
    images = rows.shape[0]
    count = images * GRID
    whole = lambda shape: pl.BlockSpec(shape, lambda e: (0,) * len(shape))
    return pl.pallas_call(
        functools.partial(expert_kernel, images),
        grid=(EXPERTS,),
        in_specs=[
            whole((count, D)),
            whole((count, D)),
            whole((count, 128)),
            whole(rows.shape),
            pl.BlockSpec((1, D, FF), lambda e: (e, 0, 0)),
            pl.BlockSpec((1, FF, D), lambda e: (e, 0, 0)),
        ],
        out_specs=[
            whole((count, 2 * D)),
            whole((images, EXPERTS, GRID)),
            pl.BlockSpec((1, D, FF), lambda e: (e, 0, 0)),
            pl.BlockSpec((1, FF, D), lambda e: (e, 0, 0)),
        ],
        out_shape=[
            jax.ShapeDtypeStruct((count, 2 * D), F32),
            jax.ShapeDtypeStruct((images, EXPERTS, GRID), F32),
            jax.ShapeDtypeStruct((EXPERTS, D, FF), BF16),
            jax.ShapeDtypeStruct((EXPERTS, FF, D), BF16),
        ],
        scratch_shapes=[
            pltpu.VMEM((count, 2 * D), BF16),
            pltpu.VMEM((images * CAP, D), BF16),
            pltpu.VMEM((images * CAP, D + 128), F32),
            pltpu.VMEM((images * CAP, D), BF16),
        ],
        compiler_params=pltpu.CompilerParams(vmem_limit_bytes=VMEM_LIMIT),
        name="experts",
    )(normed_b, cotangent, aux, rows, expert_in, expert_out)


def norm_back(upstream, unit_rows, inverse, gain):
    scaled = upstream * gain
    centered = scaled - jnp.mean(scaled, axis=-1, keepdims=True)
    centered = centered - unit_rows * jnp.mean(scaled * unit_rows, axis=-1, keepdims=True)
    return inverse * centered


def backward_kernel(
    task_ref,
    tokens_ref,
    cot_ref,
    valid_ref,
    dense_ref,
    mixed_ref,
    attended_ref,
    resid_ref,
    normed_ref,
    aux_ref,
    lse_ref,
    sums_ref,
    dprobs_ref,
    output_ref,
    grad_tokens_ref,
    grad_dense_ref,
    grad_rows_ref,
    dmixed,
    dattended,
    acc_k,
    acc_v,
    dq_t,
):
    image = pl.program_id(0)
    task = task_ref[image]
    misc = misc_rows(dense_ref)
    lane = lanes((GRID, 128))
    upstream = cot_ref[...].astype(F32)
    resid = resid_ref[...]
    output_ref[...] = (resid + sums_ref[:, :D]).astype(BF16)
    unit_b, inverse_b = norm_rows(resid)
    probs = jnp.where(lane < EXPERTS, aux_ref[...], 0.0)
    dprobs = jnp.concatenate(
        [dprobs_ref[0], jnp.zeros((128 - EXPERTS, GRID), F32)], axis=0
    ).T
    dlogits = probs * (dprobs - jnp.sum(dprobs * probs, axis=-1, keepdims=True))
    dlogits = dlogits.astype(BF16)
    router = router_of(dense_ref, task)
    grad_router = tn(normed_ref[...], dlogits)
    dnormed_b = sums_ref[:, D:] + nt(dlogits, router)
    dresid = upstream + norm_back(dnormed_b, unit_b, inverse_b, misc[2:3])
    dbranch = dresid.astype(BF16)
    grad_proj_out = tn(attended_ref[...], dbranch)
    dattended[...] = nt(dbranch, dense_ref[:, 3 * D : MISC]).astype(BF16)
    live_col = column_of(valid_ref[pl.ds(image, 1), :].astype(F32))
    lse_col = jnp.concatenate([lse_ref[0], jnp.zeros((120, GRID), F32)], axis=0).T
    key_ext = jnp.where((lane == 0) & (live_col < 0.5), NEGATIVE, 0.0)
    key_ext = jnp.where((lane >= 1) & (lane <= 3), 1.0, key_ext).astype(BF16)
    value_ext = jnp.where(lane < 3, 1.0, 0.0).astype(BF16)
    small = lanes((QB, 128))
    half = small // HEAD_DIM

    def pair_step(pair, carry):
        at = pl.multiple_of(pair * 128, 128)
        keys = mixed_ref[:, pl.ds(D + at, 128)]
        values = mixed_ref[:, pl.ds(2 * D + at, 128)]
        key_full = jnp.concatenate([keys, key_ext], axis=1)
        value_full = jnp.concatenate([values, value_ext], axis=1)
        key_t = keys.astype(F32).T.astype(BF16)
        for block in range(GRID // QB):
            span = pl.ds(block * QB, QB)
            query = mixed_ref[span, pl.ds(at, 128)].astype(F32) * SCALE
            grad = dattended[span, pl.ds(at, 128)].astype(F32)
            seen = attended_ref[span, pl.ds(at, 128)].astype(F32) * grad
            for part in range(2):
                own = half == part
                inner = jnp.sum(jnp.where(own, seen, 0.0), axis=-1, keepdims=True)
                high, mid, low = split3(-inner)
                grad_ext = jnp.where(
                    small == 0, high, jnp.where(small == 1, mid, jnp.where(small == 2, low, 0.0))
                ).astype(BF16)
                head = pair * 2 + part
                shift = jnp.sum(
                    jnp.where(small == head, lse_col[block * QB : (block + 1) * QB], 0.0),
                    axis=-1,
                    keepdims=True,
                )
                high, mid, low = split3(-shift)
                query_ext = jnp.where(
                    small == 0,
                    1.0,
                    jnp.where(
                        small == 1, high, jnp.where(small == 2, mid, jnp.where(small == 3, low, 0.0))
                    ),
                ).astype(BF16)
                my_query = jnp.where(own, query, 0.0).astype(BF16)
                my_grad = jnp.where(own, grad, 0.0).astype(BF16)
                weights = jnp.exp(nt(key_full, jnp.concatenate([my_query, query_ext], axis=1)))
                drift = nt(value_full, jnp.concatenate([my_grad, grad_ext], axis=1))
                dscores = (weights * drift).astype(BF16)
                dkey = nn(dscores, my_query)
                dvalue = nn(weights.astype(BF16), my_grad)
                if block == 0 and part == 0:
                    acc_k[...] = dkey
                    acc_v[...] = dvalue
                else:
                    acc_k[...] += dkey
                    acc_v[...] += dvalue
                rows = slice(part * HEAD_DIM, (part + 1) * HEAD_DIM)
                dq_t[rows, span] = nn(key_t[rows], dscores)
        dmixed[:, pl.ds(at, 128)] = (dq_t[...].T * SCALE).astype(BF16)
        dmixed[:, pl.ds(D + at, 128)] = acc_k[...].astype(BF16)
        dmixed[:, pl.ds(2 * D + at, 128)] = acc_v[...].astype(BF16)
        return carry

    lax.fori_loop(0, PAIRS, pair_step, 0)
    unit_a, inverse_a = norm_rows(tokens_ref[...].astype(F32))
    normed_a = (unit_a * misc[0:1] + misc[1:2]).astype(BF16)
    grad_proj_in = tn(normed_a, dmixed[...])
    dnormed_a = nt(dmixed[...], dense_ref[:, : 3 * D])
    grad_tokens_ref[...] = (dresid + norm_back(dnormed_a, unit_a, inverse_a, misc[0:1])).astype(BF16)
    sums = [
        jnp.sum(dnormed_a * unit_a, axis=0, keepdims=True),
        jnp.sum(dnormed_a, axis=0, keepdims=True),
        jnp.sum(dnormed_b * unit_b, axis=0, keepdims=True),
        jnp.sum(dnormed_b, axis=0, keepdims=True),
        jnp.zeros((4, D), F32),
    ]
    sums = jnp.concatenate(sums, axis=0)
    placed = jnp.where(task == 0, pltpu.roll(grad_router, 4, 1), pltpu.roll(grad_router, 12, 1))

    @pl.when(image == 0)
    def _():
        grad_dense_ref[:, : 3 * D] = grad_proj_in
        grad_dense_ref[:, 3 * D : MISC] = grad_proj_out
        grad_dense_ref[:, MISC:] = placed
        grad_rows_ref[...] = sums

    @pl.when(image > 0)
    def _():
        grad_dense_ref[:, : 3 * D] += grad_proj_in
        grad_dense_ref[:, 3 * D : MISC] += grad_proj_out
        grad_dense_ref[:, MISC:] += placed
        grad_rows_ref[...] += sums

    @pl.when(image == pl.num_programs(0) - 1)
    def _():
        columns = jnp.concatenate([grad_rows_ref[...], jnp.zeros((120, D), F32)], axis=0).T
        keep = lanes((D, 128)) < 4
        grad_dense_ref[:, MISC:] = jnp.where(keep, columns, grad_dense_ref[:, MISC:])


def backward_call(
    task_ids, tokens, cotangent, valid, dense, mixed, attended, resid, normed_b, aux, lse, sums, dprobs
):
    images = valid.shape[0]
    rows = images * GRID
    by_image = lambda width: pl.BlockSpec((GRID, width), lambda i, *_: (i, 0))
    whole = lambda shape: pl.BlockSpec(shape, lambda i, *_: (0,) * len(shape))
    lead = lambda shape: pl.BlockSpec((1,) + shape, lambda i, *_: (i, 0, 0))
    return pl.pallas_call(
        backward_kernel,
        grid_spec=pltpu.PrefetchScalarGridSpec(
            num_scalar_prefetch=1,
            grid=(images,),
            in_specs=[
                by_image(D),
                by_image(D),
                whole(valid.shape),
                whole(dense.shape),
                by_image(3 * D),
                by_image(D),
                by_image(D),
                by_image(D),
                by_image(128),
                lead((8, GRID)),
                by_image(2 * D),
                lead((EXPERTS, GRID)),
            ],
            out_specs=[by_image(D), by_image(D), whole((D, DENSE)), whole((8, D))],
            scratch_shapes=[
                pltpu.VMEM((GRID, 3 * D), BF16),
                pltpu.VMEM((GRID, D), BF16),
                pltpu.VMEM((GRID, 128), F32),
                pltpu.VMEM((GRID, 128), F32),
                pltpu.VMEM((128, GRID), F32),
            ],
        ),
        out_shape=[
            jax.ShapeDtypeStruct((rows, D), BF16),
            jax.ShapeDtypeStruct((rows, D), BF16),
            jax.ShapeDtypeStruct((D, DENSE), F32),
            jax.ShapeDtypeStruct((8, D), F32),
        ],
        compiler_params=pltpu.CompilerParams(vmem_limit_bytes=VMEM_LIMIT),
        name="attention_backward",
    )(task_ids, tokens, cotangent, valid, dense, mixed, attended, resid, normed_b, aux, lse, sums, dprobs)


MESH = pl.DeviceIdType.MESH
ZS = 4
XS = 2
CORES = 2
HALF_ROWS = 48
WIDE_LANES = 768
DENSE_LANES = 512
DENSE_COLS = 2048
FCH = 768


class Place:
    def __init__(self):
        self.w = lax.axis_index("wide")
        self.y = lax.axis_index("narrow")
        self.c = lax.rem(self.w, CORES)
        self.x = lax.rem(self.w // CORES, XS)
        self.z = self.w // (CORES * XS)

    def wide(self, z, x, c):
        return (z * XS + x) * CORES + c

    def core_peer(self):
        return {"wide": self.wide(self.z, self.x, 1 - self.c)}

    def x_peer(self):
        return {"wide": self.wide(self.z, 1 - self.x, self.c)}

    def y_peer(self):
        return {"narrow": 1 - self.y}

    def z_ahead(self, k):
        return lax.rem(self.z + k, ZS)

    def z_behind(self, k):
        return lax.rem(self.z + ZS - k, ZS)

    def z_peer(self, k):
        return {"wide": self.wide(self.z_ahead(k), self.x, self.c)}


def remote(src, dst, sems, to):
    return pltpu.make_async_remote_copy(
        src_ref=src, dst_ref=dst, send_sem=sems[0], recv_sem=sems[1], device_id=to, device_id_type=MESH
    )


class Gather:
    def __init__(self, place, mine, wall, zs, zr, xs, xr, ys, yr, as_, ar, bs, br):
        self.p = place
        self.mine, self.wall = mine, wall
        self.z_sem, self.x_sem, self.y_sem = (zs, zr), (xs, xr), (ys, yr)
        self.a_sem, self.b_sem = (as_, ar), (bs, br)

    def pair(self, sems, *at):
        return sems[0].at[at], sems[1].at[at]

    def z_copy(self, e, k):
        p = self.p
        return remote(self.mine.at[e], self.wall.at[e, p.x, p.c, p.z], self.pair(self.z_sem, e, k - 1), p.z_peer(k))

    def z_landed(self, e, k):
        p = self.p
        here = self.wall.at[e, p.x, p.c, p.z_behind(k)]
        return remote(here, here, self.pair(self.z_sem, e, k - 1), p.z_peer(k))

    def x_copy(self, e, x):
        p = self.p
        here = self.wall.at[e, x, p.c, :, p.y]
        return remote(here, here, self.pair(self.x_sem, e), p.x_peer())

    def y_copy(self, e, y):
        p = self.p
        here = self.wall.at[e, 1 - p.x, p.c, :, y]
        return remote(here, here, self.pair(self.y_sem, e), p.y_peer())

    def a_copy(self, e, c):
        p = self.p
        here = self.wall.at[e, p.x, c]
        return remote(here, here, self.pair(self.a_sem, e), p.core_peer())

    def b_copy(self, e, c):
        p = self.p
        here = self.wall.at[e, 1 - p.x, c]
        return remote(here, here, self.pair(self.b_sem, e), p.core_peer())

    def t0(self, e):
        for k in range(1, ZS):
            self.z_copy(e, k).start()

    def t1(self, e):
        for k in range(1, ZS):
            self.z_landed(e, k).wait_recv()
        self.x_copy(e, self.p.x).start()
        self.a_copy(e, self.p.c).start()

    def t2(self, e):
        self.x_copy(e, 1 - self.p.x).wait_recv()
        self.y_copy(e, self.p.y).start()

    def t3(self, e):
        self.y_copy(e, 1 - self.p.y).wait_recv()
        self.b_copy(e, self.p.c).start()

    def t4(self, e):
        self.a_copy(e, 1 - self.p.c).wait_recv()
        self.b_copy(e, 1 - self.p.c).wait_recv()

    def drain(self, e):
        for k in range(1, ZS):
            self.z_copy(e, k).wait_send()
        self.x_copy(e, self.p.x).wait_send()
        self.a_copy(e, self.p.c).wait_send()
        self.y_copy(e, self.p.y).wait_send()
        self.b_copy(e, self.p.c).wait_send()


def add16(a, b):
    return (a.astype(F32) + b.astype(F32)).astype(BF16)


class Scatter:
    def __init__(self, place, gs, rc, s1, rxa, ryb, s2a, s2b, rya, rxb, s3, rz, fb, send, land):
        self.p = place
        self.gs, self.rc, self.s1 = gs, rc, s1
        self.rxa, self.ryb, self.s2a, self.s2b = rxa, ryb, s2a, s2b
        self.rya, self.rxb, self.s3, self.rz, self.fb = rya, rxb, s3, rz, fb
        self.send, self.land = send, land

    def sems(self, which, slot):
        return self.send.at[which, slot], self.land.at[which, slot]

    def cut(self, ref, lanes_):
        return ref.at[..., pl.ds(0, lanes_)] if lanes_ != WIDE_LANES else ref

    def c_copy(self, slot, n):
        p = self.p
        return remote(
            self.cut(self.gs.at[slot, 1 - p.c], n), self.cut(self.rc.at[slot], n), self.sems(0, slot), p.core_peer()
        )

    def xa_copy(self, slot, n):
        p = self.p
        return remote(
            self.cut(self.s1.at[1 - p.x, pl.ds(0, 2)], n),
            self.cut(self.rxa.at[slot], n),
            self.sems(1, slot),
            p.x_peer(),
        )

    def yb_copy(self, slot, n):
        p = self.p
        return remote(
            self.cut(self.s1.at[:, pl.ds(2, 2), 1 - p.y], n),
            self.cut(self.ryb.at[slot], n),
            self.sems(2, slot),
            p.y_peer(),
        )

    def ya_copy(self, slot, n):
        p = self.p
        return remote(
            self.cut(self.s2a.at[:, 1 - p.y], n), self.cut(self.rya.at[slot], n), self.sems(3, slot), p.y_peer()
        )

    def xb_copy(self, slot, n):
        p = self.p
        return remote(
            self.cut(self.s2b.at[1 - p.x], n), self.cut(self.rxb.at[slot], n), self.sems(4, slot), p.x_peer()
        )

    def z_copy(self, slot, k, n):
        p = self.p
        return remote(
            self.cut(self.s3.at[p.z_ahead(k)], n),
            self.cut(self.rz.at[slot, k - 1], n),
            self.sems(4 + k, slot),
            p.z_peer(k),
        )

    def f_copy(self, slot, y, n):
        here = self.cut(self.fb.at[slot, y], n)
        return remote(here, here, self.sems(8, slot), self.p.y_peer())

    def r0(self, slot, n=WIDE_LANES):
        self.c_copy(slot, n).start()

    def r1(self, slot, n=WIDE_LANES):
        p = self.p
        self.c_copy(slot, n).wait()
        for x in range(XS):
            for z in range(ZS):
                self.s1[x, z, :, :, :n] = add16(self.gs[slot, p.c, x, z, :, :, :n], self.rc[slot, x, z, :, :, :n])
        self.xa_copy(slot, n).start()
        self.yb_copy(slot, n).start()

    def r2(self, slot, n=WIDE_LANES):
        p = self.p
        self.xa_copy(slot, n).wait()
        self.yb_copy(slot, n).wait()
        for z in range(2):
            self.s2a[z, :, :, :n] = add16(self.s1[p.x, z, :, :, :n], self.rxa[slot, z, :, :, :n])
            for x in range(XS):
                self.s2b[x, z, :, :n] = add16(self.s1[x, 2 + z, p.y, :, :n], self.ryb[slot, x, z, :, :n])
        self.ya_copy(slot, n).start()
        self.xb_copy(slot, n).start()

    def r3(self, slot, n=WIDE_LANES):
        p = self.p
        self.ya_copy(slot, n).wait()
        self.xb_copy(slot, n).wait()
        for z in range(2):
            self.s3[z, :, :n] = add16(self.s2a[z, p.y, :, :n], self.rya[slot, z, :, :n])
            self.s3[2 + z, :, :n] = add16(self.s2b[p.x, z, :, :n], self.rxb[slot, z, :, :n])
        for k in range(1, ZS):
            self.z_copy(slot, k, n).start()

    def r4(self, slot, n=WIDE_LANES):
        p = self.p
        for k in range(1, ZS):
            self.z_copy(slot, k, n).wait()
        total = self.s3[p.z, :, :n].astype(F32)
        for k in range(1, ZS):
            total = total + self.rz[slot, k - 1, :, :n].astype(F32)
        self.fb[slot, p.y, :, :n] = total.astype(BF16)
        self.f_copy(slot, p.y, n).start()

    def r5(self, slot, n=WIDE_LANES):
        p = self.p
        self.f_copy(slot, p.y, n).wait_send()
        self.f_copy(slot, 1 - p.y, n).wait_recv()
        return self.fb[slot, 0, :, :n].astype(F32), self.fb[slot, 1, :, :n].astype(F32)


def routing(task, count, ids_ref, valid_ref, image, slots_ref):
    at = pl.multiple_of(image * GRID, GRID)
    live = valid_ref[pl.ds(image, 1), :] > 0
    kind = lax.broadcasted_iota(jnp.int32, (EXPERTS, GRID), 0)
    marks = []
    for rank in range(TOPMAX):
        hit = (ids_ref[pl.ds(rank, 1), pl.ds(at, GRID)] == kind) & live & (rank < count)
        marks.append(jnp.where(hit, 1.0, 0.0))
    used = jnp.concatenate(marks, axis=0)
    span = 256
    from_at = lax.broadcasted_iota(jnp.int32, (span, span), 0)
    earlier = jnp.where(from_at < lanes((span, span)), 1.0, 0.0).astype(BF16)
    running = jnp.zeros((TOPMAX * EXPERTS, 1), F32)
    pieces = []
    for block in range(GRID // span):
        part = used[:, block * span : (block + 1) * span]
        pieces.append(nn(part.astype(BF16), earlier) + running)
        running = running + jnp.sum(part, axis=1, keepdims=True)
    before = jnp.concatenate(pieces, axis=1)
    found = jnp.zeros((EXPERTS, GRID), F32)
    base = jnp.zeros((EXPERTS, 1), F32)
    for rank in range(TOPMAX):
        rows = slice(rank * EXPERTS, (rank + 1) * EXPERTS)
        slot = before[rows] + base
        found = found + jnp.where((used[rows] > 0.5) & (slot < CAP), slot + 1.0, 0.0)
        base = base + running[rows]
    slots_ref[image, :EXPERTS] = found - 1.0


def whole_kernel(
    images,
    task_ref,
    count_ref,
    tokens_ref,
    cot_ref,
    valid_ref,
    ids_ref,
    dmine,
    mine,
    output_ref,
    grad_tokens_ref,
    grad_in_ref,
    grad_out_ref,
    grad_dense_ref,
    wall,
    dense,
    mixed,
    attended,
    resid,
    both,
    aux,
    rows_s,
    lse,
    sums,
    dprobs_s,
    stage,
    win,
    wout,
    given,
    upstream_s,
    gate_s,
    dres_s,
    dattended,
    acc_k,
    acc_v,
    dq_t,
    gd,
    gsums,
    gs,
    rc,
    s1,
    rxa,
    ryb,
    s2a,
    s2b,
    rya,
    rxb,
    s3,
    rz,
    fb,
    dz,
    dx,
    zs,
    zr,
    hop_s,
    hop_r,
    local,
    outward,
    send,
    land,
):
    att_t = gd.at[:, pl.ds(DENSE_COLS - GRID, GRID)]
    held = gd.at[:, pl.ds(0, FCH)]
    db = stage.at[1]
    p = Place()
    peers = [p.core_peer(), p.x_peer(), p.y_peer()] + [p.z_peer(k) for k in range(1, ZS)]
    barrier = pltpu.get_barrier_semaphore()
    for peer in peers:
        pl.semaphore_signal(barrier, inc=1, device_id=peer, device_id_type=MESH)
    pl.semaphore_wait(barrier, len(peers))
    gather = Gather(
        p,
        mine,
        wall,
        zs,
        zr,
        hop_s.at[0],
        hop_r.at[0],
        hop_s.at[1],
        hop_r.at[1],
        hop_s.at[2],
        hop_r.at[2],
        hop_s.at[3],
        hop_r.at[3],
    )
    scatter = Scatter(p, gs, rc, s1, rxa, ryb, s2a, s2b, rya, rxb, s3, rz, fb, send, land)

    def dz_copy(k):
        return remote(dmine, db.at[p.x, p.c, p.z, :, :, pl.ds(0, DENSE_LANES)], (dz.at[0, k], dz.at[1, k]), p.z_peer(k))

    def dz_landed(k):
        here = db.at[p.x, p.c, p.z_behind(k), :, :, pl.ds(0, DENSE_LANES)]
        return remote(here, here, (dz.at[0, k], dz.at[1, k]), p.z_peer(k))

    def dx_copy(x):
        here = db.at[x, p.c, :, :, :, pl.ds(0, DENSE_LANES)]
        return remote(here, here, (dx.at[0, 0], dx.at[1, 0]), p.x_peer())

    def da_copy(x, c):
        here = db.at[x, c, :, :, :, pl.ds(0, DENSE_LANES)]
        return remote(here, here, (dx.at[0, 1], dx.at[1, 1]), p.core_peer())

    def db_copy(x, c):
        here = db.at[x, c, :, :, :, pl.ds(0, DENSE_LANES)]
        return remote(here, here, (dx.at[0, 2], dx.at[1, 2]), p.core_peer())

    cot_copy = pltpu.make_async_copy(cot_ref, both.at[:, pl.ds(D, D)], local.at[3])
    cot_copy.start()
    for k in range(1, ZS):
        dz_copy(k).start()
    own_copy = pltpu.make_async_copy(mine, wall.at[:, p.x, p.c, p.z], local.at[2])
    own_copy.start()
    gather.t0(0)
    gather.t0(1)
    db[p.x, p.c, p.z, :, :, pl.ds(0, DENSE_LANES)] = dmine[...]

    def route_step(image, carry):
        task = task_ref[image]
        routing(task, count_ref[task], ids_ref, valid_ref, image, rows_s)
        return carry

    lax.fori_loop(0, images, route_step, 0)
    for k in range(1, ZS):
        dz_landed(k).wait_recv()
    dx_copy(p.x).start()
    da_copy(p.x, p.c).start()
    dx_copy(1 - p.x).wait_recv()
    db_copy(1 - p.x, p.c).start()
    da_copy(p.x, 1 - p.c).wait_recv()
    db_copy(1 - p.x, 1 - p.c).wait_recv()
    own_copy.wait()
    cot_copy.wait()
    for k in range(1, ZS):
        dz_copy(k).wait_send()
    dx_copy(p.x).wait_send()
    da_copy(p.x, p.c).wait_send()
    db_copy(1 - p.x, p.c).wait_send()
    for z in range(ZS):
        for x in range(XS):
            rows = pl.ds((z * XS + x) * HALF_ROWS, HALF_ROWS)
            for half in range(2):
                one = db[x, 0, z, half, :, pl.ds(0, DENSE_LANES)].astype(F32)
                two = db[x, 1, z, half, :, pl.ds(0, DENSE_LANES)].astype(F32)
                for part in range(2):
                    cut = slice(part * 24, part * 24 + 24)
                    at = half * 1024 + part * DENSE_LANES
                    width = min(DENSE_LANES, MISC + 128 - at)
                    if width > 0:
                        dense[rows, at : at + width] = jnp.concatenate(
                            [one[cut, :width], two[cut, :width]], axis=0
                        ).astype(BF16)

    misc = dense[:, MISC:].astype(F32).T
    lane = lanes((GRID, 128))

    def forward_ticks(step, point):
        def when(at, action):
            @pl.when(step == at)
            def _():
                action()

        def first(e):
            gather.t1(e)
            gather.t0(e + 2)

        def load(e):
            gather.t4(e)
            pltpu.make_async_copy(wall.at[e], stage.at[e], local.at[e]).start()

        if point == 0:
            when(0, lambda: first(0))
            when(1, lambda: gather.t2(0))
            when(2, lambda: gather.t3(0))
            when(3, lambda: first(2))
            when(4, lambda: gather.t2(2))
        else:
            when(1, lambda: first(1))
            when(2, lambda: gather.t2(1))
            when(3, lambda: (gather.t3(1), load(0)))

    def forward_image(image, carry):
        at_row = pl.multiple_of(image * GRID, GRID)
        mine_rows = pl.ds(at_row, GRID)
        task = task_ref[image]
        inputs = tokens_ref[mine_rows, :].astype(F32)
        unit_a, _ = norm_rows(inputs)
        normed_a = (unit_a * misc[0:1] + misc[1:2]).astype(BF16)
        mixed[mine_rows, :] = nn(normed_a, dense[:, : 3 * D]).astype(BF16)
        live_col = column_of(valid_ref[pl.ds(image, 1), :].astype(F32))
        key_ext = jnp.where((lane == 0) & (live_col < 0.5), NEGATIVE, 0.0).astype(BF16)
        query_ext = jnp.where(lanes((QB, 128)) == 0, 1.0, 0.0).astype(BF16)
        ones_rows = jnp.ones((16, GRID), BF16)
        half = lanes((QB, 128)) // HEAD_DIM

        def pair_step(pair, carry):
            at = pl.multiple_of(pair * 128, 128)
            keys = mixed[mine_rows, pl.ds(D + at, 128)]
            values = mixed[mine_rows, pl.ds(2 * D + at, 128)]
            key_full = jnp.concatenate([keys, key_ext], axis=1)
            value_t = jnp.concatenate([values.astype(F32).T.astype(BF16), ones_rows], axis=0)
            for block in range(GRID // QB):
                span = pl.ds(block * QB, QB)
                query = mixed[pl.ds(pl.multiple_of(at_row + block * QB, QB), QB), pl.ds(at, 128)].astype(F32) * SCALE
                for part in range(2):
                    own = jnp.where(half == part, query, 0.0).astype(BF16)
                    scores = nt(key_full, jnp.concatenate([own, query_ext], axis=1))
                    top = jnp.max(scores, axis=0, keepdims=True)
                    raised = jnp.exp(scores - top).astype(BF16)
                    produced = nn(value_t, raised)
                    total = produced[128:129]
                    mine_part = produced[part * HEAD_DIM : (part + 1) * HEAD_DIM] / total
                    att_t[pl.ds(at + part * HEAD_DIM, HEAD_DIM), span] = mine_part
                    lse[image, pl.ds(pair * 2 + part, 1), span] = top + jnp.log(total)
                if block % 2 == 1:
                    forward_ticks(image * PAIRS + pair, block // 2)
            return carry

        lax.fori_loop(0, PAIRS, pair_step, 0)
        seen = att_t[...].T.astype(BF16)
        attended[mine_rows, :] = seen
        branch = inputs + nn(seen, dense[:, 3 * D : MISC])
        resid[mine_rows, :] = branch
        unit_b, _ = norm_rows(branch)
        normed_b = (unit_b * misc[2:3] + misc[3:4]).astype(BF16)
        both[mine_rows, :D] = normed_b
        logits = nn(normed_b, router_of(dense, task))
        logits = jnp.where(lane < EXPERTS, logits, NEGATIVE)
        raised = jnp.exp(logits - jnp.max(logits, axis=-1, keepdims=True))
        probs = raised / jnp.sum(raised, axis=-1, keepdims=True)
        aux[mine_rows, :] = probs
        probs_t = probs.T[:EXPERTS]
        rows_s[image, EXPERTS:] = jnp.where(rows_s[image, :EXPERTS] >= 0.0, probs_t, 0.0)
        return carry

    lax.fori_loop(0, images, forward_image, 0)

    def finish(e, halves):
        first, second = halves
        grad_in_ref[e, :, :WIDE_LANES] = first[:24]
        grad_in_ref[e, :, WIDE_LANES:] = first[24:]
        grad_out_ref[e, :HALF_ROWS] = second[:, :D]
        grad_out_ref[e, HALF_ROWS:] = second[:, D:]

    def guard(e, action):
        @pl.when((e >= 0) & (e < EXPERTS))
        def _():
            action(e)

    def point_a(i):
        guard(i - 4, lambda e: scatter.r4(lax.rem(e, 2)))
        guard(i - 3, lambda e: scatter.r3(lax.rem(e, 2)))

    def point_b(i):
        guard(i - 2, lambda e: scatter.r2(lax.rem(e, 2)))
        guard(i - 1, lambda e: scatter.r1(lax.rem(e, 2)))
        guard(i - 4, lambda e: finish(e, scatter.r5(lax.rem(e, 2))))

    slot_at = lax.broadcasted_iota(jnp.int32, (CAP, GRID), 0).astype(F32)
    c1 = math.sqrt(2.0 / math.pi)
    c3 = c1 * 0.044715

    def expert_step(expert, carry):
        slot = lax.rem(expert, 2)

        @pl.when(expert + 3 < EXPERTS)
        def _():
            gather.t1(expert + 3)

        @pl.when(expert + 5 < EXPERTS)
        def _():
            gather.t0(expert + 5)

        point_a(expert)
        pltpu.make_async_copy(wall.at[expert], stage.at[slot], local.at[slot]).wait()
        for z in range(ZS):
            for x in range(XS):
                chip = z * XS + x
                one = stage[slot, x, 0, z, 0].astype(F32)
                two = stage[slot, x, 1, z, 0].astype(F32)
                rows = pl.ds(chip * HALF_ROWS, HALF_ROWS)
                win[rows, :WIDE_LANES] = jnp.concatenate([one[:24], two[:24]], axis=0).astype(BF16)
                win[rows, WIDE_LANES:] = jnp.concatenate([one[24:], two[24:]], axis=0).astype(BF16)
                for c in range(CORES):
                    base = (chip * CORES + c) * 96
                    wout[pl.ds(base, HALF_ROWS), :] = stage[slot, x, c, z, 1, :, :D]
                    wout[pl.ds(base + HALF_ROWS, HALF_ROWS), :] = stage[slot, x, c, z, 1, :, D:]
        for image in range(images):
            part = pl.ds(image * CAP, CAP)
            slot_row = rows_s[image, pl.ds(expert, 1), :]
            gate_row = rows_s[image, pl.ds(EXPERTS + expert, 1), :]
            match = slot_at == slot_row
            sent = nn(jnp.where(match, 1.0, 0.0).astype(BF16), both[pl.ds(image * GRID, GRID), :])
            gate = jnp.sum(jnp.where(match, gate_row, 0.0), axis=1, keepdims=True)
            given[part, :] = sent[:, :D].astype(BF16)
            upstream_s[part, :] = sent[:, D:].astype(BF16)
            gate_s[part, :] = jnp.broadcast_to(gate, (CAP, 128))
            dres_s[part, :] = (gate * sent[:, D:]).astype(BF16)
        slots = given[...]
        dres = dres_s[...]
        result = jnp.zeros((images * CAP, D), F32)
        back = jnp.zeros((images * CAP, D), F32)
        for chunk in range(FF // FCH):
            span = pl.ds(chunk * FCH, FCH)
            w_in = win[:, span]
            w_out = wout[span, :]
            pre = nn(slots, w_in)
            square = pre * pre
            curve = jnp.tanh(pre * (c1 + c3 * square))
            lifted = 0.5 * (1.0 + curve)
            hidden = (pre * lifted).astype(BF16)
            slope = lifted + (0.5 * pre) * (1.0 - curve * curve) * (c1 + (3.0 * c3) * square)
            result = result + nn(hidden, w_out)
            dpre = (nt(dres, w_out) * slope).astype(BF16)
            back = back + nt(dpre, w_in)
            term = tn(hidden, dres)
            for one in range(FCH // 96):
                w = chunk * (FCH // 96) + one
                z, x, c = w // (XS * CORES), (w // CORES) % XS, w % CORES
                gs[slot, c, x, z, 1, :, :D] = term[one * 96 : one * 96 + 48].astype(BF16)
                gs[slot, c, x, z, 1, :, D:] = term[one * 96 + 48 : one * 96 + 96].astype(BF16)
            term = tn(slots, dpre)
            if chunk == 0:
                held[...] = term
                guard(expert + 2, gather_third)
                guard(expert + 1, load_next)
                point_b(expert)
            else:
                for w in range(ZS * XS * CORES):
                    z, x, c = w // (XS * CORES), (w // CORES) % XS, w % CORES
                    rows = slice(w * 24, w * 24 + 24)
                    gs[slot, c, x, z, 0] = jnp.concatenate([held[rows, :], term[rows]], axis=0).astype(BF16)
        result = result.astype(BF16).astype(F32)
        dgate = jnp.sum(result * upstream_s[...].astype(F32), axis=1, keepdims=True)
        gated = result * gate_s[:, :1]
        returned = jnp.concatenate([gated.astype(BF16), back.astype(BF16)], axis=1)
        scatter.r0(slot)

        @pl.when(expert + 3 < EXPERTS)
        def _():
            gather.t2(expert + 3)

        for image in range(images):
            part = slice(image * CAP, (image + 1) * CAP)
            span = pl.ds(image * GRID, GRID)
            slot_row = rows_s[image, pl.ds(expert, 1), :]
            match = slot_at == slot_row
            dprobs_s[image, pl.ds(expert, 1), :] = jnp.sum(
                jnp.where(match, dgate[part], 0.0), axis=0, keepdims=True
            )
            hit = jnp.where(match, 1.0, 0.0).astype(BF16)
            landed = tn(hit, returned[part])
            sums[span, :] = jnp.where(expert == 0, landed, sums[span, :] + landed)
        return carry

    def gather_third(e):
        gather.t3(e)

    def load_next(e):
        gather.t4(e)
        slot = lax.rem(e, 2)
        pltpu.make_async_copy(wall.at[e], stage.at[slot], local.at[slot]).start()

    lax.fori_loop(0, EXPERTS, expert_step, 0)

    def out_copy(image):
        rows = pl.ds(pl.multiple_of(image * GRID, GRID), GRID)
        return pltpu.make_async_copy(both.at[rows, pl.ds(D, D)], output_ref.at[rows, :], outward.at[0, image])

    def grad_copy(image):
        rows = pl.ds(pl.multiple_of(image * GRID, GRID), GRID)
        return pltpu.make_async_copy(both.at[rows, pl.ds(0, D)], grad_tokens_ref.at[rows, :], outward.at[1, image])

    small = lanes((QB, 128))
    half = small // HEAD_DIM

    def backward_image(image, carry):
        at_row = pl.multiple_of(image * GRID, GRID)
        mine_rows = pl.ds(at_row, GRID)
        task = task_ref[image]
        upstream = both[mine_rows, D:].astype(F32)
        branch = resid[mine_rows, :]
        unit_b, inverse_b = norm_rows(branch)
        probs = aux[mine_rows, :]
        dprobs = jnp.concatenate([dprobs_s[image], jnp.zeros((128 - EXPERTS, GRID), F32)], axis=0).T
        dlogits = probs * (dprobs - jnp.sum(dprobs * probs, axis=-1, keepdims=True))
        dlogits = dlogits.astype(BF16)
        grad_router = tn(both[mine_rows, :D], dlogits)
        both[mine_rows, D:] = (branch + sums[mine_rows, :D]).astype(BF16)
        out_copy(image).start()
        dnormed_b = sums[mine_rows, D:] + nt(dlogits, router_of(dense, task))
        dresid = upstream + norm_back(dnormed_b, unit_b, inverse_b, misc[2:3])
        resid[mine_rows, :] = dresid
        dbranch = dresid.astype(BF16)
        grad_proj_out = tn(attended[mine_rows, :], dbranch)
        dattended[...] = nt(dbranch, dense[:, 3 * D : MISC]).astype(BF16)
        moe_sums = jnp.concatenate(
            [jnp.sum(dnormed_b * unit_b, axis=0, keepdims=True), jnp.sum(dnormed_b, axis=0, keepdims=True)], axis=0
        )
        live_col = column_of(valid_ref[pl.ds(image, 1), :].astype(F32))
        lse_col = jnp.concatenate([lse[image], jnp.zeros((120, GRID), F32)], axis=0).T
        key_ext = jnp.where((lane == 0) & (live_col < 0.5), NEGATIVE, 0.0)
        key_ext = jnp.where((lane >= 1) & (lane <= 3), 1.0, key_ext).astype(BF16)
        value_ext = jnp.where(lane < 3, 1.0, 0.0).astype(BF16)

        def pair_step(pair, carry):
            step = EXPERTS + image * PAIRS + pair
            point_a(step)
            at = pl.multiple_of(pair * 128, 128)
            keys = mixed[mine_rows, pl.ds(D + at, 128)]
            values = mixed[mine_rows, pl.ds(2 * D + at, 128)]
            key_full = jnp.concatenate([keys, key_ext], axis=1)
            value_full = jnp.concatenate([values, value_ext], axis=1)
            key_t = keys.astype(F32).T.astype(BF16)
            for block in range(GRID // QB):
                span = pl.ds(block * QB, QB)
                rows_here = pl.ds(pl.multiple_of(at_row + block * QB, QB), QB)
                query = mixed[rows_here, pl.ds(at, 128)].astype(F32) * SCALE
                grad = dattended[span, pl.ds(at, 128)].astype(F32)
                seen = attended[rows_here, pl.ds(at, 128)].astype(F32) * grad
                for part in range(2):
                    own = half == part
                    inner = jnp.sum(jnp.where(own, seen, 0.0), axis=-1, keepdims=True)
                    high, mid, low = split3(-inner)
                    grad_ext = jnp.where(
                        small == 0, high, jnp.where(small == 1, mid, jnp.where(small == 2, low, 0.0))
                    ).astype(BF16)
                    head = pair * 2 + part
                    shift = jnp.sum(
                        jnp.where(small == head, lse_col[block * QB : (block + 1) * QB], 0.0),
                        axis=-1,
                        keepdims=True,
                    )
                    high, mid, low = split3(-shift)
                    query_ext = jnp.where(
                        small == 0,
                        1.0,
                        jnp.where(
                            small == 1, high, jnp.where(small == 2, mid, jnp.where(small == 3, low, 0.0))
                        ),
                    ).astype(BF16)
                    my_query = jnp.where(own, query, 0.0).astype(BF16)
                    my_grad = jnp.where(own, grad, 0.0).astype(BF16)
                    weights = jnp.exp(nt(key_full, jnp.concatenate([my_query, query_ext], axis=1)))
                    drift = nt(value_full, jnp.concatenate([my_grad, grad_ext], axis=1))
                    dscores = (weights * drift).astype(BF16)
                    dkey = nn(dscores, my_query)
                    dvalue = nn(weights.astype(BF16), my_grad)
                    if block == 0 and part == 0:
                        acc_k[...] = dkey
                        acc_v[...] = dvalue
                    else:
                        acc_k[...] += dkey
                        acc_v[...] += dvalue
                    rows = slice(part * HEAD_DIM, (part + 1) * HEAD_DIM)
                    dq_t[rows, span] = nn(key_t[rows], dscores)
                if block == 1:
                    point_b(step)
            mixed[mine_rows, pl.ds(at, 128)] = (dq_t[...].T * SCALE).astype(BF16)
            mixed[mine_rows, pl.ds(D + at, 128)] = acc_k[...].astype(BF16)
            mixed[mine_rows, pl.ds(2 * D + at, 128)] = acc_v[...].astype(BF16)
            return carry

        lax.fori_loop(0, PAIRS, pair_step, 0)
        unit_a, inverse_a = norm_rows(tokens_ref[mine_rows, :].astype(F32))
        normed_a = (unit_a * misc[0:1] + misc[1:2]).astype(BF16)
        dmixed = mixed[mine_rows, :]
        grad_proj_in = tn(normed_a, dmixed)
        dnormed_a = nt(dmixed, dense[:, : 3 * D])
        both[mine_rows, :D] = (
            resid[mine_rows, :] + norm_back(dnormed_a, unit_a, inverse_a, misc[0:1])
        ).astype(BF16)
        grad_copy(image).start()
        totals = jnp.concatenate(
            [
                jnp.sum(dnormed_a * unit_a, axis=0, keepdims=True),
                jnp.sum(dnormed_a, axis=0, keepdims=True),
                moe_sums,
                jnp.zeros((4, D), F32),
            ],
            axis=0,
        )
        placed = jnp.where(task == 0, pltpu.roll(grad_router, 4, 1), pltpu.roll(grad_router, 12, 1))
        fresh = image == 0
        gd[:, : 3 * D] = jnp.where(fresh, grad_proj_in, gd[:, : 3 * D] + grad_proj_in)
        gd[:, 3 * D : MISC] = jnp.where(fresh, grad_proj_out, gd[:, 3 * D : MISC] + grad_proj_out)
        gd[:, MISC : MISC + 128] = jnp.where(fresh, placed, gd[:, MISC : MISC + 128] + placed)
        gsums[...] = jnp.where(fresh, totals, gsums[...] + totals)
        return carry

    gd[...] = jnp.zeros_like(gd)
    gsums[...] = jnp.zeros_like(gsums)
    lax.fori_loop(0, images, backward_image, 0)

    columns = jnp.concatenate([gsums[...], jnp.zeros((120, D), F32)], axis=0).T
    gd[:, MISC : MISC + 128] = jnp.where(lanes((D, 128)) < 4, columns, gd[:, MISC : MISC + 128])
    for w in range(ZS * XS * CORES):
        z, x, c = w // (XS * CORES), (w // CORES) % XS, w % CORES
        rows = slice(w * 24, w * 24 + 24)
        for part in range(2):
            at = part * 1024
            gs[0, c, x, z, part, :, :DENSE_LANES] = jnp.concatenate(
                [gd[rows, at : at + DENSE_LANES], gd[rows, at + DENSE_LANES : at + 2 * DENSE_LANES]], axis=0
            ).astype(BF16)
    scatter.r0(0, DENSE_LANES)
    scatter.r1(0, DENSE_LANES)
    scatter.r2(0, DENSE_LANES)
    scatter.r3(0, DENSE_LANES)
    scatter.r4(0, DENSE_LANES)
    for part, value in enumerate(scatter.r5(0, DENSE_LANES)):
        at = part * 1024
        grad_dense_ref[:, at : at + DENSE_LANES] = value[:24]
        grad_dense_ref[:, at + DENSE_LANES : at + 2 * DENSE_LANES] = value[24:]

    def drain(e, carry):
        gather.drain(e)
        return carry

    lax.fori_loop(0, EXPERTS, drain, 0)

    def written(image, carry):
        out_copy(image).wait()
        grad_copy(image).wait()
        return carry

    lax.fori_loop(0, images, written, 0)


def whole_call(task_ids, top_counts, tokens, cotangent, valid, ids_t, dmine, mine):
    images = valid.shape[0]
    rows = images * GRID
    smem = pl.BlockSpec(memory_space=pltpu.SMEM)
    vmem = pl.BlockSpec(memory_space=pltpu.VMEM)
    anywhere = pl.BlockSpec(memory_space=pl.ANY)
    piece = (HALF_ROWS, WIDE_LANES)
    sem = pltpu.SemaphoreType.DMA
    return pl.pallas_call(
        functools.partial(whole_kernel, images),
        in_specs=[smem, smem, vmem, anywhere, vmem, vmem, vmem, anywhere],
        out_specs=[anywhere, anywhere, vmem, vmem, vmem, anywhere],
        out_shape=[
            jax.ShapeDtypeStruct((rows, D), BF16),
            jax.ShapeDtypeStruct((rows, D), BF16),
            jax.ShapeDtypeStruct((EXPERTS, 24, FF), F32),
            jax.ShapeDtypeStruct((EXPERTS, 96, D), F32),
            jax.ShapeDtypeStruct((24, DENSE_COLS), F32),
            jax.ShapeDtypeStruct((EXPERTS, XS, CORES, ZS, 2) + piece, BF16),
        ],
        scratch_shapes=[
            pltpu.VMEM((D, DENSE), BF16),
            pltpu.VMEM((rows, 3 * D), BF16),
            pltpu.VMEM((rows, D), BF16),
            pltpu.VMEM((rows, D), F32),
            pltpu.VMEM((rows, 2 * D), BF16),
            pltpu.VMEM((rows, 128), F32),
            pltpu.VMEM((images, 2 * EXPERTS, GRID), F32),
            pltpu.VMEM((images, 8, GRID), F32),
            pltpu.VMEM((rows, 2 * D), F32),
            pltpu.VMEM((images, EXPERTS, GRID), F32),
            pltpu.VMEM((2, XS, CORES, ZS, 2) + piece, BF16),
            pltpu.VMEM((D, FF), BF16),
            pltpu.VMEM((FF, D), BF16),
            pltpu.VMEM((images * CAP, D), BF16),
            pltpu.VMEM((images * CAP, D), BF16),
            pltpu.VMEM((images * CAP, 128), F32),
            pltpu.VMEM((images * CAP, D), BF16),
            pltpu.VMEM((GRID, D), BF16),
            pltpu.VMEM((GRID, 128), F32),
            pltpu.VMEM((GRID, 128), F32),
            pltpu.VMEM((128, GRID), F32),
            pltpu.VMEM((D, DENSE_COLS), F32),
            pltpu.VMEM((8, D), F32),
            pltpu.VMEM((2, CORES, XS, ZS, 2) + piece, BF16),
            pltpu.VMEM((2, XS, ZS, 2) + piece, BF16),
            pltpu.VMEM((XS, ZS, 2) + piece, BF16),
            pltpu.VMEM((2, 2, 2) + piece, BF16),
            pltpu.VMEM((2, XS, 2) + piece, BF16),
            pltpu.VMEM((2, 2) + piece, BF16),
            pltpu.VMEM((XS, 2) + piece, BF16),
            pltpu.VMEM((2, 2) + piece, BF16),
            pltpu.VMEM((2, 2) + piece, BF16),
            pltpu.VMEM((ZS,) + piece, BF16),
            pltpu.VMEM((2, ZS - 1) + piece, BF16),
            pltpu.VMEM((2, 2) + piece, BF16),
            sem((2, ZS)),
            sem((2, 3)),
            sem((EXPERTS, ZS - 1)),
            sem((EXPERTS, ZS - 1)),
            sem((4, EXPERTS)),
            sem((4, EXPERTS)),
            sem((4,)),
            sem((2, images)),
            sem((9, 2)),
            sem((9, 2)),
        ],
        compiler_params=pltpu.CompilerParams(
            vmem_limit_bytes=VMEM_LIMIT, collective_id=0, has_side_effects=True
        ),
        name="whole_step",
    )(task_ids, top_counts, tokens, cotangent, valid, ids_t, dmine, mine)


def whole_body(
    tokens,
    cotangent,
    valid,
    task_ids,
    top_counts,
    expert_ids,
    attn_gain,
    attn_shift,
    proj_in,
    proj_out,
    moe_gain,
    moe_shift,
    router,
    expert_in,
    expert_out,
):
    own = attn_gain.shape[0]
    vectors = jnp.stack([attn_gain, attn_shift, moe_gain, moe_shift], axis=1)
    blank = jnp.zeros((own, DENSE_COLS - MISC - 4 - TASKS * EXPERTS), BF16)
    packed = jnp.concatenate([proj_in, proj_out, vectors, router[0], router[1], blank], axis=1)
    dmine = packed.reshape(own, 2, 2, DENSE_LANES).transpose(1, 2, 0, 3).reshape(2, HALF_ROWS, DENSE_LANES)
    first = expert_in.reshape(EXPERTS, own, 2, WIDE_LANES).transpose(0, 2, 1, 3).reshape(EXPERTS, HALF_ROWS, WIDE_LANES)
    second = jnp.concatenate([expert_out[:, :HALF_ROWS], expert_out[:, HALF_ROWS:]], axis=2)
    mine = jnp.stack([first, second], axis=1)
    output, grad_tokens, grad_in, grad_out, grad_dense, _ = whole_call(
        task_ids, top_counts, tokens, cotangent, valid, expert_ids.T, dmine, mine
    )
    columns = grad_dense[:, MISC : MISC + 4].T
    grad_router = jnp.stack(
        [grad_dense[:, MISC + 4 : MISC + 12], grad_dense[:, MISC + 12 : MISC + 20]], axis=0
    )
    return (
        output,
        grad_tokens,
        columns[0],
        columns[1],
        grad_dense[:, : 3 * D],
        grad_dense[:, 3 * D : MISC],
        columns[2],
        columns[3],
        grad_router,
        grad_in,
        grad_out,
    )


def body(
    tokens,
    cotangent,
    valid,
    task_ids,
    top_counts,
    expert_ids,
    attn_gain,
    attn_shift,
    proj_in,
    proj_out,
    moe_gain,
    moe_shift,
    router,
    expert_in,
    expert_out,
):
    own = attn_gain.shape[0]
    misc = jnp.concatenate(
        [
            jnp.stack([attn_gain, attn_shift, moe_gain, moe_shift], axis=1),
            router[0],
            router[1],
            jnp.zeros((own, 128 - 4 - TASKS * EXPERTS), BF16),
        ],
        axis=1,
    )
    packed = jnp.concatenate([proj_in, proj_out, misc], axis=1)
    dense = lax.all_gather(packed, "wide", axis=0, tiled=True)
    full_in = lax.all_gather(expert_in, "wide", axis=1, tiled=True)
    full_out = lax.all_gather(expert_out, "wide", axis=1, tiled=True)
    mixed, attended, resid, normed_b, aux, rows, lse = forward_call(
        task_ids, top_counts, tokens, valid, expert_ids, dense
    )
    sums, dprobs, grad_in, grad_out = expert_call(normed_b, cotangent, aux, rows, full_in, full_out)
    part_in = lax.psum_scatter(grad_in, "wide", scatter_dimension=1, tiled=True)
    part_out = lax.psum_scatter(grad_out, "wide", scatter_dimension=1, tiled=True)
    output, grad_tokens, grad_dense, _ = backward_call(
        task_ids, tokens, cotangent, valid, dense, mixed, attended, resid, normed_b, aux, lse, sums, dprobs
    )
    part_dense = lax.psum_scatter(grad_dense.astype(BF16), "wide", scatter_dimension=0, tiled=True)
    sum_in, sum_out, sum_dense = lax.psum((part_in, part_out, part_dense), "narrow")
    sum_in = sum_in.astype(F32)
    sum_out = sum_out.astype(F32)
    sum_dense = sum_dense.astype(F32)
    vectors = sum_dense[:, MISC : MISC + 4].T
    grad_router = jnp.stack(
        [sum_dense[:, MISC + 4 : MISC + 12], sum_dense[:, MISC + 12 : MISC + 20]], axis=0
    )
    return (
        output,
        grad_tokens,
        vectors[0],
        vectors[1],
        sum_dense[:, : 3 * D],
        sum_dense[:, 3 * D : MISC],
        vectors[2],
        vectors[3],
        grad_router,
        sum_in,
        sum_out,
    )


def solution(mesh):
    rows = P(("narrow", "wide"), None)
    middle = P(None, "wide", None)
    one_kernel = mesh.shape["narrow"] == 2 and mesh.shape["wide"] == ZS * XS * CORES
    return jax.shard_map(
        whole_body if one_kernel else body,
        mesh=mesh,
        in_specs=(
            rows,
            rows,
            rows,
            P(("narrow", "wide")),
            P(),
            rows,
            P("wide"),
            P("wide"),
            P("wide", None),
            P("wide", None),
            P("wide"),
            P("wide"),
            middle,
            middle,
            middle,
        ),
        out_specs=(
            rows,
            rows,
            P("wide"),
            P("wide"),
            P("wide", None),
            P("wide", None),
            P("wide"),
            P("wide"),
            middle,
            middle,
            middle,
        ),
        check_vma=False,
    )
```

```python
import functools
import math

import jax
import jax.numpy as jnp
from jax import lax
from jax.experimental import pallas as pl
from jax.experimental.pallas import tpu as pltpu
from jax.sharding import PartitionSpec as P

D = 384
HEADS = 6
HEAD_DIM = 64
FF = 1536
EXPERTS = 8
TOPMAX = 4
TASKS = 2
GRID = 1024
CAP = 256
PAIRS = HEADS // 2
QB = 256
FC = 512
EPSILON = 1e-06
NEGATIVE = -1e30
SCALE = 1.0 / math.sqrt(HEAD_DIM)
MISC = 3 * D + D
DENSE = MISC + 128

F32 = jnp.float32
BF16 = jnp.bfloat16
VMEM_LIMIT = 62 * 1024 * 1024


def nn(a, b):
    return lax.dot_general(a, b, (((1,), (0,)), ((), ())), preferred_element_type=F32)


def nt(a, b):
    return lax.dot_general(a, b, (((1,), (1,)), ((), ())), preferred_element_type=F32)


def tn(a, b):
    return lax.dot_general(a, b, (((0,), (0,)), ((), ())), preferred_element_type=F32)


def lanes(shape):
    return lax.broadcasted_iota(jnp.int32, shape, 1)


def norm_rows(values):
    center = values - jnp.mean(values, axis=-1, keepdims=True)
    inverse = lax.rsqrt(jnp.mean(center * center, axis=-1, keepdims=True) + EPSILON)
    return center * inverse, inverse


def split3(value):
    high = value.astype(BF16).astype(F32)
    rest = value - high
    mid = rest.astype(BF16).astype(F32)
    return high, mid, rest - mid


def misc_rows(dense_ref):
    return dense_ref[:, MISC:].astype(F32).T


def router_of(dense_ref, task):
    block = dense_ref[:, MISC:].astype(F32)
    first = pltpu.roll(block, 128 - 4, 1)
    second = pltpu.roll(block, 128 - 12, 1)
    chosen = jnp.where(task == 0, first, second)
    return jnp.where(lanes(chosen.shape) < EXPERTS, chosen, 0.0).astype(BF16)


def column_of(row):
    return jnp.broadcast_to(row, (128, row.shape[1])).T


def forward_kernel(
    task_ref,
    count_ref,
    tokens_ref,
    valid_ref,
    ids_ref,
    dense_ref,
    mixed_ref,
    attended_ref,
    resid_ref,
    normed_ref,
    aux_ref,
    rows_ref,
    lse_ref,
    att_t,
):
    image = pl.program_id(0)
    task = task_ref[image]
    count = count_ref[task]
    misc = misc_rows(dense_ref)
    inputs = tokens_ref[...].astype(F32)
    unit_a, _ = norm_rows(inputs)
    normed_a = (unit_a * misc[0:1] + misc[1:2]).astype(BF16)
    mixed_ref[...] = nn(normed_a, dense_ref[:, : 3 * D]).astype(BF16)
    live_col = column_of(valid_ref[pl.ds(image, 1), :].astype(F32))
    lane = lanes((GRID, 128))
    key_ext = jnp.where((lane == 0) & (live_col < 0.5), NEGATIVE, 0.0).astype(BF16)
    query_ext = jnp.where(lanes((QB, 128)) == 0, 1.0, 0.0).astype(BF16)
    ones_rows = jnp.ones((16, GRID), BF16)

    def pair_step(pair, carry):
        at = pl.multiple_of(pair * 128, 128)
        keys = mixed_ref[:, pl.ds(D + at, 128)]
        values = mixed_ref[:, pl.ds(2 * D + at, 128)]
        key_full = jnp.concatenate([keys, key_ext], axis=1)
        value_t = jnp.concatenate([values.astype(F32).T.astype(BF16), ones_rows], axis=0)
        half = lanes((QB, 128)) // HEAD_DIM
        for block in range(GRID // QB):
            span = pl.ds(block * QB, QB)
            query = mixed_ref[span, pl.ds(at, 128)].astype(F32) * SCALE
            for part in range(2):
                own = jnp.where(half == part, query, 0.0).astype(BF16)
                scores = nt(key_full, jnp.concatenate([own, query_ext], axis=1))
                top = jnp.max(scores, axis=0, keepdims=True)
                raised = jnp.exp(scores - top).astype(BF16)
                produced = nn(value_t, raised)
                total = produced[128:129]
                mine = produced[part * HEAD_DIM : (part + 1) * HEAD_DIM] / total
                att_t[pl.ds(at + part * HEAD_DIM, HEAD_DIM), span] = mine
                lse_ref[0, pl.ds(pair * 2 + part, 1), span] = top + jnp.log(total)
        return carry

    lax.fori_loop(0, PAIRS, pair_step, 0)
    lse_ref[0, HEADS:, :] = jnp.zeros((8 - HEADS, GRID), F32)
    attended = att_t[...].T.astype(BF16)
    attended_ref[...] = attended
    resid = inputs + nn(attended, dense_ref[:, 3 * D : MISC])
    resid_ref[...] = resid
    unit_b, _ = norm_rows(resid)
    normed_b = (unit_b * misc[2:3] + misc[3:4]).astype(BF16)
    normed_ref[...] = normed_b
    logits = nn(normed_b, router_of(dense_ref, task))
    logits = jnp.where(lane < EXPERTS, logits, NEGATIVE)
    raised = jnp.exp(logits - jnp.max(logits, axis=-1, keepdims=True))
    probs = raised / jnp.sum(raised, axis=-1, keepdims=True)
    choice = lane // EXPERTS
    wanted = jnp.full((GRID, 128), -1, jnp.int32)
    for rank in range(TOPMAX):
        wanted = jnp.where(choice == rank, ids_ref[:, rank : rank + 1], wanted)
    used = (wanted == lane % EXPERTS) & (choice < count) & (live_col > 0.5)
    used = jnp.where(used, 1.0, 0.0)
    span = 256
    row_at = lax.broadcasted_iota(jnp.int32, (span, span), 0)
    earlier = jnp.where(row_at > lanes((span, span)), 1.0, 0.0).astype(BF16)
    running = jnp.zeros((1, 128), F32)
    pieces = []
    for block in range(GRID // span):
        part = used[block * span : (block + 1) * span]
        pieces.append(nn(earlier, part.astype(BF16)) + running)
        running = running + jnp.sum(part, axis=0, keepdims=True)
    before = jnp.concatenate(pieces, axis=0)
    totals = jnp.broadcast_to(running, (8, 128))
    lane8 = lanes((8, 128))
    base = jnp.zeros((8, 128), F32)
    for rank in range(1, TOPMAX):
        shift = rank * EXPERTS
        base = base + jnp.where(lane8 >= shift, pltpu.roll(totals, shift, 1), 0.0)
    slot = before + base[0:1]
    found = jnp.where((used > 0.5) & (slot < CAP), slot + 1.0, 0.0)
    folded = found
    for rank in range(1, TOPMAX):
        folded = folded + pltpu.roll(found, 128 - rank * EXPERTS, 1)
    slots = jnp.where(lane < EXPERTS, folded - 1.0, -1.0)
    gates = jnp.where(slots >= 0.0, probs, 0.0)
    aux = probs + jnp.where(
        (choice == 1), pltpu.roll(slots, EXPERTS, 1), 0.0
    ) + jnp.where(choice == 2, pltpu.roll(gates, 2 * EXPERTS, 1), 0.0)
    aux_ref[...] = aux
    rows_ref[0] = aux.T[0 : 4 * EXPERTS]


def forward_call(task_ids, top_counts, tokens, valid, expert_ids, dense):
    images = valid.shape[0]
    rows = images * GRID
    by_image = lambda width: pl.BlockSpec((GRID, width), lambda i, *_: (i, 0))
    whole = lambda shape: pl.BlockSpec(shape, lambda i, *_: (0,) * len(shape))
    lead = lambda shape: pl.BlockSpec((1,) + shape, lambda i, *_: (i, 0, 0))
    return pl.pallas_call(
        forward_kernel,
        grid_spec=pltpu.PrefetchScalarGridSpec(
            num_scalar_prefetch=2,
            grid=(images,),
            in_specs=[by_image(D), whole(valid.shape), by_image(TOPMAX), whole(dense.shape)],
            out_specs=[
                by_image(3 * D),
                by_image(D),
                by_image(D),
                by_image(D),
                by_image(128),
                lead((4 * EXPERTS, GRID)),
                lead((8, GRID)),
            ],
            scratch_shapes=[pltpu.VMEM((D, GRID), F32)],
        ),
        out_shape=[
            jax.ShapeDtypeStruct((rows, 3 * D), BF16),
            jax.ShapeDtypeStruct((rows, D), BF16),
            jax.ShapeDtypeStruct((rows, D), F32),
            jax.ShapeDtypeStruct((rows, D), BF16),
            jax.ShapeDtypeStruct((rows, 128), F32),
            jax.ShapeDtypeStruct((images, 4 * EXPERTS, GRID), F32),
            jax.ShapeDtypeStruct((images, 8, GRID), F32),
        ],
        compiler_params=pltpu.CompilerParams(vmem_limit_bytes=VMEM_LIMIT),
        name="attention_forward",
    )(task_ids, top_counts, tokens, valid, expert_ids, dense)


def expert_kernel(
    images,
    normed_ref,
    cot_ref,
    aux_ref,
    rows_ref,
    in_ref,
    out_ref,
    sums_ref,
    dprobs_ref,
    grad_in_ref,
    grad_out_ref,
    both,
    given,
    upstream,
    dres_s,
):
    expert = pl.program_id(0)

    @pl.when(expert == 0)
    def _():
        for image in range(images):
            span = pl.ds(image * GRID, GRID)
            both[span, :D] = normed_ref[span, :]
            both[span, D:] = cot_ref[span, :]

    slot_at = lax.broadcasted_iota(jnp.int32, (CAP, GRID), 0).astype(F32)
    for image in range(images):
        part = pl.ds(image * CAP, CAP)
        slot_row = rows_ref[image, pl.ds(EXPERTS + expert, 1), :]
        gate_row = rows_ref[image, pl.ds(2 * EXPERTS + expert, 1), :]
        match = slot_at == slot_row
        sent = nn(jnp.where(match, 1.0, 0.0).astype(BF16), both[pl.ds(image * GRID, GRID), :])
        gate = jnp.sum(jnp.where(match, gate_row, 0.0), axis=1, keepdims=True)
        given[part, :] = sent[:, :D].astype(BF16)
        upstream[part, :D] = sent[:, D:]
        upstream[part, D:] = jnp.broadcast_to(gate, (CAP, 128))
        dres_s[part, :] = (gate * sent[:, D:]).astype(BF16)
    slots = given[...]
    dres = dres_s[...]
    result = jnp.zeros((images * CAP, D), F32)
    back = jnp.zeros((images * CAP, D), F32)
    c1 = math.sqrt(2.0 / math.pi)
    c3 = c1 * 0.044715
    for chunk in range(FF // FC):
        span = pl.ds(chunk * FC, FC)
        w_in = in_ref[0, :, span]
        w_out = out_ref[0, span, :]
        pre = nn(slots, w_in)
        square = pre * pre
        curve = jnp.tanh(pre * (c1 + c3 * square))
        lifted = 0.5 * (1.0 + curve)
        hidden = (pre * lifted).astype(BF16)
        slope = lifted + (0.5 * pre) * (1.0 - curve * curve) * (c1 + (3.0 * c3) * square)
        result = result + nn(hidden, w_out)
        dpre = (nt(dres, w_out) * slope).astype(BF16)
        back = back + nt(dpre, w_in)
        grad_out_ref[0, span, :] = tn(hidden, dres).astype(grad_out_ref.dtype)
        grad_in_ref[0, :, span] = tn(slots, dpre).astype(grad_in_ref.dtype)
    result = result.astype(BF16).astype(F32)
    dgate = jnp.sum(result * upstream[:, :D], axis=1, keepdims=True)
    gated = result * upstream[:, D : D + 1]
    returned = jnp.concatenate([gated.astype(BF16), back.astype(BF16)], axis=1)
    for image in range(images):
        part = slice(image * CAP, (image + 1) * CAP)
        span = pl.ds(image * GRID, GRID)
        slot_row = rows_ref[image, pl.ds(EXPERTS + expert, 1), :]
        match = slot_at == slot_row
        dprobs_ref[image, pl.ds(expert, 1), :] = jnp.sum(
            jnp.where(match, dgate[part], 0.0), axis=0, keepdims=True
        )
        hit = jnp.where(match, 1.0, 0.0).astype(BF16)
        landed = tn(hit, returned[part])

        @pl.when(expert == 0)
        def _():
            sums_ref[span, :] = landed

        @pl.when(expert > 0)
        def _():
            sums_ref[span, :] = sums_ref[span, :] + landed


def expert_call(normed_b, cotangent, aux, rows, expert_in, expert_out):
    images = rows.shape[0]
    count = images * GRID
    whole = lambda shape: pl.BlockSpec(shape, lambda e: (0,) * len(shape))
    return pl.pallas_call(
        functools.partial(expert_kernel, images),
        grid=(EXPERTS,),
        in_specs=[
            whole((count, D)),
            whole((count, D)),
            whole((count, 128)),
            whole(rows.shape),
            pl.BlockSpec((1, D, FF), lambda e: (e, 0, 0)),
            pl.BlockSpec((1, FF, D), lambda e: (e, 0, 0)),
        ],
        out_specs=[
            whole((count, 2 * D)),
            whole((images, EXPERTS, GRID)),
            pl.BlockSpec((1, D, FF), lambda e: (e, 0, 0)),
            pl.BlockSpec((1, FF, D), lambda e: (e, 0, 0)),
        ],
        out_shape=[
            jax.ShapeDtypeStruct((count, 2 * D), F32),
            jax.ShapeDtypeStruct((images, EXPERTS, GRID), F32),
            jax.ShapeDtypeStruct((EXPERTS, D, FF), BF16),
            jax.ShapeDtypeStruct((EXPERTS, FF, D), BF16),
        ],
        scratch_shapes=[
            pltpu.VMEM((count, 2 * D), BF16),
            pltpu.VMEM((images * CAP, D), BF16),
            pltpu.VMEM((images * CAP, D + 128), F32),
            pltpu.VMEM((images * CAP, D), BF16),
        ],
        compiler_params=pltpu.CompilerParams(vmem_limit_bytes=VMEM_LIMIT),
        name="experts",
    )(normed_b, cotangent, aux, rows, expert_in, expert_out)


def norm_back(upstream, unit_rows, inverse, gain):
    scaled = upstream * gain
    centered = scaled - jnp.mean(scaled, axis=-1, keepdims=True)
    centered = centered - unit_rows * jnp.mean(scaled * unit_rows, axis=-1, keepdims=True)
    return inverse * centered


def backward_kernel(
    task_ref,
    tokens_ref,
    cot_ref,
    valid_ref,
    dense_ref,
    mixed_ref,
    attended_ref,
    resid_ref,
    normed_ref,
    aux_ref,
    lse_ref,
    sums_ref,
    dprobs_ref,
    output_ref,
    grad_tokens_ref,
    grad_dense_ref,
    grad_rows_ref,
    dmixed,
    dattended,
    acc_k,
    acc_v,
    dq_t,
):
    image = pl.program_id(0)
    task = task_ref[image]
    misc = misc_rows(dense_ref)
    lane = lanes((GRID, 128))
    upstream = cot_ref[...].astype(F32)
    resid = resid_ref[...]
    output_ref[...] = (resid + sums_ref[:, :D]).astype(BF16)
    unit_b, inverse_b = norm_rows(resid)
    probs = jnp.where(lane < EXPERTS, aux_ref[...], 0.0)
    dprobs = jnp.concatenate(
        [dprobs_ref[0], jnp.zeros((128 - EXPERTS, GRID), F32)], axis=0
    ).T
    dlogits = probs * (dprobs - jnp.sum(dprobs * probs, axis=-1, keepdims=True))
    dlogits = dlogits.astype(BF16)
    router = router_of(dense_ref, task)
    grad_router = tn(normed_ref[...], dlogits)
    dnormed_b = sums_ref[:, D:] + nt(dlogits, router)
    dresid = upstream + norm_back(dnormed_b, unit_b, inverse_b, misc[2:3])
    dbranch = dresid.astype(BF16)
    grad_proj_out = tn(attended_ref[...], dbranch)
    dattended[...] = nt(dbranch, dense_ref[:, 3 * D : MISC]).astype(BF16)
    live_col = column_of(valid_ref[pl.ds(image, 1), :].astype(F32))
    lse_col = jnp.concatenate([lse_ref[0], jnp.zeros((120, GRID), F32)], axis=0).T
    key_ext = jnp.where((lane == 0) & (live_col < 0.5), NEGATIVE, 0.0)
    key_ext = jnp.where((lane >= 1) & (lane <= 3), 1.0, key_ext).astype(BF16)
    value_ext = jnp.where(lane < 3, 1.0, 0.0).astype(BF16)
    small = lanes((QB, 128))
    half = small // HEAD_DIM

    def pair_step(pair, carry):
        at = pl.multiple_of(pair * 128, 128)
        keys = mixed_ref[:, pl.ds(D + at, 128)]
        values = mixed_ref[:, pl.ds(2 * D + at, 128)]
        key_full = jnp.concatenate([keys, key_ext], axis=1)
        value_full = jnp.concatenate([values, value_ext], axis=1)
        key_t = keys.astype(F32).T.astype(BF16)
        for block in range(GRID // QB):
            span = pl.ds(block * QB, QB)
            query = mixed_ref[span, pl.ds(at, 128)].astype(F32) * SCALE
            grad = dattended[span, pl.ds(at, 128)].astype(F32)
            seen = attended_ref[span, pl.ds(at, 128)].astype(F32) * grad
            for part in range(2):
                own = half == part
                inner = jnp.sum(jnp.where(own, seen, 0.0), axis=-1, keepdims=True)
                high, mid, low = split3(-inner)
                grad_ext = jnp.where(
                    small == 0, high, jnp.where(small == 1, mid, jnp.where(small == 2, low, 0.0))
                ).astype(BF16)
                head = pair * 2 + part
                shift = jnp.sum(
                    jnp.where(small == head, lse_col[block * QB : (block + 1) * QB], 0.0),
                    axis=-1,
                    keepdims=True,
                )
                high, mid, low = split3(-shift)
                query_ext = jnp.where(
                    small == 0,
                    1.0,
                    jnp.where(
                        small == 1, high, jnp.where(small == 2, mid, jnp.where(small == 3, low, 0.0))
                    ),
                ).astype(BF16)
                my_query = jnp.where(own, query, 0.0).astype(BF16)
                my_grad = jnp.where(own, grad, 0.0).astype(BF16)
                weights = jnp.exp(nt(key_full, jnp.concatenate([my_query, query_ext], axis=1)))
                drift = nt(value_full, jnp.concatenate([my_grad, grad_ext], axis=1))
                dscores = (weights * drift).astype(BF16)
                dkey = nn(dscores, my_query)
                dvalue = nn(weights.astype(BF16), my_grad)
                if block == 0 and part == 0:
                    acc_k[...] = dkey
                    acc_v[...] = dvalue
                else:
                    acc_k[...] += dkey
                    acc_v[...] += dvalue
                rows = slice(part * HEAD_DIM, (part + 1) * HEAD_DIM)
                dq_t[rows, span] = nn(key_t[rows], dscores)
        dmixed[:, pl.ds(at, 128)] = (dq_t[...].T * SCALE).astype(BF16)
        dmixed[:, pl.ds(D + at, 128)] = acc_k[...].astype(BF16)
        dmixed[:, pl.ds(2 * D + at, 128)] = acc_v[...].astype(BF16)
        return carry

    lax.fori_loop(0, PAIRS, pair_step, 0)
    unit_a, inverse_a = norm_rows(tokens_ref[...].astype(F32))
    normed_a = (unit_a * misc[0:1] + misc[1:2]).astype(BF16)
    grad_proj_in = tn(normed_a, dmixed[...])
    dnormed_a = nt(dmixed[...], dense_ref[:, : 3 * D])
    grad_tokens_ref[...] = (dresid + norm_back(dnormed_a, unit_a, inverse_a, misc[0:1])).astype(BF16)
    sums = [
        jnp.sum(dnormed_a * unit_a, axis=0, keepdims=True),
        jnp.sum(dnormed_a, axis=0, keepdims=True),
        jnp.sum(dnormed_b * unit_b, axis=0, keepdims=True),
        jnp.sum(dnormed_b, axis=0, keepdims=True),
        jnp.zeros((4, D), F32),
    ]
    sums = jnp.concatenate(sums, axis=0)
    placed = jnp.where(task == 0, pltpu.roll(grad_router, 4, 1), pltpu.roll(grad_router, 12, 1))

    @pl.when(image == 0)
    def _():
        grad_dense_ref[:, : 3 * D] = grad_proj_in
        grad_dense_ref[:, 3 * D : MISC] = grad_proj_out
        grad_dense_ref[:, MISC:] = placed
        grad_rows_ref[...] = sums

    @pl.when(image > 0)
    def _():
        grad_dense_ref[:, : 3 * D] += grad_proj_in
        grad_dense_ref[:, 3 * D : MISC] += grad_proj_out
        grad_dense_ref[:, MISC:] += placed
        grad_rows_ref[...] += sums

    @pl.when(image == pl.num_programs(0) - 1)
    def _():
        columns = jnp.concatenate([grad_rows_ref[...], jnp.zeros((120, D), F32)], axis=0).T
        keep = lanes((D, 128)) < 4
        grad_dense_ref[:, MISC:] = jnp.where(keep, columns, grad_dense_ref[:, MISC:])


def backward_call(
    task_ids, tokens, cotangent, valid, dense, mixed, attended, resid, normed_b, aux, lse, sums, dprobs
):
    images = valid.shape[0]
    rows = images * GRID
    by_image = lambda width: pl.BlockSpec((GRID, width), lambda i, *_: (i, 0))
    whole = lambda shape: pl.BlockSpec(shape, lambda i, *_: (0,) * len(shape))
    lead = lambda shape: pl.BlockSpec((1,) + shape, lambda i, *_: (i, 0, 0))
    return pl.pallas_call(
        backward_kernel,
        grid_spec=pltpu.PrefetchScalarGridSpec(
            num_scalar_prefetch=1,
            grid=(images,),
            in_specs=[
                by_image(D),
                by_image(D),
                whole(valid.shape),
                whole(dense.shape),
                by_image(3 * D),
                by_image(D),
                by_image(D),
                by_image(D),
                by_image(128),
                lead((8, GRID)),
                by_image(2 * D),
                lead((EXPERTS, GRID)),
            ],
            out_specs=[by_image(D), by_image(D), whole((D, DENSE)), whole((8, D))],
            scratch_shapes=[
                pltpu.VMEM((GRID, 3 * D), BF16),
                pltpu.VMEM((GRID, D), BF16),
                pltpu.VMEM((GRID, 128), F32),
                pltpu.VMEM((GRID, 128), F32),
                pltpu.VMEM((128, GRID), F32),
            ],
        ),
        out_shape=[
            jax.ShapeDtypeStruct((rows, D), BF16),
            jax.ShapeDtypeStruct((rows, D), BF16),
            jax.ShapeDtypeStruct((D, DENSE), F32),
            jax.ShapeDtypeStruct((8, D), F32),
        ],
        compiler_params=pltpu.CompilerParams(vmem_limit_bytes=VMEM_LIMIT),
        name="attention_backward",
    )(task_ids, tokens, cotangent, valid, dense, mixed, attended, resid, normed_b, aux, lse, sums, dprobs)


MESH = pl.DeviceIdType.MESH
ZS = 4
XS = 2
CORES = 2
HALF_ROWS = 48
WIDE_LANES = 768
DENSE_LANES = 512
DENSE_COLS = 2048
FCH = 768
QF = 512
RB = 256
LATE = 3 * D + D
HALVES = 3
AHEAD = 3


class Place:
    def __init__(self):
        self.w = lax.axis_index("wide")
        self.y = lax.axis_index("narrow")
        self.c = lax.rem(self.w, CORES)
        self.x = lax.rem(self.w // CORES, XS)
        self.z = self.w // (CORES * XS)

    def wide(self, z, x, c):
        return (z * XS + x) * CORES + c

    def core_peer(self):
        return {"wide": self.wide(self.z, self.x, 1 - self.c)}

    def x_peer(self):
        return {"wide": self.wide(self.z, 1 - self.x, self.c)}

    def y_peer(self):
        return {"narrow": 1 - self.y}

    def z_ahead(self, k):
        return lax.rem(self.z + k, ZS)

    def z_behind(self, k):
        return lax.rem(self.z + ZS - k, ZS)

    def z_peer(self, k):
        return {"wide": self.wide(self.z_ahead(k), self.x, self.c)}


def remote(src, dst, sems, to):
    return pltpu.make_async_remote_copy(
        src_ref=src, dst_ref=dst, send_sem=sems[0], recv_sem=sems[1], device_id=to, device_id_type=MESH
    )


class Gather:
    def __init__(self, place, mine, wall, zs, zr, hop_s, hop_r, cs, cr):
        self.p = place
        self.mine, self.wall = mine, wall
        self.z_sem, self.col_sem = (zs, zr), (cs, cr)
        self.x_sem, self.y_sem, self.a_sem, self.b_sem = [(hop_s.at[i], hop_r.at[i]) for i in range(4)]

    def pair(self, sems, *at):
        return sems[0].at[at], sems[1].at[at]

    def by_kind(self, e, full, half):
        if isinstance(e, int):
            (half if e < HALVES else full)()
            return
        pl.when(e < HALVES)(half)
        pl.when(e >= HALVES)(full)

    def z_copy(self, e, k):
        p = self.p
        return remote(self.mine.at[e], self.wall.at[e, p.x, p.c, p.z], self.pair(self.z_sem, e, k - 1), p.z_peer(k))

    def z_landed(self, e, k):
        p = self.p
        here = self.wall.at[e, p.x, p.c, p.z_behind(k)]
        return remote(here, here, self.pair(self.z_sem, e, k - 1), p.z_peer(k))

    def zh_copy(self, e, k):
        p = self.p
        return remote(
            self.mine.at[e, p.y], self.wall.at[e, p.x, p.c, p.z, p.y], self.pair(self.z_sem, e, k - 1), p.z_peer(k)
        )

    def col_copy(self, e, k, y):
        p = self.p
        here = self.wall.at[e, p.x, p.c, p.z_behind(k), y]
        return remote(here, here, self.pair(self.col_sem, e, k - 1), p.y_peer())

    def zh_landed(self, e, k):
        p = self.p
        here = self.wall.at[e, p.x, p.c, p.z_behind(k), p.y]
        return remote(here, here, self.pair(self.z_sem, e, k - 1), p.z_peer(k))

    def x_copy(self, e, x):
        p = self.p
        here = self.wall.at[e, x, p.c, :, p.y]
        return remote(here, here, self.pair(self.x_sem, e), p.x_peer())

    def y_copy(self, e, y):
        p = self.p
        here = self.wall.at[e, 1 - p.x, p.c, :, y]
        return remote(here, here, self.pair(self.y_sem, e), p.y_peer())

    def a_copy(self, e, c):
        p = self.p
        here = self.wall.at[e, p.x, c]
        return remote(here, here, self.pair(self.a_sem, e), p.core_peer())

    def b_copy(self, e, c):
        p = self.p
        here = self.wall.at[e, 1 - p.x, c]
        return remote(here, here, self.pair(self.b_sem, e), p.core_peer())

    def each(self, action):
        def run():
            for k in range(1, ZS):
                action(k)

        return run

    def t0(self, e):
        self.by_kind(
            e,
            self.each(lambda k: self.z_copy(e, k).start()),
            self.each(lambda k: self.zh_copy(e, k).start()),
        )

    def t1(self, e):
        def full():
            for k in range(1, ZS):
                self.z_landed(e, k).wait_recv()
            self.x_copy(e, self.p.x).start()
            self.a_copy(e, self.p.c).start()

        def half():
            for k in range(1, ZS):
                self.zh_landed(e, k).wait_recv()
            self.x_copy(e, self.p.x).start()
            for k in range(1, ZS):
                self.col_copy(e, k, self.p.y).start()

        self.by_kind(e, full, half)

    def t2(self, e):
        def half():
            for k in range(1, ZS):
                self.col_copy(e, k, 1 - self.p.y).wait_recv()
            self.a_copy(e, self.p.c).start()

        self.x_copy(e, 1 - self.p.x).wait_recv()
        self.y_copy(e, self.p.y).start()
        self.by_kind(e, lambda: None, half)

    def t3(self, e):
        self.y_copy(e, 1 - self.p.y).wait_recv()
        self.b_copy(e, self.p.c).start()

    def t4(self, e):
        self.a_copy(e, 1 - self.p.c).wait_recv()
        self.b_copy(e, 1 - self.p.c).wait_recv()

    def drain(self, e):
        def half():
            for k in range(1, ZS):
                self.zh_copy(e, k).wait_send()
                self.col_copy(e, k, self.p.y).wait_send()

        self.by_kind(e, self.each(lambda k: self.z_copy(e, k).wait_send()), half)
        self.x_copy(e, self.p.x).wait_send()
        self.a_copy(e, self.p.c).wait_send()
        self.y_copy(e, self.p.y).wait_send()
        self.b_copy(e, self.p.c).wait_send()


def add16(a, b):
    return (a.astype(F32) + b.astype(F32)).astype(BF16)


CHUNKS = EXPERTS + 2
AZ = 2
BZ = ZS - AZ


class Scatter:
    def __init__(self, place, gs, rc, s1, ha, hb, la, lb, ma, mb, s2a, s2b, rya, rxb, s3, rz, fb, send, land, keep):
        self.p = place
        self.gs, self.rc, self.s1 = gs, rc, s1
        self.ha, self.hb = ha, hb
        self.la, self.lb, self.ma, self.mb = la, lb, ma, mb
        self.s2a, self.s2b = s2a, s2b
        self.rya, self.rxb, self.s3, self.rz, self.fb = rya, rxb, s3, rz, fb
        self.send, self.land, self.keep = send, land, keep

    def sems(self, which, slot):
        return self.send.at[which, slot], self.land.at[which, slot]

    def cut(self, ref, n):
        return ref.at[..., pl.ds(0, n)] if n != WIDE_LANES else ref

    def slot(self, k):
        return lax.rem(k, 2)

    def c_copy(self, k, n):
        p, slot = self.p, self.slot(k)
        return remote(
            self.cut(self.gs.at[slot, 1 - p.c], n), self.cut(self.rc.at[slot], n), self.sems(0, slot), p.core_peer()
        )

    def store_a(self, k, n):
        return pltpu.make_async_copy(
            self.cut(self.s1.at[:, pl.ds(0, AZ)], n), self.cut(self.ha.at[k], n), self.keep.at[0]
        )

    def store_b(self, k, n):
        return pltpu.make_async_copy(
            self.cut(self.s1.at[:, pl.ds(AZ, BZ)], n), self.cut(self.hb.at[k], n), self.keep.at[1]
        )

    def xa_copy(self, k, n):
        p = self.p
        return remote(
            self.cut(self.ha.at[k, 1 - p.x], n),
            self.cut(self.ma.at[self.slot(k)], n),
            self.sems(7, self.slot(k)),
            p.x_peer(),
        )

    def yb_copy(self, k, n):
        p = self.p
        return remote(
            self.cut(self.hb.at[k, :, :, 1 - p.y], n),
            self.cut(self.mb.at[self.slot(k)], n),
            self.sems(8, self.slot(k)),
            p.y_peer(),
        )

    def loads(self, k, n):
        p = self.p
        return [
            pltpu.make_async_copy(self.cut(self.ha.at[k, p.x], n), self.cut(self.la, n), self.keep.at[2]),
            pltpu.make_async_copy(self.cut(self.hb.at[k, :, :, p.y], n), self.cut(self.lb, n), self.keep.at[3]),
        ]

    def ya_copy(self, k, n):
        p, slot = self.p, self.slot(k)
        return remote(
            self.cut(self.s2a.at[:, 1 - p.y], n), self.cut(self.rya.at[slot], n), self.sems(1, slot), p.y_peer()
        )

    def xb_copy(self, k, n):
        p, slot = self.p, self.slot(k)
        return remote(
            self.cut(self.s2b.at[1 - p.x], n), self.cut(self.rxb.at[slot], n), self.sems(2, slot), p.x_peer()
        )

    def z_copy(self, k, ahead, n):
        p, slot = self.p, self.slot(k)
        return remote(
            self.cut(self.s3.at[p.z_ahead(ahead)], n),
            self.cut(self.rz.at[slot, ahead - 1], n),
            self.sems(2 + ahead, slot),
            p.z_peer(ahead),
        )

    def f_copy(self, k, y, n):
        slot = self.slot(k)
        here = self.cut(self.fb.at[slot, y], n)
        return remote(here, here, self.sems(6, slot), self.p.y_peer())

    def r0(self, k, n=WIDE_LANES):
        self.c_copy(k, n).start()

    def r1a(self, k, n=WIDE_LANES):
        p, slot = self.p, self.slot(k)
        self.c_copy(k, n).wait()
        for x in range(XS):
            for z in range(ZS):
                self.s1[x, z, :, :, :n] = add16(self.gs[slot, p.c, x, z, :, :, :n], self.rc[slot, x, z, :, :, :n])
        self.store_a(k, n).start()
        self.store_b(k, n).start()

    def r1w(self, k, n=WIDE_LANES):
        self.store_a(k, n).wait()
        self.store_b(k, n).wait()

    def r1b(self, k, n=WIDE_LANES):
        self.xa_copy(k, n).start()
        self.yb_copy(k, n).start()

    def r2a(self, k, n=WIDE_LANES):
        for copy in self.loads(k, n):
            copy.start()

    def r2b(self, k, n=WIDE_LANES):
        slot = self.slot(k)
        for copy in self.loads(k, n):
            copy.wait()
        self.xa_copy(k, n).wait()
        self.yb_copy(k, n).wait()
        for z in range(AZ):
            self.s2a[z, :, :, :n] = add16(self.la[z, :, :, :n], self.ma[slot, z, :, :, :n])
        for z in range(BZ):
            for x in range(XS):
                self.s2b[x, z, :, :n] = add16(self.lb[x, z, :, :n], self.mb[slot, x, z, :, :n])
        self.ya_copy(k, n).start()
        self.xb_copy(k, n).start()

    def r3(self, k, n=WIDE_LANES):
        p, slot = self.p, self.slot(k)
        self.ya_copy(k, n).wait()
        self.xb_copy(k, n).wait()
        for z in range(AZ):
            self.s3[z, :, :n] = add16(self.s2a[z, p.y, :, :n], self.rya[slot, z, :, :n])
        for z in range(BZ):
            self.s3[AZ + z, :, :n] = add16(self.s2b[p.x, z, :, :n], self.rxb[slot, z, :, :n])
        for ahead in range(1, ZS):
            self.z_copy(k, ahead, n).start()

    def r4(self, k, n=WIDE_LANES):
        p, slot = self.p, self.slot(k)
        for ahead in range(1, ZS):
            self.z_copy(k, ahead, n).wait()
        total = self.s3[p.z, :, :n].astype(F32)
        for ahead in range(1, ZS):
            total = total + self.rz[slot, ahead - 1, :, :n].astype(F32)
        self.fb[slot, p.y, :, :n] = total.astype(BF16)
        self.f_copy(k, p.y, n).start()

    def r5(self, k, n=WIDE_LANES):
        p, slot = self.p, self.slot(k)
        self.f_copy(k, p.y, n).wait_send()
        self.f_copy(k, 1 - p.y, n).wait_recv()
        return self.fb[slot, 0, :, :n].astype(F32), self.fb[slot, 1, :, :n].astype(F32)


def routing(task, count, ids_ref, valid_ref, image, slots_ref):
    at = pl.multiple_of(image * GRID, GRID)
    live = valid_ref[pl.ds(image, 1), :] > 0
    kind = lax.broadcasted_iota(jnp.int32, (EXPERTS, GRID), 0)
    marks = []
    for rank in range(TOPMAX):
        hit = (ids_ref[pl.ds(rank, 1), pl.ds(at, GRID)] == kind) & live & (rank < count)
        marks.append(jnp.where(hit, 1.0, 0.0))
    used = jnp.concatenate(marks, axis=0)
    span = 256
    from_at = lax.broadcasted_iota(jnp.int32, (span, span), 0)
    earlier = jnp.where(from_at < lanes((span, span)), 1.0, 0.0).astype(BF16)
    running = jnp.zeros((TOPMAX * EXPERTS, 1), F32)
    pieces = []
    for block in range(GRID // span):
        part = used[:, block * span : (block + 1) * span]
        pieces.append(nn(part.astype(BF16), earlier) + running)
        running = running + jnp.sum(part, axis=1, keepdims=True)
    before = jnp.concatenate(pieces, axis=1)
    found = jnp.zeros((EXPERTS, GRID), F32)
    base = jnp.zeros((EXPERTS, 1), F32)
    for rank in range(TOPMAX):
        rows = slice(rank * EXPERTS, (rank + 1) * EXPERTS)
        slot = before[rows] + base
        found = found + jnp.where((used[rows] > 0.5) & (slot < CAP), slot + 1.0, 0.0)
        base = base + running[rows]
    slots_ref[image, :EXPERTS] = found - 1.0


def whole_kernel(
    images,
    task_ref,
    count_ref,
    tokens_ref,
    cot_ref,
    valid_ref,
    ids_ref,
    dmine,
    mine,
    flat,
    output_ref,
    grad_tokens_ref,
    grad_in_ref,
    grad_out_ref,
    grad_proj_in_ref,
    grad_proj_out_ref,
    grad_misc_ref,
    wall,
    ha,
    hb,
    dense,
    mixed,
    attended,
    resid,
    both,
    probs_s,
    rows_s,
    lse,
    returned_s,
    dprobs_s,
    stage,
    win,
    wout,
    given,
    upstream_s,
    gate_s,
    dres_s,
    dattended,
    acc_k,
    acc_v,
    dq_t,
    gd,
    gs,
    rc,
    s1,
    la,
    lb,
    ma,
    mb,
    s2a,
    s2b,
    rya,
    rxb,
    s3,
    rz,
    fb,
    dz,
    dx,
    zs,
    zr,
    hop_s,
    hop_r,
    cs,
    cr,
    local,
    outward,
    send,
    land,
    keep,
):
    att_t = gd.at[:, pl.ds(DENSE_COLS - GRID, GRID)]
    held = gd.at[:, pl.ds(0, FCH)]
    db = stage
    p = Place()
    peers = [p.core_peer(), p.x_peer(), p.y_peer()] + [p.z_peer(k) for k in range(1, ZS)]
    barrier = pltpu.get_barrier_semaphore()
    for peer in peers:
        pl.semaphore_signal(barrier, inc=1, device_id=peer, device_id_type=MESH)
    pl.semaphore_wait(barrier, len(peers))
    gather = Gather(p, mine, wall, zs, zr, hop_s, hop_r, cs, cr)
    scatter = Scatter(
        p, gs, rc, s1, ha, hb, la, lb, ma, mb, s2a, s2b, rya, rxb, s3, rz, fb, send, land, keep
    )

    def dz_copy(k):
        return remote(dmine, db.at[p.x, p.c, p.z, :, :, pl.ds(0, DENSE_LANES)], (dz.at[0, k], dz.at[1, k]), p.z_peer(k))

    def dz_landed(k):
        here = db.at[p.x, p.c, p.z_behind(k), :, :, pl.ds(0, DENSE_LANES)]
        return remote(here, here, (dz.at[0, k], dz.at[1, k]), p.z_peer(k))

    def dx_copy(x):
        here = db.at[x, p.c, :, :, :, pl.ds(0, DENSE_LANES)]
        return remote(here, here, (dx.at[0, 0], dx.at[1, 0]), p.x_peer())

    def da_copy(x, c):
        here = db.at[x, c, :, :, :, pl.ds(0, DENSE_LANES)]
        return remote(here, here, (dx.at[0, 1], dx.at[1, 1]), p.core_peer())

    def db_copy(x, c):
        here = db.at[x, c, :, :, :, pl.ds(0, DENSE_LANES)]
        return remote(here, here, (dx.at[0, 2], dx.at[1, 2]), p.core_peer())

    cot_copy = pltpu.make_async_copy(cot_ref, both.at[:, pl.ds(D, D)], local.at[3])
    cot_copy.start()
    for k in range(1, ZS):
        dz_copy(k).start()
    own_in = pltpu.make_async_copy(flat, returned_s.at[0, pl.ds(0, EXPERTS * 2 * HALF_ROWS)], local.at[1])
    own_in.start()
    for e in range(AHEAD):
        gather.t0(e)
    db[p.x, p.c, p.z, :, :, pl.ds(0, DENSE_LANES)] = dmine[...]

    def route_step(image, carry):
        task = task_ref[image]
        routing(task, count_ref[task], ids_ref, valid_ref, image, rows_s)
        return carry

    own_in.wait()
    for e in range(EXPERTS):
        for part in range(2):
            pltpu.make_async_copy(
                returned_s.at[0, pl.ds((e * 2 + part) * HALF_ROWS, HALF_ROWS)],
                wall.at[e, p.x, p.c, p.z, part],
                local.at[2],
            ).start()
    lax.fori_loop(0, images, route_step, 0)
    for k in range(1, ZS):
        dz_landed(k).wait_recv()
    dx_copy(p.x).start()
    da_copy(p.x, p.c).start()
    dx_copy(1 - p.x).wait_recv()
    db_copy(1 - p.x, p.c).start()
    da_copy(p.x, 1 - p.c).wait_recv()
    db_copy(1 - p.x, 1 - p.c).wait_recv()
    pltpu.make_async_copy(mine, wall.at[:, p.x, p.c, p.z], local.at[2]).wait()
    cot_copy.wait()
    for k in range(1, ZS):
        dz_copy(k).wait_send()
    dx_copy(p.x).wait_send()
    da_copy(p.x, p.c).wait_send()
    db_copy(1 - p.x, p.c).wait_send()
    for z in range(ZS):
        for x in range(XS):
            rows = pl.ds((z * XS + x) * HALF_ROWS, HALF_ROWS)
            for half in range(2):
                one = db[x, 0, z, half, :, pl.ds(0, DENSE_LANES)].astype(F32)
                two = db[x, 1, z, half, :, pl.ds(0, DENSE_LANES)].astype(F32)
                for part in range(2):
                    cut = slice(part * 24, part * 24 + 24)
                    at = half * 1024 + part * DENSE_LANES
                    width = min(DENSE_LANES, MISC + 128 - at)
                    if width > 0:
                        dense[rows, at : at + width] = jnp.concatenate(
                            [one[cut, :width], two[cut, :width]], axis=0
                        ).astype(BF16)

    misc = dense[:, MISC:].astype(F32).T
    lane = lanes((GRID, 128))

    def load(e):
        gather.t4(e)
        pltpu.make_async_copy(wall.at[e], stage, local.at[0]).start()

    def first(e):
        gather.t1(e)
        gather.t0(e + AHEAD)

    plan = {
        (0, 0): lambda: first(0),
        (0, 3): lambda: (gather.t2(0), first(1)),
        (1, 2): lambda: (gather.t3(0), gather.t2(1), first(2)),
        (1, 3): lambda: load(0),
    }

    def forward_ticks(image, point):
        for which in range(2):
            if (which, point) in plan:

                @pl.when(image == which)
                def _():
                    plan[(which, point)]()

    def forward_image(image, carry):
        at_row = pl.multiple_of(image * GRID, GRID)
        mine_rows = pl.ds(at_row, GRID)
        task = task_ref[image]

        def rows_of(block, size):
            return pl.ds(pl.multiple_of(at_row + block * size, size), size)

        for block in range(GRID // RB):
            rows = rows_of(block, RB)
            unit_a, _ = norm_rows(tokens_ref[rows, :].astype(F32))
            normed_a = (unit_a * misc[0:1] + misc[1:2]).astype(BF16)
            mixed[rows, :] = nn(normed_a, dense[:, : 3 * D]).astype(BF16)
        forward_ticks(image, 0)
        live_col = column_of(valid_ref[pl.ds(image, 1), :].astype(F32))
        key_ext = jnp.where((lane == 0) & (live_col < 0.5), NEGATIVE, 0.0).astype(BF16)
        query_ext = jnp.where(lanes((QF, 128)) == 0, 1.0, 0.0).astype(BF16)
        ones_rows = jnp.ones((16, GRID), BF16)
        half = lanes((QF, 128)) // HEAD_DIM
        units = [(pair, block, part) for pair in range(PAIRS) for block in range(GRID // QF) for part in range(2)]
        held_values = {}

        def start(unit):
            pair, block, part = unit
            keys = mixed[mine_rows, D + pair * 128 : D + pair * 128 + 128]
            query = mixed[rows_of(block, QF), pair * 128 : pair * 128 + 128].astype(F32) * SCALE
            own = jnp.where(half == part, query, 0.0).astype(BF16)
            return nt(jnp.concatenate([keys, key_ext], axis=1), jnp.concatenate([own, query_ext], axis=1))

        def finish_unit(unit, top, raised):
            pair, block, part = unit
            if (block, part) == (0, 0):
                values = mixed[mine_rows, 2 * D + pair * 128 : 2 * D + pair * 128 + 128]
                held_values[0] = jnp.concatenate([values.astype(F32).T.astype(BF16), ones_rows], axis=0)
            span = pl.ds(block * QF, QF)
            produced = nn(held_values[0], raised)
            total = produced[128:129]
            at = pair * 128 + part * HEAD_DIM
            att_t[pl.ds(at, HEAD_DIM), span] = produced[part * HEAD_DIM : (part + 1) * HEAD_DIM] / total
            lse[image, pl.ds(pair * 2 + part, 1), span] = top + jnp.log(total)

        scores = start(units[0])
        waiting = None
        for index, unit in enumerate(units):
            later = start(units[index + 1]) if index + 1 < len(units) else None
            top = jnp.max(scores, axis=0, keepdims=True)
            raised = jnp.exp(scores - top).astype(BF16)
            if waiting is not None:
                finish_unit(*waiting)
            waiting = (unit, top, raised)
            scores = later
            if index % 4 == 3:
                forward_ticks(image, index // 4 + 1)
        finish_unit(*waiting)
        router = router_of(dense, task)
        lane_rb = lanes((RB, 128))
        for block in range(GRID // RB):
            rows = rows_of(block, RB)
            seen = att_t[:, block * RB : (block + 1) * RB].T.astype(BF16)
            attended[rows, :] = seen
            branch = tokens_ref[rows, :].astype(F32) + nn(seen, dense[:, 3 * D : MISC])
            resid[rows, :] = branch
            unit_b, _ = norm_rows(branch)
            normed_b = (unit_b * misc[2:3] + misc[3:4]).astype(BF16)
            both[rows, :D] = normed_b
            logits = jnp.where(lane_rb < EXPERTS, nn(normed_b, router), NEGATIVE)
            raised = jnp.exp(logits - jnp.max(logits, axis=-1, keepdims=True))
            probs = raised / jnp.sum(raised, axis=-1, keepdims=True)
            span = slice(block * RB, (block + 1) * RB)
            probs_t = probs.T[:EXPERTS]
            probs_s[image, :, span] = probs_t
            rows_s[image, EXPERTS:, span] = jnp.where(rows_s[image, :EXPERTS, span] >= 0.0, probs_t, 0.0)
        return carry

    lax.fori_loop(0, images, forward_image, 0)

    def finish(e, halves):
        first, second = halves
        grad_in_ref[e] = jnp.concatenate([first[:24], first[24:]], axis=1).astype(BF16)
        grad_out_ref[e, :HALF_ROWS] = second[:, :D].astype(BF16)
        grad_out_ref[e, HALF_ROWS:] = second[:, D:].astype(BF16)

    def guard(e, action):
        @pl.when((e >= 0) & (e < EXPERTS))
        def _():
            action(e)

    def active(i):
        early = (i >= 3) & (i < EXPERTS)
        late = (i > EXPERTS) & (i < 2 * EXPERTS - 2) & (lax.rem(i, 2) == 1)
        return jnp.where(i < EXPERTS, i - 3, (i + 1) // 2), early | late

    def lagging(i, action):
        e, now = active(i)

        @pl.when(now)
        def _():
            action(e)

    def point_a(i):
        guard(i - 2, scatter.r1w)

        @pl.when(i == 2)
        def _():
            scatter.r1b(0)

        lagging(i, scatter.r2a)

    def second(e):
        scatter.r2b(e)

        @pl.when(e + 1 < EXPERTS)
        def _():
            scatter.r1b(e + 1)

    def point_b(i):
        lagging(i - 3, lambda e: finish(e, scatter.r5(e)))
        lagging(i - 2, scatter.r4)
        lagging(i - 1, scatter.r3)
        lagging(i, second)
        guard(i - 1, scatter.r1a)

    slot_at = lax.broadcasted_iota(jnp.int32, (CAP, GRID), 0).astype(F32)
    c1 = math.sqrt(2.0 / math.pi)
    c3 = c1 * 0.044715

    def expert_step(expert, carry):
        slot = lax.rem(expert, 2)

        guard(expert + 1, gather.t3)
        guard(expert + 2, gather.t2)
        guard(expert + 3, gather.t1)
        guard(expert + 3 + AHEAD, gather.t0)
        pltpu.make_async_copy(wall.at[expert], stage, local.at[0]).wait()
        for z in range(ZS):
            for x in range(XS):
                chip = z * XS + x
                one = stage[x, 0, z, 0].astype(F32)
                two = stage[x, 1, z, 0].astype(F32)
                rows = pl.ds(chip * HALF_ROWS, HALF_ROWS)
                win[rows, :WIDE_LANES] = jnp.concatenate([one[:24], two[:24]], axis=0).astype(BF16)
                win[rows, WIDE_LANES:] = jnp.concatenate([one[24:], two[24:]], axis=0).astype(BF16)
                for c in range(CORES):
                    base = (chip * CORES + c) * 96
                    wout[pl.ds(base, HALF_ROWS), :] = stage[x, c, z, 1, :, :D]
                    wout[pl.ds(base + HALF_ROWS, HALF_ROWS), :] = stage[x, c, z, 1, :, D:]
        point_a(expert)
        for image in range(images):
            part = pl.ds(image * CAP, CAP)
            slot_row = rows_s[image, pl.ds(expert, 1), :]
            gate_row = rows_s[image, pl.ds(EXPERTS + expert, 1), :]
            match = slot_at == slot_row
            sent = nn(jnp.where(match, 1.0, 0.0).astype(BF16), both[pl.ds(image * GRID, GRID), :])
            gate = jnp.sum(jnp.where(match, gate_row, 0.0), axis=1, keepdims=True)
            given[part, :] = sent[:, :D].astype(BF16)
            upstream_s[part, :] = sent[:, D:].astype(BF16)
            gate_s[part, :] = jnp.broadcast_to(gate, (CAP, 128))
            dres_s[part, :] = (gate * sent[:, D:]).astype(BF16)
        slots = given[...]
        dres = dres_s[...]
        result = jnp.zeros((images * CAP, D), F32)
        back = jnp.zeros((images * CAP, D), F32)
        for chunk in range(FF // FCH):
            span = pl.ds(chunk * FCH, FCH)
            w_in = win[:, span]
            w_out = wout[span, :]
            pre = nn(slots, w_in)
            square = pre * pre
            curve = jnp.tanh(pre * (c1 + c3 * square))
            lifted = 0.5 * (1.0 + curve)
            hidden = (pre * lifted).astype(BF16)
            slope = lifted + (0.5 * pre) * (1.0 - curve * curve) * (c1 + (3.0 * c3) * square)
            result = result + nn(hidden, w_out)
            dpre = (nt(dres, w_out) * slope).astype(BF16)
            back = back + nt(dpre, w_in)
            term = tn(hidden, dres)
            for one in range(FCH // 96):
                w = chunk * (FCH // 96) + one
                z, x, c = w // (XS * CORES), (w // CORES) % XS, w % CORES
                gs[slot, c, x, z, 1, :, :D] = term[one * 96 : one * 96 + 48].astype(BF16)
                gs[slot, c, x, z, 1, :, D:] = term[one * 96 + 48 : one * 96 + 96].astype(BF16)
            term = tn(slots, dpre)
            if chunk == 0:
                held[...] = term
            else:
                for w in range(ZS * XS * CORES):
                    z, x, c = w // (XS * CORES), (w // CORES) % XS, w % CORES
                    rows = slice(w * 24, w * 24 + 24)
                    gs[slot, c, x, z, 0] = jnp.concatenate([held[rows, :], term[rows]], axis=0).astype(BF16)
        guard(expert + 1, load)
        result = result.astype(BF16).astype(F32)
        dgate = jnp.sum(result * upstream_s[...].astype(F32), axis=1, keepdims=True)
        gated = result * gate_s[:, :1]
        into = pl.ds(pl.multiple_of(expert * CAP, CAP), CAP)
        for image in range(images):
            part = slice(image * CAP, (image + 1) * CAP)
            returned_s[image, into, :D] = gated[part].astype(BF16)
            returned_s[image, into, D:] = back[part].astype(BF16)

        for image in range(images):
            part = slice(image * CAP, (image + 1) * CAP)
            slot_row = rows_s[image, pl.ds(expert, 1), :]
            dprobs_s[image, pl.ds(expert, 1), :] = jnp.sum(
                jnp.where(slot_at == slot_row, dgate[part], 0.0), axis=0, keepdims=True
            )
        point_b(expert)
        scatter.r0(expert)
        return carry

    lax.fori_loop(0, EXPERTS, expert_step, 0)

    def out_copy(image):
        rows = pl.ds(pl.multiple_of(image * GRID, GRID), GRID)
        return pltpu.make_async_copy(both.at[rows, pl.ds(D, D)], output_ref.at[rows, :], outward.at[0, image])

    def grad_copy(image):
        rows = pl.ds(pl.multiple_of(image * GRID, GRID), GRID)
        return pltpu.make_async_copy(both.at[rows, pl.ds(0, D)], grad_tokens_ref.at[rows, :], outward.at[1, image])

    gd[...] = jnp.zeros_like(gd)
    lane_rb = lanes((RB, 128))
    slot_lane = lanes((RB, CAP)).astype(F32)

    def merge_image(image, carry):
        at_row = pl.multiple_of(image * GRID, GRID)
        task = task_ref[image]
        router = router_of(dense, task)
        point_a(EXPERTS + image)
        columns = jnp.concatenate(
            [rows_s[image, :EXPERTS], probs_s[image], dprobs_s[image], jnp.zeros((128 - 3 * EXPERTS, GRID), F32)], axis=0
        ).T
        grad_router = jnp.zeros((D, 128), F32)
        grad_out = jnp.zeros((D, D), F32)
        gain_sum = jnp.zeros((1, D), F32)
        shift_sum = jnp.zeros((1, D), F32)

        def landing(block):
            cols = columns[block * RB : (block + 1) * RB]
            hits = [
                jnp.where(slot_lane == cols[:, e : e + 1], 1.0, 0.0).astype(BF16) for e in range(EXPERTS)
            ]
            return nn(jnp.concatenate(hits, axis=1), returned_s[image])

        landed = landing(0)
        for block in range(GRID // RB):
            later = landing(block + 1) if block + 1 < GRID // RB else None
            rows = pl.ds(pl.multiple_of(at_row + block * RB, RB), RB)
            upstream = both[rows, D:].astype(F32)
            branch = resid[rows, :]
            both[rows, D:] = (branch + landed[:, :D]).astype(BF16)
            unit_b, inverse_b = norm_rows(branch)
            cols = columns[block * RB : (block + 1) * RB]
            probs = jnp.where(lane_rb < EXPERTS, pltpu.roll(cols, 128 - EXPERTS, 1), 0.0)
            dprobs = jnp.where(lane_rb < EXPERTS, pltpu.roll(cols, 128 - 2 * EXPERTS, 1), 0.0)
            dlogits = probs * (dprobs - jnp.sum(dprobs * probs, axis=-1, keepdims=True))
            dlogits = dlogits.astype(BF16)
            grad_router = grad_router + tn(both[rows, :D], dlogits)
            dnormed_b = landed[:, D:] + nt(dlogits, router)
            gain_sum = gain_sum + jnp.sum(dnormed_b * unit_b, axis=0, keepdims=True)
            shift_sum = shift_sum + jnp.sum(dnormed_b, axis=0, keepdims=True)
            dresid = upstream + norm_back(dnormed_b, unit_b, inverse_b, misc[2:3])
            resid[rows, :] = dresid
            dbranch = dresid.astype(BF16)
            grad_out = grad_out + tn(attended[rows, :], dbranch)
            dattended[rows, :] = nt(dbranch, dense[:, 3 * D : MISC]).astype(BF16)
            unit_a, _ = norm_rows(tokens_ref[rows, :].astype(F32))
            both[rows, :D] = (unit_a * misc[0:1] + misc[1:2]).astype(BF16)
            landed = later
        out_copy(image).start()
        point_b(EXPERTS + image)
        placed = jnp.where(task == 0, pltpu.roll(grad_router, 4, 1), pltpu.roll(grad_router, 12, 1))
        vectors = jnp.concatenate([jnp.zeros((2, D), F32), gain_sum, shift_sum, jnp.zeros((124, D), F32)], axis=0).T
        gd[:, :D] += grad_out
        gd[:, D : D + 128] += placed + vectors
        return carry

    lax.fori_loop(0, images, merge_image, 0)

    small = lanes((QB, 128))
    half = small // HEAD_DIM
    EARLY = D + 128

    def pack(slot, first_col, count):
        n = count // 4
        for w in range(ZS * XS * CORES):
            z, x, c = w // (XS * CORES), (w // CORES) % XS, w % CORES
            rows = slice(w * 24, w * 24 + 24)
            for part in range(2):
                at = first_col + part * 2 * n
                gs[slot, c, x, z, part, :, :n] = jnp.concatenate(
                    [gd[rows, at : at + n], gd[rows, at + n : at + 2 * n]], axis=0
                ).astype(BF16)

    def unpack(values):
        blocks = []
        for value in values:
            blocks += [value[:24], value[24:]]
        return jnp.concatenate(blocks, axis=1)

    def place_pair(pair, columns):
        for kind in range(3):
            at = kind * D + pair * 128
            grad_proj_in_ref[:, at : at + 128] = columns[:, kind * 128 : kind * 128 + 128]

    def backward_step(step, carry):
        pair = step // 2
        image = lax.rem(step, 2)
        at_row = pl.multiple_of(image * GRID, GRID)
        mine_rows = pl.ds(at_row, GRID)
        point_a(EXPERTS + 2 + step)

        @pl.when(step == 5)
        def _():
            scatter.r1w(EXPERTS, 384)
            scatter.r1b(EXPERTS, 384)

        live_col = column_of(valid_ref[pl.ds(image, 1), :].astype(F32))
        lse_col = jnp.concatenate([lse[image], jnp.zeros((120, GRID), F32)], axis=0).T
        key_ext = jnp.where((lane == 0) & (live_col < 0.5), NEGATIVE, 0.0)
        key_ext = jnp.where((lane >= 1) & (lane <= 3), 1.0, key_ext).astype(BF16)
        value_ext = jnp.where(lane < 3, 1.0, 0.0).astype(BF16)
        at = pl.multiple_of(pair * 128, 128)
        keys = mixed[mine_rows, pl.ds(D + at, 128)]
        values = mixed[mine_rows, pl.ds(2 * D + at, 128)]
        key_full = jnp.concatenate([keys, key_ext], axis=1)
        value_full = jnp.concatenate([values, value_ext], axis=1)
        key_t = keys.astype(F32).T.astype(BF16)
        for block in range(GRID // QB):
            span = pl.ds(block * QB, QB)
            rows_here = pl.ds(pl.multiple_of(at_row + block * QB, QB), QB)
            query = mixed[rows_here, pl.ds(at, 128)].astype(F32) * SCALE
            grad = dattended[rows_here, pl.ds(at, 128)].astype(F32)
            seen = attended[rows_here, pl.ds(at, 128)].astype(F32) * grad
            for part in range(2):
                own = half == part
                inner = jnp.sum(jnp.where(own, seen, 0.0), axis=-1, keepdims=True)
                high, mid, low = split3(-inner)
                grad_ext = jnp.where(
                    small == 0, high, jnp.where(small == 1, mid, jnp.where(small == 2, low, 0.0))
                ).astype(BF16)
                head = pair * 2 + part
                shift = jnp.sum(
                    jnp.where(small == head, lse_col[block * QB : (block + 1) * QB], 0.0),
                    axis=-1,
                    keepdims=True,
                )
                high, mid, low = split3(-shift)
                query_ext = jnp.where(
                    small == 0,
                    1.0,
                    jnp.where(
                        small == 1, high, jnp.where(small == 2, mid, jnp.where(small == 3, low, 0.0))
                    ),
                ).astype(BF16)
                my_query = jnp.where(own, query, 0.0).astype(BF16)
                my_grad = jnp.where(own, grad, 0.0).astype(BF16)
                weights = jnp.exp(nt(key_full, jnp.concatenate([my_query, query_ext], axis=1)))
                drift = nt(value_full, jnp.concatenate([my_grad, grad_ext], axis=1))
                dscores = (weights * drift).astype(BF16)
                dkey = nn(dscores, my_query)
                dvalue = nn(weights.astype(BF16), my_grad)
                if block == 0 and part == 0:
                    acc_k[...] = dkey
                    acc_v[...] = dvalue
                else:
                    acc_k[...] += dkey
                    acc_v[...] += dvalue
                rows = slice(part * HEAD_DIM, (part + 1) * HEAD_DIM)
                dq_t[rows, span] = nn(key_t[rows], dscores)
        mixed[mine_rows, pl.ds(at, 128)] = (dq_t[...].T * SCALE).astype(BF16)
        mixed[mine_rows, pl.ds(D + at, 128)] = acc_k[...].astype(BF16)
        mixed[mine_rows, pl.ds(2 * D + at, 128)] = acc_v[...].astype(BF16)

        @pl.when(image == 1)
        def _():
            for kind in range(3):
                got = tn(both[:, :D], mixed[:, pl.ds(pl.multiple_of(kind * D + at, 128), 128)])
                for which in range(PAIRS):
                    into = EARLY + which * D if which < 2 else LATE

                    @pl.when(pair == which)
                    def _():
                        gd[:, into + kind * 128 : into + kind * 128 + 128] = got

        point_b(EXPERTS + 2 + step)

        @pl.when(step == 4)
        def _():
            scatter.r1a(EXPERTS, 384)

        @pl.when(step == 3)
        def _():
            pack(0, 0, LATE)
            scatter.r0(EXPERTS, 384)

        return carry

    lax.fori_loop(0, 2 * PAIRS, backward_step, 0)
    scatter.r2a(EXPERTS, 384)
    finish(EXPERTS - 1, scatter.r5(EXPERTS - 1))

    gain_sum = jnp.zeros((1, D), F32)
    shift_sum = jnp.zeros((1, D), F32)
    for block in range(images * GRID // RB):
        rows = pl.ds(block * RB, RB)
        dnormed_a = nt(mixed[rows, :], dense[:, : 3 * D])
        unit_a, inverse_a = norm_rows(tokens_ref[rows, :].astype(F32))
        gain_sum = gain_sum + jnp.sum(dnormed_a * unit_a, axis=0, keepdims=True)
        shift_sum = shift_sum + jnp.sum(dnormed_a, axis=0, keepdims=True)
        both[rows, :D] = (resid[rows, :] + norm_back(dnormed_a, unit_a, inverse_a, misc[0:1])).astype(BF16)
    for image in range(images):
        grad_copy(image).start()
    scatter.r2b(EXPERTS, 384)
    gd[:, LATE + D :] = jnp.concatenate([gain_sum, shift_sum, jnp.zeros((126, D), F32)], axis=0).T
    pack(1, LATE, 512)
    early_k, late_k = EXPERTS, EXPERTS + 1
    scatter.r0(late_k, 128)
    scatter.r3(early_k, 384)
    scatter.r1a(late_k, 128)
    scatter.r1w(late_k, 128)
    scatter.r1b(late_k, 128)
    scatter.r4(early_k, 384)
    scatter.r2a(late_k, 128)
    scatter.r2b(late_k, 128)
    early = unpack(scatter.r5(early_k, 384))
    grad_proj_out_ref[...] = early[:, :D]
    for pair in range(2):
        place_pair(pair, early[:, EARLY + pair * D : EARLY + (pair + 1) * D])
    scatter.r3(late_k, 128)
    scatter.r4(late_k, 128)
    late = unpack(scatter.r5(late_k, 128))
    place_pair(2, late[:, :D])
    grad_misc_ref[...] = early[:, D : D + 128] + late[:, D:]

    def drain(e, carry):
        gather.drain(e)
        return carry

    lax.fori_loop(0, EXPERTS, drain, 0)

    def written(image, carry):
        out_copy(image).wait()
        grad_copy(image).wait()
        return carry

    lax.fori_loop(0, images, written, 0)


def whole_call(task_ids, top_counts, tokens, cotangent, valid, ids_t, dmine, mine, flat):
    images = valid.shape[0]
    rows = images * GRID
    smem = pl.BlockSpec(memory_space=pltpu.SMEM)
    vmem = pl.BlockSpec(memory_space=pltpu.VMEM)
    anywhere = pl.BlockSpec(memory_space=pl.ANY)
    piece = (HALF_ROWS, WIDE_LANES)
    sem = pltpu.SemaphoreType.DMA
    return pl.pallas_call(
        functools.partial(whole_kernel, images),
        in_specs=[smem, smem, vmem, anywhere, vmem, vmem, vmem, anywhere, anywhere],
        out_specs=[anywhere, anywhere, vmem, vmem, vmem, vmem, vmem] + [anywhere] * 3,
        out_shape=[
            jax.ShapeDtypeStruct((rows, D), BF16),
            jax.ShapeDtypeStruct((rows, D), BF16),
            jax.ShapeDtypeStruct((EXPERTS, 24, FF), BF16),
            jax.ShapeDtypeStruct((EXPERTS, 96, D), BF16),
            jax.ShapeDtypeStruct((24, 3 * D), F32),
            jax.ShapeDtypeStruct((24, D), F32),
            jax.ShapeDtypeStruct((24, 128), F32),
            jax.ShapeDtypeStruct((EXPERTS, XS, CORES, ZS, 2) + piece, BF16),
            jax.ShapeDtypeStruct((CHUNKS, XS, AZ, 2) + piece, BF16),
            jax.ShapeDtypeStruct((CHUNKS, XS, BZ, 2) + piece, BF16),
        ],
        scratch_shapes=[
            pltpu.VMEM((D, DENSE), BF16),
            pltpu.VMEM((rows, 3 * D), BF16),
            pltpu.VMEM((rows, D), BF16),
            pltpu.VMEM((rows, D), F32),
            pltpu.VMEM((rows, 2 * D), BF16),
            pltpu.VMEM((images, EXPERTS, GRID), F32),
            pltpu.VMEM((images, 2 * EXPERTS, GRID), F32),
            pltpu.VMEM((images, 8, GRID), F32),
            pltpu.VMEM((images, EXPERTS * CAP, 2 * D), BF16),
            pltpu.VMEM((images, EXPERTS, GRID), F32),
            pltpu.VMEM((XS, CORES, ZS, 2) + piece, BF16),
            pltpu.VMEM((D, FF), BF16),
            pltpu.VMEM((FF, D), BF16),
            pltpu.VMEM((images * CAP, D), BF16),
            pltpu.VMEM((images * CAP, D), BF16),
            pltpu.VMEM((images * CAP, 128), F32),
            pltpu.VMEM((images * CAP, D), BF16),
            pltpu.VMEM((rows, D), BF16),
            pltpu.VMEM((GRID, 128), F32),
            pltpu.VMEM((GRID, 128), F32),
            pltpu.VMEM((128, GRID), F32),
            pltpu.VMEM((D, DENSE_COLS), F32),
            pltpu.VMEM((2, CORES, XS, ZS, 2) + piece, BF16),
            pltpu.VMEM((2, XS, ZS, 2) + piece, BF16),
            pltpu.VMEM((XS, ZS, 2) + piece, BF16),
            pltpu.VMEM((AZ, 2) + piece, BF16),
            pltpu.VMEM((XS, BZ) + piece, BF16),
            pltpu.VMEM((2, AZ, 2) + piece, BF16),
            pltpu.VMEM((2, XS, BZ) + piece, BF16),
            pltpu.VMEM((AZ, 2) + piece, BF16),
            pltpu.VMEM((XS, BZ) + piece, BF16),
            pltpu.VMEM((2, AZ) + piece, BF16),
            pltpu.VMEM((2, BZ) + piece, BF16),
            pltpu.VMEM((ZS,) + piece, BF16),
            pltpu.VMEM((2, ZS - 1) + piece, BF16),
            pltpu.VMEM((2, 2) + piece, BF16),
            sem((2, ZS)),
            sem((2, 3)),
            sem((EXPERTS, ZS - 1)),
            sem((EXPERTS, ZS - 1)),
            sem((4, EXPERTS)),
            sem((4, EXPERTS)),
            sem((EXPERTS, ZS - 1)),
            sem((EXPERTS, ZS - 1)),
            sem((4,)),
            sem((2, images)),
            sem((9, 2)),
            sem((9, 2)),
            sem((4,)),
        ],
        compiler_params=pltpu.CompilerParams(
            vmem_limit_bytes=VMEM_LIMIT, collective_id=0, has_side_effects=True
        ),
        name="whole_step",
    )(task_ids, top_counts, tokens, cotangent, valid, ids_t, dmine, mine, flat)


def whole_body(
    tokens,
    cotangent,
    valid,
    task_ids,
    top_counts,
    expert_ids,
    attn_gain,
    attn_shift,
    proj_in,
    proj_out,
    moe_gain,
    moe_shift,
    router,
    expert_in,
    expert_out,
):
    own = attn_gain.shape[0]
    lane = jnp.arange(128, dtype=jnp.int32)[None, :]
    small = jnp.zeros((own, 128), BF16)
    for index, vector in enumerate((attn_gain, attn_shift, moe_gain, moe_shift)):
        small = jnp.where(lane == index, vector[:, None], small)
    for task in range(TASKS):
        at = 4 + task * EXPERTS
        small = small + jnp.pad(router[task], ((0, 0), (at, 128 - at - EXPERTS)))
    cuts = [
        proj_in[:, :DENSE_LANES],
        proj_in[:, DENSE_LANES : 2 * DENSE_LANES],
        jnp.concatenate([proj_in[:, 2 * DENSE_LANES :], proj_out], axis=1),
        jnp.pad(small, ((0, 0), (0, DENSE_LANES - 128))),
    ]
    dmine = jnp.concatenate(cuts, axis=0).reshape(2, HALF_ROWS, DENSE_LANES)
    first = expert_in.reshape(EXPERTS, own, 2, WIDE_LANES).transpose(0, 2, 1, 3).reshape(EXPERTS, HALF_ROWS, WIDE_LANES)
    second = jnp.concatenate([expert_out[:, :HALF_ROWS], expert_out[:, HALF_ROWS:]], axis=2)
    mine = jnp.stack([first, second], axis=1)
    output, grad_tokens, grad_in, grad_out, grad_proj_in, grad_proj_out, grad_small, *_ = whole_call(
        task_ids,
        top_counts,
        tokens,
        cotangent,
        valid,
        expert_ids.T,
        dmine,
        mine,
        mine.reshape(EXPERTS * 2 * HALF_ROWS, WIDE_LANES),
    )
    columns = grad_small[:, :4].T
    grad_router = jnp.stack([grad_small[:, 4:12], grad_small[:, 12:20]], axis=0)
    return (
        output,
        grad_tokens,
        columns[0],
        columns[1],
        grad_proj_in,
        grad_proj_out,
        columns[2],
        columns[3],
        grad_router,
        grad_in.astype(F32),
        grad_out.astype(F32),
    )


def body(
    tokens,
    cotangent,
    valid,
    task_ids,
    top_counts,
    expert_ids,
    attn_gain,
    attn_shift,
    proj_in,
    proj_out,
    moe_gain,
    moe_shift,
    router,
    expert_in,
    expert_out,
):
    own = attn_gain.shape[0]
    misc = jnp.concatenate(
        [
            jnp.stack([attn_gain, attn_shift, moe_gain, moe_shift], axis=1),
            router[0],
            router[1],
            jnp.zeros((own, 128 - 4 - TASKS * EXPERTS), BF16),
        ],
        axis=1,
    )
    packed = jnp.concatenate([proj_in, proj_out, misc], axis=1)
    dense = lax.all_gather(packed, "wide", axis=0, tiled=True)
    full_in = lax.all_gather(expert_in, "wide", axis=1, tiled=True)
    full_out = lax.all_gather(expert_out, "wide", axis=1, tiled=True)
    mixed, attended, resid, normed_b, aux, rows, lse = forward_call(
        task_ids, top_counts, tokens, valid, expert_ids, dense
    )
    sums, dprobs, grad_in, grad_out = expert_call(normed_b, cotangent, aux, rows, full_in, full_out)
    part_in = lax.psum_scatter(grad_in, "wide", scatter_dimension=1, tiled=True)
    part_out = lax.psum_scatter(grad_out, "wide", scatter_dimension=1, tiled=True)
    output, grad_tokens, grad_dense, _ = backward_call(
        task_ids, tokens, cotangent, valid, dense, mixed, attended, resid, normed_b, aux, lse, sums, dprobs
    )
    part_dense = lax.psum_scatter(grad_dense.astype(BF16), "wide", scatter_dimension=0, tiled=True)
    sum_in, sum_out, sum_dense = lax.psum((part_in, part_out, part_dense), "narrow")
    sum_in = sum_in.astype(F32)
    sum_out = sum_out.astype(F32)
    sum_dense = sum_dense.astype(F32)
    vectors = sum_dense[:, MISC : MISC + 4].T
    grad_router = jnp.stack(
        [sum_dense[:, MISC + 4 : MISC + 12], sum_dense[:, MISC + 12 : MISC + 20]], axis=0
    )
    return (
        output,
        grad_tokens,
        vectors[0],
        vectors[1],
        sum_dense[:, : 3 * D],
        sum_dense[:, 3 * D : MISC],
        vectors[2],
        vectors[3],
        grad_router,
        sum_in,
        sum_out,
    )


def solution(mesh):
    rows = P(("narrow", "wide"), None)
    middle = P(None, "wide", None)
    one_kernel = mesh.shape["narrow"] == 2 and mesh.shape["wide"] == ZS * XS * CORES
    return jax.shard_map(
        whole_body if one_kernel else body,
        mesh=mesh,
        in_specs=(
            rows,
            rows,
            rows,
            P(("narrow", "wide")),
            P(),
            rows,
            P("wide"),
            P("wide"),
            P("wide", None),
            P("wide", None),
            P("wide"),
            P("wide"),
            middle,
            middle,
            middle,
        ),
        out_specs=(
            rows,
            rows,
            P("wide"),
            P("wide"),
            P("wide", None),
            P("wide", None),
            P("wide"),
            P("wide"),
            middle,
            middle,
            middle,
        ),
        check_vma=False,
    )
```
